32 devices in a mesh: cfg: 2 (over x), sx: 16 (over z, y, core).
Axes of the slice: x: 2, y: 2, z: 4, core: 2. Of those that a mesh axis runs over, the one named last changes fastest.
Arguments:
- eigvecs: bfloat16 [512, 2, 3, 16, 1024], P('cfg', None, None, 'sx'), parts along dimension 0, may hold values from -6 to 6
- link_seed: int32 [6], P('cfg'), parts along dimension 0, may hold values from 1 to 46336
- ownership: int32 [2080], replicated, may hold values from 0 to 2079, each once
Outputs:
- elementals: float32 [4160, 96], P(('cfg', 'sx')), parts along dimension 0
The draws below stay inside these ranges and needn't reach their ends.
There are 2 independent parts, one for each index of `cfg`. The reference program is written for one: setup_inputs(seed, part) draws one part's arguments, and reference() takes and returns one part's arrays. A program takes and returns all parts, laid end to end along the dimension named above; an argument that names none is the same for every part. Nothing has to cross between parts.
Inputs may be any that keep to these rules, and one draw needn't show every extreme that they name: ownership is a permutation of the pair tiles 0 to 2079.
All inputs are finite; a program needn't handle non-finite values.
Results may differ from the reference program's by a relative error of at most 0.0029.
Values may be sent and summed in bfloat16 or wider, within the bound.
No kernel may reach another device: no remote copies, remote signals or barrier semaphores. Data moves between devices by JAX's collectives and lax.ppermute only.
A program may use at most 192 MiB of HBM per device.

```python
import math
import jax
import jax.numpy as jnp
import numpy as np
from jax import lax

NEV = 256
TM = 4
NY = 16
NZ = 64
PLANE = 1024
NX = 16
PAIRS = 2080


def steps_of(stream_key, extent, pieces, low, high):
    gain = 1.0
    for axis_at, shards_of in pieces:
        steps = jax.random.uniform(jax.random.fold_in(jax.random.fold_in(stream_key, 6), axis_at), (shards_of,), jnp.float32, low / len(pieces), high / len(pieces))
        gain = gain * jnp.repeat(jnp.exp(steps), extent[axis_at] // shards_of).reshape((-1,) + (1,) * (len(extent) - 1 - axis_at))
    return gain


def scatter_about(rng, shape, scale, most, shards=(), kind=jnp.bfloat16):
    drawn = jax.random.normal(rng, shape, jnp.float32) * scale
    if len(shards) > 0:
        drawn = steps_of(rng, shape, shards, -0.22, 0.18) * drawn
    return jnp.clip(drawn, min=-most, max=most).astype(kind)


def setup_inputs(seed: int = 0, part: int = 0) -> dict:
    splits = jax.random.split(jax.random.key(seed), 4)
    part_splits = jax.random.split(jax.random.fold_in(splits[3], part), 4)
    return {
        "eigvecs": scatter_about(part_splits[0], (NEV, 2, 3, NX, PLANE), 1.0, 6.0, ((3, 16),)),
        "link_seed": jax.random.randint(part_splits[1], (3,), 1, 46337).astype(jnp.int32),
        "ownership": jax.random.permutation(splits[2], PAIRS).astype(jnp.int32),
    }


def scramble(seed_value, site_code):
    modulus = 46337
    low_part = site_code % modulus
    high_part = site_code // modulus
    mixed_value = (seed_value * seed_value + low_part) % modulus
    mixed_value = (mixed_value * mixed_value + high_part * 977 + 31) % modulus
    angles = []
    for angle_index in range(7):
        scrambled = (mixed_value + 5171 * angle_index + 1) % modulus
        scrambled = (scrambled * scrambled + low_part) % modulus
        scrambled = (scrambled * scrambled + 12345) % modulus
        angles.append(scrambled.astype(jnp.float32) * (2.0 * math.pi / modulus) - math.pi)
    return angles

def link_field(seed_value, site_code):
    angles = scramble(seed_value, site_code)
    cos_alpha, sin_alpha = (jnp.cos(angles[0]), jnp.sin(angles[0]))
    cos_beta, sin_beta = (jnp.cos(angles[1]), jnp.sin(angles[1]))
    cos_gamma, sin_gamma = (jnp.cos(angles[2]), jnp.sin(angles[2]))
    rotation = [[cos_alpha * cos_beta * cos_gamma - sin_alpha * sin_gamma, -cos_alpha * cos_beta * sin_gamma - sin_alpha * cos_gamma, cos_alpha * sin_beta], [sin_alpha * cos_beta * cos_gamma + cos_alpha * sin_gamma, -sin_alpha * cos_beta * sin_gamma + cos_alpha * cos_gamma, sin_alpha * sin_beta], [-sin_beta * cos_gamma, sin_beta * sin_gamma, cos_beta]]
    phase_left = [angles[3], angles[4], -angles[3] - angles[4]]
    phase_right = [angles[5], angles[6], -angles[5] - angles[6]]
    link_real = jnp.stack([jnp.stack([rotation[row_index][column] * jnp.cos(phase_left[row_index] + phase_right[column]) for column in range(3)]) for row_index in range(3)])
    link_imag = jnp.stack([jnp.stack([rotation[row_index][column] * jnp.sin(phase_left[row_index] + phase_right[column]) for column in range(3)]) for row_index in range(3)])
    return (link_real, link_imag)

def hop_vectors(link_real, link_imag, vectors):
    real_part = vectors[:, 0].astype(jnp.float32)
    imag_part = vectors[:, 1].astype(jnp.float32)
    out_real = []
    out_imag = []
    for colour in range(3):
        acc_real = jnp.zeros(real_part[:, 0].shape, jnp.float32)
        acc_imag = jnp.zeros(real_part[:, 0].shape, jnp.float32)
        for source in range(3):
            u_real = link_real[colour, source]
            u_imag = link_imag[colour, source]
            acc_real = acc_real + u_real * real_part[:, source] - u_imag * imag_part[:, source]
            acc_imag = acc_imag + u_real * imag_part[:, source] + u_imag * real_part[:, source]
        out_real.append(acc_real)
        out_imag.append(acc_imag)
    return jnp.stack([jnp.stack(out_real, 1), jnp.stack(out_imag, 1)], 1).astype(jnp.bfloat16)

def shift_plane(vectors, axis_number):
    shape = vectors.shape
    spread = vectors.reshape(shape[:4] + (NY, NZ))
    return jnp.roll(spread, -1, axis_number).reshape(shape)

def conjugate_stack(vectors):
    return jnp.concatenate([vectors, jnp.stack([-vectors[:, 1], vectors[:, 0]], 1)], 0)

def antisymmetric(products):
    real_part = products[:, 0] - jnp.swapaxes(products[:, 0], 1, 2)
    imag_part = products[:, 1] + jnp.swapaxes(products[:, 1], 1, 2)
    return jnp.stack([real_part, imag_part], 1)

def pick_tiles(products, chosen_rows):
    tile_count = NEV // TM
    tiles = products.reshape(3, 2, tile_count, TM, tile_count, TM).transpose(2, 4, 0, 1, 3, 5)
    return jnp.take(tiles.reshape(tile_count * tile_count, 6 * TM * TM), chosen_rows, axis=0)

def reference(eigvecs, link_seed, ownership):
    width = 6 * PLANE
    plane_index = jnp.arange(PLANE, dtype=jnp.int32)

    def layer_step(total, layer_index):
        layer = lax.dynamic_slice_in_dim(eigvecs, layer_index, 1, 3)
        upper_index = ((layer_index + 1) % NX).astype(jnp.int32)
        nearest = lax.dynamic_slice_in_dim(eigvecs, upper_index, 1, 3)
        site_code = (layer_index * PLANE + plane_index)[None, :]
        hop_x = hop_vectors(*link_field(link_seed[0], site_code), nearest)
        hop_y = hop_vectors(*link_field(link_seed[1], site_code), shift_plane(layer, 4))
        hop_z = hop_vectors(*link_field(link_seed[2], site_code), shift_plane(layer, 5))
        lefts = conjugate_stack(layer).reshape(2 * NEV, width).astype(jnp.float32)
        rights = jnp.concatenate([hop_x, hop_y, hop_z], 0).reshape(3 * NEV, width).astype(jnp.float32)
        term = lax.dot_general(lefts, rights, (((1,), (1,)), ((), ())), precision=lax.Precision.HIGHEST, preferred_element_type=jnp.float32)
        return (total + term, None)
    start_total = jnp.zeros((2 * NEV, 3 * NEV), jnp.float32)
    gram_matrix, _ = lax.scan(layer_step, start_total, jnp.arange(NX, dtype=jnp.int32))
    products = gram_matrix.reshape(2, NEV, 3, NEV).transpose(2, 0, 1, 3)
    normalise = 1.0 / math.sqrt(12.0 * NX * PLANE)
    derived = antisymmetric(products) * normalise
    upper_rows, upper_cols = np.triu_indices(NEV // TM)
    pair_rows = jnp.asarray((upper_rows * (NEV // TM) + upper_cols).astype(np.int32))
    chosen_rows = jnp.take(pair_rows, ownership)
    return pick_tiles(derived, chosen_rows)
```

```python
import functools
import math

import jax
import jax.numpy as jnp
from jax import lax
from jax.experimental import pallas as pl
from jax.experimental.pallas import tpu as pltpu
from jax.sharding import PartitionSpec as P

TM = 4
NZ = 64
LANES = 128
MODULUS = 46337
CHUNKS = 4
F32 = jnp.float32
BF16 = jnp.bfloat16
NT = (((1,), (1,)), ((), ()))


def dot(left, right, dims=(((1,), (0,)), ((), ()))):
    return lax.dot_general(left, right, dims, preferred_element_type=F32)


def iota(shape, axis):
    return lax.broadcasted_iota(jnp.int32, shape, axis)


def round_up(value, step):
    return -(-value // step) * step


def link_angles(seed, site):
    low = lax.rem(site, MODULUS)
    high = lax.div(site, MODULUS)
    mixed = lax.rem(seed * seed + low, MODULUS)
    mixed = lax.rem(mixed * mixed + high * 977 + 31, MODULUS)
    angles = []
    for index in range(7):
        g = lax.rem(mixed + (5171 * index + 1), MODULUS)
        g = lax.rem(g * g + low, MODULUS)
        g = lax.rem(g * g + 12345, MODULUS)
        angles.append(g.astype(F32) * (2.0 * math.pi / MODULUS) - math.pi)
    return angles


def store_links(u_ref, seed, site):
    a = link_angles(seed, site)
    ca, sa = jnp.cos(a[0]), jnp.sin(a[0])
    cb, sb = jnp.cos(a[1]), jnp.sin(a[1])
    cg, sg = jnp.cos(a[2]), jnp.sin(a[2])
    rotation = [
        [ca * cb * cg - sa * sg, -ca * cb * sg - sa * cg, ca * sb],
        [sa * cb * cg + ca * sg, -sa * cb * sg + ca * cg, sa * sb],
        [-sb * cg, sb * sg, cb],
    ]
    left = [a[3], a[4], -a[3] - a[4]]
    right = [a[5], a[6], -a[5] - a[6]]
    for c in range(3):
        for s in range(3):
            phase = left[c] + right[s]
            u_ref[2 * (3 * c + s)] = rotation[c][s] * jnp.cos(phase)
            u_ref[2 * (3 * c + s) + 1] = rotation[c][s] * jnp.sin(phase)


def hop(load, out_ref, u_ref, modes, plane, shift):
    tiles = plane // LANES
    for t in range(tiles):

        def body(block, carry, t=t):
            rows = pl.ds(pl.multiple_of(block * 16, 16), 16)
            lane = iota((16, LANES), 1)
            v = []
            for source in range(3):
                for part in range(2):
                    x = load(part, source, rows, t).astype(F32)
                    if shift == "y":
                        above = load(part, source, rows, (t + 1) % tiles).astype(F32)
                        x = pltpu.roll(jnp.where(lane < NZ, above, x), NZ, 1)
                    elif shift == "z":
                        inside = pltpu.roll(x, LANES - 1, 1)
                        wrapped = pltpu.roll(x, NZ - 1, 1)
                        x = jnp.where(lane % NZ == NZ - 1, wrapped, inside)
                    v.append(x)
            for c in range(3):
                real = imag = None
                for s in range(3):
                    ur = u_ref[2 * (3 * c + s), t : t + 1, :]
                    ui = u_ref[2 * (3 * c + s) + 1, t : t + 1, :]
                    re, im = v[2 * s], v[2 * s + 1]
                    real = ur * re if real is None else real + ur * re
                    real = real - ui * im
                    imag = ur * im if imag is None else imag + ur * im
                    imag = imag + ui * re
                lanes = slice(c * plane + t * LANES, c * plane + (t + 1) * LANES)
                out_ref[rows, lanes] = real.astype(BF16)
                low = pl.ds(pl.multiple_of(modes + block * 16, 16), 16)
                out_ref[low, lanes] = imag.astype(BF16)
            return carry

        lax.fori_loop(0, modes // 16, body, 0)


def products(hop_ref, left_ref, modes, all_modes):
    by_real = dot(hop_ref[...], left_ref[:all_modes, :], NT)
    by_imag = dot(hop_ref[...], left_ref[all_modes:, :], NT)
    real = by_real[:modes] + by_imag[modes:]
    imag = by_real[modes:] - by_imag[:modes]
    return real, imag


class Slots:
    def __init__(self, all_modes, slots, directions):
        self.tiles = all_modes // TM
        assert 2 * self.tiles == LANES
        self.half = self.tiles // 2
        self.depth = round_up((self.half + 1) * self.tiles, 2 * LANES)
        self.columns = 2 * TM * TM * directions
        self.groups = LANES // self.columns
        self.per_group = -(-slots // self.groups)
        self.rows = round_up(self.per_group, 8)
        self.sent = round_up(self.rows, 16)

    def arrange(self, ownership, devices):
        slots = ownership.shape[0] // devices
        spread = jnp.pad(
            ownership.reshape(devices, slots),
            ((0, 0), (0, self.groups * self.per_group - slots)),
            constant_values=-1,
        ).reshape(devices, self.groups, self.per_group)
        spread = jnp.pad(
            spread, ((0, 0), (0, 0), (0, self.rows - self.per_group)), constant_values=-1
        )
        return spread.reshape(devices, self.groups * self.rows, 1)

    def codes(self):
        lane = iota((1, self.depth), 1)
        first, second = lane // self.tiles, lane % self.tiles
        last = self.tiles - 1
        diagonal = first == self.half
        turned = jnp.logical_or(diagonal, second < first)
        i = jnp.where(diagonal, last - second, jnp.where(turned, last - first, first))
        j = jnp.where(turned, last - second, second)
        pair = i * self.tiles - (i * (i - 1)) // 2 + (j - i)
        known = jnp.logical_and(
            first <= self.half, jnp.logical_not(jnp.logical_and(diagonal, second >= self.half))
        )
        return jnp.where(known, pair, -2)


def store_table(table_ref, fold_ref, base, real, imag, slots):
    all_modes = real.shape[0]
    n, half = slots.tiles, slots.half
    parts = [real.T - real, imag.T + imag]

    def choose(count, width, turned):
        row, column = iota((count, all_modes), 0), iota((count, all_modes), 1)
        r, i = row // width, row % width
        if turned:
            i = n - 1 - i
        return (column == i * TM + r).astype(F32).astype(BF16)

    pick = [choose(TM * half, half, turned) for turned in (False, True)]
    spread = [choose(all_modes, n, turned) for turned in (False, True)]
    row_i = iota((TM * half, all_modes), 0) % half
    lane_j = iota((TM * half, all_modes), 1) % n
    corners = []
    for part in range(2):
        entries = parts[part].astype(BF16)
        straight, turned = [
            dot(dot(pick[k], entries).astype(BF16), spread[k], NT) for k in range(2)
        ]
        folded = jnp.where(lane_j >= row_i, straight, turned)
        for k in range(TM // 2):
            fold_ref[k, part * TM * half : (part + 1) * TM * half, :] = folded[
                :, k * LANES : (k + 1) * LANES
            ]
        diagonal = jnp.where(lane_j == row_i, turned, 0.0)
        for r in range(TM):
            corners.append(
                jnp.sum(diagonal[r * half : (r + 1) * half], axis=0, keepdims=True)
            )
    low = iota((2 * TM, LANES), 1) < n

    def split(even, odd, lanes):
        for pair in range(TM // 2):
            e, o = even[pair], odd[pair]
            top = base + 2 * pair * 2 * TM
            table_ref[top : top + 2 * TM, lanes] = jnp.where(low, e, pltpu.roll(o, n, 1))
            table_ref[top + 2 * TM : top + 4 * TM, lanes] = jnp.where(
                low, pltpu.roll(e, n, 1), o
            )

    halves = [slice(k * LANES, (k + 1) * LANES) for k in range(TM // 2)]
    for two in range(half // 2):
        even = [fold_ref[k, pl.ds(2 * two, 2 * TM, stride=half), :] for k in range(TM // 2)]
        odd = [fold_ref[k, pl.ds(2 * two + 1, 2 * TM, stride=half), :] for k in range(TM // 2)]
        split(even, odd, slice(two * LANES, (two + 1) * LANES))
    corner = jnp.concatenate(corners, 0)
    nothing = jnp.zeros((2 * TM, LANES), F32)
    start = half * n
    split([corner[:, h] for h in halves], [nothing] * len(halves), slice(start, start + LANES))
    rest = slots.depth - start - LANES
    if rest:
        table_ref[base : base + 2 * TM * TM, start + LANES :] = jnp.zeros(
            (2 * TM * TM, rest), F32
        )


def send_tiles(out_ref, owner_ref, table_ref, slots, directions):
    block = 2 * TM * TM
    row, column = iota((LANES, slots.columns), 0), iota((LANES, slots.columns), 1)
    entry = row % slots.columns
    direction, inside = entry // block, entry % block
    u = inside % TM
    part_r = inside // TM
    order = column == direction * block + u * (2 * TM) + part_r
    table = dot(order.astype(F32).astype(BF16), table_ref[...].astype(BF16)).astype(BF16)
    codes = slots.codes()
    lane_group = iota((slots.rows, LANES), 1) // slots.columns

    def body(device, carry):
        owners = owner_ref[device]
        chosen = (owners == codes).astype(F32).astype(BF16)
        picked = dot(chosen, table, NT)
        packed = picked[: slots.rows]
        for group in range(1, slots.groups):
            piece = picked[group * slots.rows : (group + 1) * slots.rows]
            packed = jnp.where(lane_group == group, piece, packed)
        if slots.sent > slots.rows:
            packed = jnp.concatenate(
                [packed, jnp.zeros((slots.sent - slots.rows, LANES), F32)], 0
            )
        out_ref[device] = packed.astype(BF16)
        return carry

    lax.fori_loop(0, out_ref.shape[0], body, 0)


def inner_kernel(
    slots, seed_ref, where_ref, owner_ref, *refs
):
    vectors = refs[:CHUNKS]
    sent_ref, left_ref, links_x_ref, hop_ref, u_ref, table_ref, fold_ref = refs[CHUNKS:]
    _, _, part_modes, plane = vectors[0].shape
    all_modes = part_modes * CHUNKS
    for q in range(CHUNKS):
        for c in range(3):
            for part in range(2):
                left_ref[
                    part * all_modes + q * part_modes : part * all_modes + (q + 1) * part_modes,
                    c * plane : (c + 1) * plane,
                ] = vectors[q][c, part]
    tiles = plane // LANES
    site = iota((tiles, LANES), 0) * LANES + iota((tiles, LANES), 1) + where_ref[0] * plane
    store_links(links_x_ref, seed_ref[0], site)

    def load(part, colour, rows, t):
        return left_ref[
            pl.ds(pl.multiple_of(part * all_modes + rows.start, 16), 16),
            colour * plane + t * LANES : colour * plane + (t + 1) * LANES,
        ]

    for d, shift in ((1, "y"), (2, "z")):
        store_links(u_ref, seed_ref[d], site)
        hop(load, hop_ref, u_ref, all_modes, plane, shift)
        real, imag = products(hop_ref, left_ref, all_modes, all_modes)
        store_table(table_ref, fold_ref, (d - 1) * 2 * TM * TM, real, imag, slots)
    send_tiles(sent_ref, owner_ref, table_ref, slots, 2)


def hop_received(vector_ref, links_ref, left_hbm, left_ref, hop_ref, sem):
    copy = pltpu.make_async_copy(left_hbm, left_ref, sem)
    copy.start()
    _, _, modes, plane = vector_ref.shape

    def load(part, colour, rows, t):
        return vector_ref[colour, part, rows, t * LANES : (t + 1) * LANES]

    hop(load, hop_ref, links_ref, modes, plane, None)
    copy.wait()
    return products(hop_ref, left_ref, modes, left_ref.shape[0] // 2)


def outer_kernel(vector_ref, links_ref, left_hbm, out_ref, left_ref, hop_ref, sem):
    real, imag = hop_received(vector_ref, links_ref, left_hbm, left_ref, hop_ref, sem)
    out_ref[0] = real
    out_ref[1] = imag


def last_kernel(slots, owner_ref, *refs):
    before = refs[: CHUNKS - 1]
    (vector_ref, links_ref, left_hbm, sent_ref, left_ref, hop_ref, sem, table_ref, fold_ref) = refs[
        CHUNKS - 1 :
    ]
    real, imag = hop_received(vector_ref, links_ref, left_hbm, left_ref, hop_ref, sem)
    real = jnp.concatenate([b[0] for b in before] + [real], 0)
    imag = jnp.concatenate([b[1] for b in before] + [imag], 0)
    store_table(table_ref, fold_ref, 0, real, imag, slots)
    send_tiles(sent_ref, owner_ref, table_ref, slots, 1)


def finish_kernel(normalise, slots_x, slots_yz, x_ref, yz_ref, out_ref):
    here = out_ref.shape[0]
    start = 0
    for slots, ref in ((slots_x, x_ref), (slots_yz, yz_ref)):
        total = ref[0].astype(F32)
        for device in range(1, ref.shape[0]):
            total = total + ref[device].astype(F32)
        total = total * normalise
        for group in range(slots.groups):
            first = group * slots.per_group
            count = min(slots.per_group, here - first)
            out_ref[first : first + count, start : start + slots.columns] = total[
                :count, group * slots.columns : (group + 1) * slots.columns
            ]
        start += slots.columns


def params(mib):
    return pltpu.CompilerParams(vmem_limit_bytes=mib * 1024 * 1024)


def cost(flops, moved):
    return pl.CostEstimate(flops=flops, bytes_accessed=moved, transcendentals=0)


def per_device(eigvecs, link_seed, ownership):
    modes, _, _, layers, plane = eigvecs.shape
    assert layers == 1
    devices = lax.axis_size("sx")
    here = ownership.shape[0] // devices
    part_modes = modes // CHUNKS
    depth = 3 * plane
    tiles = plane // LANES
    slots_x = Slots(modes, here, 1)
    slots_yz = Slots(modes, here, 2)
    vmem = pl.BlockSpec(memory_space=pltpu.VMEM)
    smem = pl.BlockSpec(memory_space=pltpu.SMEM)
    anywhere = pl.BlockSpec(memory_space=pl.ANY)

    route = [(i, (i - 1) % devices) for i in range(devices)]
    own, upper = [], []
    for q in range(CHUNKS):
        piece = eigvecs[q * part_modes : (q + 1) * part_modes, :, :, 0]
        piece = piece.transpose(2, 1, 0, 3)
        own.append(piece)
        upper.append(lax.ppermute(piece, "sx", route))

    where = lax.axis_index("sx").reshape(1).astype(jnp.int32)
    flops = 4 * modes * modes * depth * 2

    sent_yz, left, links_x = pl.pallas_call(
        functools.partial(inner_kernel, slots_yz),
        name="inner_directions",
        out_shape=(
            jax.ShapeDtypeStruct((devices, slots_yz.sent, LANES), BF16),
            jax.ShapeDtypeStruct((2 * modes, depth), BF16),
            jax.ShapeDtypeStruct((18, tiles, LANES), F32),
        ),
        in_specs=[smem, smem, vmem] + [vmem] * CHUNKS,
        out_specs=(vmem, vmem, vmem),
        scratch_shapes=[
            pltpu.VMEM((2 * modes, depth), BF16),
            pltpu.VMEM((18, tiles, LANES), F32),
            pltpu.VMEM((slots_yz.columns, slots_yz.depth), F32),
            pltpu.VMEM((TM // 2, modes, LANES), F32),
        ],
        compiler_params=params(48),
        cost_estimate=cost(4 * flops, 12 * 2**20),
    )(link_seed, where, slots_yz.arrange(ownership, devices), *own)

    received_yz = lax.all_to_all(sent_yz, "sx", 0, 0)

    scratch = [
        pltpu.VMEM((2 * modes, depth), BF16),
        pltpu.VMEM((2 * part_modes, depth), BF16),
        pltpu.SemaphoreType.DMA,
    ]
    partial = [
        pl.pallas_call(
            outer_kernel,
            name="outer_direction",
            out_shape=jax.ShapeDtypeStruct((2, part_modes, modes), F32),
            in_specs=[vmem, vmem, anywhere],
            out_specs=vmem,
            scratch_shapes=scratch,
            compiler_params=params(32),
            cost_estimate=cost(flops // CHUNKS, 4 * 2**20),
        )(upper[q], links_x, left)
        for q in range(CHUNKS - 1)
    ]
    sent_x = pl.pallas_call(
        functools.partial(last_kernel, slots_x),
        name="outer_direction_tiles",
        out_shape=jax.ShapeDtypeStruct((devices, slots_x.sent, LANES), BF16),
        in_specs=[vmem] + [vmem] * (CHUNKS - 1) + [vmem, vmem, anywhere],
        out_specs=vmem,
        scratch_shapes=scratch
        + [
            pltpu.VMEM((slots_x.columns, slots_x.depth), F32),
            pltpu.VMEM((TM // 2, modes, LANES), F32),
        ],
        compiler_params=params(48),
        cost_estimate=cost(flops, 8 * 2**20),
    )(slots_x.arrange(ownership, devices), *partial, upper[-1], links_x, left)
    received_x = lax.all_to_all(sent_x, "sx", 0, 0)

    extent_x = layers * devices
    normalise = 1.0 / math.sqrt(12.0 * extent_x * plane)
    return pl.pallas_call(
        functools.partial(finish_kernel, normalise, slots_x, slots_yz),
        name="sum_of_devices",
        out_shape=jax.ShapeDtypeStruct((here, slots_x.columns + slots_yz.columns), F32),
        in_specs=[vmem, vmem],
        out_specs=vmem,
        compiler_params=params(32),
    )(received_x, received_yz)


def solution(mesh):
    return jax.shard_map(
        per_device,
        mesh=mesh,
        in_specs=(P("cfg", None, None, "sx", None), P("cfg"), P()),
        out_specs=P(("cfg", "sx"), None),
        check_vma=False,
    )
```

```python
import functools
import math

import jax
import jax.numpy as jnp
from jax import lax
from jax.experimental import pallas as pl
from jax.experimental.pallas import tpu as pltpu
from jax.sharding import PartitionSpec as P

TM = 4
NZ = 64
LANES = 128
MODULUS = 46337
CHUNKS = 4
STEP = 32
F32 = jnp.float32
BF16 = jnp.bfloat16
NT = (((1,), (1,)), ((), ()))


def dot(left, right, dims=(((1,), (0,)), ((), ()))):
    return lax.dot_general(left, right, dims, preferred_element_type=F32)


def iota(shape, axis):
    return lax.broadcasted_iota(jnp.int32, shape, axis)


def round_up(value, step):
    return -(-value // step) * step


def divide(value):
    quotient = (value.astype(F32) * (1.0 / MODULUS)).astype(jnp.int32)
    rest = value - quotient * MODULUS
    below, above = rest < 0, rest >= MODULUS
    rest = jnp.where(below, rest + MODULUS, jnp.where(above, rest - MODULUS, rest))
    quotient = jnp.where(below, quotient - 1, jnp.where(above, quotient + 1, quotient))
    return quotient, rest


def link_angles(seed, site):
    high, low = divide(site)
    mixed = divide(seed * seed + low)[1]
    mixed = divide(mixed * mixed + high * 977 + 31)[1]
    angles = []
    for index in range(7):
        g = divide(mixed + (5171 * index + 1))[1]
        g = divide(g * g + low)[1]
        g = divide(g * g + 12345)[1]
        angles.append(g.astype(F32) * (2.0 * math.pi / MODULUS) - math.pi)
    return angles


def store_links(u_ref, seed, site):
    a = link_angles(seed, site)
    ca, sa = jnp.cos(a[0]), jnp.sin(a[0])
    cb, sb = jnp.cos(a[1]), jnp.sin(a[1])
    cg, sg = jnp.cos(a[2]), jnp.sin(a[2])
    rotation = [
        [ca * cb * cg - sa * sg, -ca * cb * sg - sa * cg, ca * sb],
        [sa * cb * cg + ca * sg, -sa * cb * sg + ca * cg, sa * sb],
        [-sb * cg, sb * sg, cb],
    ]
    left = [a[3], a[4], -a[3] - a[4]]
    right = [a[5], a[6], -a[5] - a[6]]
    for c in range(3):
        for s in range(3):
            phase = left[c] + right[s]
            u_ref[2 * (3 * c + s)] = rotation[c][s] * jnp.cos(phase)
            u_ref[2 * (3 * c + s) + 1] = rotation[c][s] * jnp.sin(phase)


def hop(load, out_ref, u_ref, modes, plane, shift):
    tiles = plane // LANES
    wide = (STEP // 8, 8, LANES)
    for t in range(tiles):
        u = [jnp.broadcast_to(u_ref[k, t : t + 1, :], (8, LANES)) for k in range(18)]

        def body(block, carry, t=t, u=u):
            rows = pl.ds(pl.multiple_of(block * STEP, STEP), STEP)
            lane = iota((STEP, LANES), 1)
            v = []
            for source in range(3):
                for part in range(2):
                    x = load(part, source, rows, t).astype(F32)
                    if shift == "y":
                        above = load(part, source, rows, (t + 1) % tiles).astype(F32)
                        x = pltpu.roll(jnp.where(lane < NZ, above, x), NZ, 1)
                    elif shift == "z":
                        following = jnp.where(lane % NZ == NZ - 1, lane + 1 - NZ, lane + 1)
                        x = jnp.take_along_axis(x, following, axis=1)
                    v.append(x.reshape(wide))
            for c in range(3):
                real = imag = None
                for s in range(3):
                    ur, ui = u[2 * (3 * c + s)], u[2 * (3 * c + s) + 1]
                    re, im = v[2 * s], v[2 * s + 1]
                    real = ur * re if real is None else real + ur * re
                    real = real - ui * im
                    imag = ur * im if imag is None else imag + ur * im
                    imag = imag + ui * re
                lanes = slice(c * plane + t * LANES, c * plane + (t + 1) * LANES)
                out_ref[rows, lanes] = real.reshape(STEP, LANES).astype(BF16)
                low = pl.ds(pl.multiple_of(modes + block * STEP, STEP), STEP)
                out_ref[low, lanes] = imag.reshape(STEP, LANES).astype(BF16)
            return carry

        lax.fori_loop(0, modes // STEP, body, 0)


def products(hop_ref, left_ref, modes, all_modes):
    by_real = dot(hop_ref[...], left_ref[:all_modes, :], NT)
    by_imag = dot(hop_ref[...], left_ref[all_modes:, :], NT)
    real = by_real[:modes] + by_imag[modes:]
    imag = by_real[modes:] - by_imag[:modes]
    return real, imag


class Slots:
    def __init__(self, all_modes, slots, directions):
        self.tiles = all_modes // TM
        assert 2 * self.tiles == LANES
        self.half = self.tiles // 2
        self.depth = round_up((self.half + 1) * self.tiles, 2 * LANES)
        self.columns = 2 * TM * TM * directions
        self.groups = LANES // self.columns
        self.per_group = -(-slots // self.groups)
        self.rows = round_up(self.per_group, 8)
        self.sent = round_up(self.rows, 16)

    def arrange(self, ownership, devices):
        slots = ownership.shape[0] // devices
        spread = jnp.pad(
            ownership.reshape(devices, slots),
            ((0, 0), (0, self.groups * self.per_group - slots)),
            constant_values=-1,
        ).reshape(devices, self.groups, self.per_group)
        spread = jnp.pad(
            spread, ((0, 0), (0, 0), (0, self.rows - self.per_group)), constant_values=-1
        )
        return spread.reshape(devices, self.groups * self.rows, 1)

    def codes(self):
        lane = iota((1, self.depth), 1)
        first, second = lane // self.tiles, lane % self.tiles
        last = self.tiles - 1
        diagonal = first == self.half
        turned = jnp.logical_or(diagonal, second < first)
        i = jnp.where(diagonal, last - second, jnp.where(turned, last - first, first))
        j = jnp.where(turned, last - second, second)
        pair = i * self.tiles - (i * (i - 1)) // 2 + (j - i)
        known = jnp.logical_and(
            first <= self.half, jnp.logical_not(jnp.logical_and(diagonal, second >= self.half))
        )
        return jnp.where(known, pair, -2)


def store_table(table_ref, fold_ref, base, real, imag, slots):
    all_modes = real.shape[0]
    n, half = slots.tiles, slots.half
    parts = [real.T - real, imag.T + imag]

    def choose(count, width, turned):
        row, column = iota((count, all_modes), 0), iota((count, all_modes), 1)
        r, i = row // width, row % width
        if turned:
            i = n - 1 - i
        return (column == i * TM + r).astype(F32).astype(BF16)

    pick = [choose(TM * half, half, turned) for turned in (False, True)]
    spread = [choose(all_modes, n, turned) for turned in (False, True)]
    row_i = iota((TM * half, all_modes), 0) % half
    lane_j = iota((TM * half, all_modes), 1) % n
    corners = []
    for part in range(2):
        entries = parts[part].astype(BF16)
        straight, turned = [
            dot(dot(pick[k], entries).astype(BF16), spread[k], NT) for k in range(2)
        ]
        folded = jnp.where(lane_j >= row_i, straight, turned)
        for k in range(TM // 2):
            fold_ref[k, part * TM * half : (part + 1) * TM * half, :] = folded[
                :, k * LANES : (k + 1) * LANES
            ]
        diagonal = jnp.where(lane_j == row_i, turned, 0.0)
        for r in range(TM):
            corners.append(
                jnp.sum(diagonal[r * half : (r + 1) * half], axis=0, keepdims=True)
            )
    low = iota((2 * TM, LANES), 1) < n

    def split(even, odd, lanes):
        for pair in range(TM // 2):
            e, o = even[pair], odd[pair]
            top = base + 2 * pair * 2 * TM
            table_ref[top : top + 2 * TM, lanes] = jnp.where(low, e, pltpu.roll(o, n, 1))
            table_ref[top + 2 * TM : top + 4 * TM, lanes] = jnp.where(
                low, pltpu.roll(e, n, 1), o
            )

    halves = [slice(k * LANES, (k + 1) * LANES) for k in range(TM // 2)]
    for two in range(half // 2):
        even = [fold_ref[k, pl.ds(2 * two, 2 * TM, stride=half), :] for k in range(TM // 2)]
        odd = [fold_ref[k, pl.ds(2 * two + 1, 2 * TM, stride=half), :] for k in range(TM // 2)]
        split(even, odd, slice(two * LANES, (two + 1) * LANES))
    corner = jnp.concatenate(corners, 0)
    nothing = jnp.zeros((2 * TM, LANES), F32)
    start = half * n
    split([corner[:, h] for h in halves], [nothing] * len(halves), slice(start, start + LANES))
    rest = slots.depth - start - LANES
    if rest:
        table_ref[base : base + 2 * TM * TM, start + LANES :] = jnp.zeros(
            (2 * TM * TM, rest), F32
        )


def send_tiles(out_ref, owner_ref, table, slots, directions):
    block = 2 * TM * TM
    row, column = iota((LANES, slots.columns), 0), iota((LANES, slots.columns), 1)
    entry = row % slots.columns
    direction, inside = entry // block, entry % block
    u = inside % TM
    part_r = inside // TM
    order = column == direction * block + u * (2 * TM) + part_r
    table = dot(order.astype(F32).astype(BF16), table).astype(BF16)
    codes = slots.codes()
    lane_group = iota((slots.rows, LANES), 1) // slots.columns

    def body(step, carry):
        for device in (2 * step, 2 * step + 1):
            owners = owner_ref[device]
            chosen = (owners == codes).astype(F32).astype(BF16)
            picked = dot(chosen, table, NT)
            packed = picked[: slots.rows]
            for group in range(1, slots.groups):
                piece = picked[group * slots.rows : (group + 1) * slots.rows]
                packed = jnp.where(lane_group == group, piece, packed)
            if slots.sent > slots.rows:
                packed = jnp.concatenate(
                    [packed, jnp.zeros((slots.sent - slots.rows, LANES), F32)], 0
                )
            out_ref[device] = packed.astype(BF16)
        return carry

    lax.fori_loop(0, out_ref.shape[0] // 2, body, 0)


def links_kernel(seed_ref, where_ref, out_ref):
    _, _, tiles, _ = out_ref.shape
    site = iota((tiles, LANES), 0) * LANES + iota((tiles, LANES), 1)
    site = site + where_ref[0] * (tiles * LANES)
    for d in range(3):
        store_links(out_ref.at[d], seed_ref[d], site)


def left_kernel(planar_ref, left_ref):
    _, _, _, part_modes, plane = planar_ref.shape
    all_modes = part_modes * CHUNKS
    for q in range(CHUNKS):
        for c in range(3):
            for part in range(2):
                start = part * all_modes + q * part_modes
                left_ref[start : start + part_modes, c * plane : (c + 1) * plane] = planar_ref[
                    q, c, part
                ]


def inner_kernel(slots, d, shift, left_ref, links_ref, out_ref, hop_ref, table_ref, fold_ref):
    all_modes, plane = left_ref.shape[0] // 2, left_ref.shape[1] // 3

    def load(part, colour, rows, t):
        return left_ref[
            pl.ds(pl.multiple_of(part * all_modes + rows.start, STEP), STEP),
            colour * plane + t * LANES : colour * plane + (t + 1) * LANES,
        ]

    hop(load, hop_ref, links_ref.at[d], all_modes, plane, shift)
    real, imag = products(hop_ref, left_ref, all_modes, all_modes)
    store_table(table_ref, fold_ref, 0, real, imag, slots)
    out_ref[...] = table_ref[...].astype(BF16)


def send_kernel(slots, directions, owner_ref, *refs):
    tables, out_ref = refs[:directions], refs[directions]
    table = jnp.concatenate([t[...] for t in tables], 0)
    send_tiles(out_ref, owner_ref, table, slots, directions)


def hop_received(vector_ref, links_ref, left_ref, hop_ref):
    _, _, modes, plane = vector_ref.shape

    def load(part, colour, rows, t):
        return vector_ref[colour, part, rows, t * LANES : (t + 1) * LANES]

    hop(load, hop_ref, links_ref.at[0], modes, plane, None)
    return products(hop_ref, left_ref, modes, left_ref.shape[0] // 2)


def outer_kernel(vector_ref, links_ref, left_ref, out_ref, hop_ref):
    out_ref[0], out_ref[1] = hop_received(vector_ref, links_ref, left_ref, hop_ref)


def last_kernel(slots, owner_ref, *refs):
    before = refs[: CHUNKS - 1]
    vector_ref, links_ref, left_ref, sent_ref, hop_ref, table_ref, fold_ref = refs[CHUNKS - 1 :]
    real, imag = hop_received(vector_ref, links_ref, left_ref, hop_ref)
    real = jnp.concatenate([b[0] for b in before] + [real], 0)
    imag = jnp.concatenate([b[1] for b in before] + [imag], 0)
    store_table(table_ref, fold_ref, 0, real, imag, slots)
    send_tiles(sent_ref, owner_ref, table_ref[...].astype(BF16), slots, 1)


def finish_kernel(normalise, slots_x, slots_yz, x_ref, yz_ref, out_ref):
    here = out_ref.shape[0]
    start = 0
    for slots, ref in ((slots_x, x_ref), (slots_yz, yz_ref)):
        total = ref[0].astype(F32)
        for device in range(1, ref.shape[0]):
            total = total + ref[device].astype(F32)
        total = total * normalise
        for group in range(slots.groups):
            first = group * slots.per_group
            count = min(slots.per_group, here - first)
            out_ref[first : first + count, start : start + slots.columns] = total[
                :count, group * slots.columns : (group + 1) * slots.columns
            ]
        start += slots.columns


def params(mib):
    return pltpu.CompilerParams(vmem_limit_bytes=mib * 1024 * 1024)


def cost(flops, moved):
    return pl.CostEstimate(flops=flops, bytes_accessed=moved, transcendentals=0)


def per_device(eigvecs, link_seed, ownership):
    modes, _, _, layers, plane = eigvecs.shape
    assert layers == 1
    devices = lax.axis_size("sx")
    here = ownership.shape[0] // devices
    part_modes = modes // CHUNKS
    depth = 3 * plane
    tiles = plane // LANES
    slots_x = Slots(modes, here, 1)
    slots_yz = Slots(modes, here, 2)
    vmem = pl.BlockSpec(memory_space=pltpu.VMEM)
    smem = pl.BlockSpec(memory_space=pltpu.SMEM)

    route = [(i, (i - 1) % devices) for i in range(devices)]
    planar = eigvecs.reshape(CHUNKS, part_modes, 2, 3, plane).transpose(0, 3, 2, 1, 4)
    planar = lax.optimization_barrier(planar)
    upper = [lax.ppermute(planar[q], "sx", route) for q in range(CHUNKS)]

    where = lax.axis_index("sx").reshape(1).astype(jnp.int32)
    flops = 4 * modes * modes * depth * 2

    links = pl.pallas_call(
        links_kernel,
        name="links",
        out_shape=jax.ShapeDtypeStruct((3, 18, tiles, LANES), F32),
        in_specs=[smem, smem],
        out_specs=vmem,
        compiler_params=params(8),
        cost_estimate=cost(2**20, 2**18),
    )(link_seed, where)
    left = pl.pallas_call(
        left_kernel,
        name="left_side",
        out_shape=jax.ShapeDtypeStruct((2 * modes, depth), BF16),
        in_specs=[vmem],
        out_specs=vmem,
        compiler_params=params(16),
        cost_estimate=cost(0, 6 * 2**20),
    )(planar)

    table_scratch = [
        pltpu.VMEM((slots_x.columns, slots_x.depth), F32),
        pltpu.VMEM((TM // 2, modes, LANES), F32),
    ]
    tables = [
        pl.pallas_call(
            functools.partial(inner_kernel, slots_x, d, shift),
            name="direction_" + shift,
            out_shape=jax.ShapeDtypeStruct((slots_x.columns, slots_x.depth), BF16),
            in_specs=[vmem, vmem],
            out_specs=vmem,
            scratch_shapes=[pltpu.VMEM((2 * modes, depth), BF16)] + table_scratch,
            compiler_params=params(24),
            cost_estimate=cost(2 * flops, 4 * 2**20),
        )(left, links)
        for d, shift in ((1, "y"), (2, "z"))
    ]
    sent_yz = pl.pallas_call(
        functools.partial(send_kernel, slots_yz, 2),
        name="send_inner",
        out_shape=jax.ShapeDtypeStruct((devices, slots_yz.sent, LANES), BF16),
        in_specs=[vmem] * 3,
        out_specs=vmem,
        compiler_params=params(24),
        cost_estimate=cost(flops, 2**20),
    )(slots_yz.arrange(ownership, devices), *tables)
    received_yz = lax.all_to_all(sent_yz, "sx", 0, 0)

    scratch = [pltpu.VMEM((2 * part_modes, depth), BF16)]
    partial = [
        pl.pallas_call(
            outer_kernel,
            name="outer_direction",
            out_shape=jax.ShapeDtypeStruct((2, part_modes, modes), F32),
            in_specs=[vmem, vmem, vmem],
            out_specs=vmem,
            scratch_shapes=scratch,
            compiler_params=params(16),
            cost_estimate=cost(flops // CHUNKS, 4 * 2**20),
        )(upper[q], links, left)
        for q in range(CHUNKS - 1)
    ]
    sent_x = pl.pallas_call(
        functools.partial(last_kernel, slots_x),
        name="outer_direction_tiles",
        out_shape=jax.ShapeDtypeStruct((devices, slots_x.sent, LANES), BF16),
        in_specs=[vmem] + [vmem] * (CHUNKS - 1) + [vmem, vmem, vmem],
        out_specs=vmem,
        scratch_shapes=scratch + table_scratch,
        compiler_params=params(24),
        cost_estimate=cost(flops, 8 * 2**20),
    )(slots_x.arrange(ownership, devices), *partial, upper[-1], links, left)
    received_x = lax.all_to_all(sent_x, "sx", 0, 0)

    extent_x = layers * devices
    normalise = 1.0 / math.sqrt(12.0 * extent_x * plane)
    return pl.pallas_call(
        functools.partial(finish_kernel, normalise, slots_x, slots_yz),
        name="sum_of_devices",
        out_shape=jax.ShapeDtypeStruct((here, slots_x.columns + slots_yz.columns), F32),
        in_specs=[vmem, vmem],
        out_specs=vmem,
        compiler_params=params(32),
    )(received_x, received_yz)


def solution(mesh):
    return jax.shard_map(
        per_device,
        mesh=mesh,
        in_specs=(P("cfg", None, None, "sx", None), P("cfg"), P()),
        out_specs=P(("cfg", "sx"), None),
        check_vma=False,
    )
```

```python
import functools
import math

import jax
import jax.numpy as jnp
from jax import lax
from jax.experimental import pallas as pl
from jax.experimental.pallas import tpu as pltpu
from jax.sharding import PartitionSpec as P

TM = 4
NZ = 64
LANES = 128
MODULUS = 46337
CHUNKS = 4
STEP = 32
F32 = jnp.float32
BF16 = jnp.bfloat16
NT = (((1,), (1,)), ((), ()))


def dot(left, right, dims=(((1,), (0,)), ((), ()))):
    return lax.dot_general(left, right, dims, preferred_element_type=F32)


def iota(shape, axis):
    return lax.broadcasted_iota(jnp.int32, shape, axis)


def round_up(value, step):
    return -(-value // step) * step


def divide(value):
    quotient = (value.astype(F32) * (1.0 / MODULUS)).astype(jnp.int32)
    rest = value - quotient * MODULUS
    below, above = rest < 0, rest >= MODULUS
    rest = jnp.where(below, rest + MODULUS, jnp.where(above, rest - MODULUS, rest))
    quotient = jnp.where(below, quotient - 1, jnp.where(above, quotient + 1, quotient))
    return quotient, rest


def link_angles(seed, site):
    high, low = divide(site)
    mixed = divide(seed * seed + low)[1]
    mixed = divide(mixed * mixed + high * 977 + 31)[1]
    angles = []
    for index in range(7):
        g = divide(mixed + (5171 * index + 1))[1]
        g = divide(g * g + low)[1]
        g = divide(g * g + 12345)[1]
        angles.append(g.astype(F32) * (2.0 * math.pi / MODULUS) - math.pi)
    return angles


def store_links(u_ref, seed, site):
    a = link_angles(seed, site)
    ca, sa = jnp.cos(a[0]), jnp.sin(a[0])
    cb, sb = jnp.cos(a[1]), jnp.sin(a[1])
    cg, sg = jnp.cos(a[2]), jnp.sin(a[2])
    rotation = [
        [ca * cb * cg - sa * sg, -ca * cb * sg - sa * cg, ca * sb],
        [sa * cb * cg + ca * sg, -sa * cb * sg + ca * cg, sa * sb],
        [-sb * cg, sb * sg, cb],
    ]
    left = [a[3], a[4], -a[3] - a[4]]
    right = [a[5], a[6], -a[5] - a[6]]
    for c in range(3):
        for s in range(3):
            phase = left[c] + right[s]
            u_ref[2 * (3 * c + s)] = rotation[c][s] * jnp.cos(phase)
            u_ref[2 * (3 * c + s) + 1] = rotation[c][s] * jnp.sin(phase)


def hop(load, out_ref, u_ref, modes, plane, shift):
    tiles = plane // LANES
    wide = (STEP // 8, 8, LANES)
    for t in range(tiles):
        u = [jnp.broadcast_to(u_ref[k, t : t + 1, :], (8, LANES)) for k in range(18)]

        def body(block, carry, t=t, u=u):
            rows = pl.ds(pl.multiple_of(block * STEP, STEP), STEP)
            lane = iota((STEP, LANES), 1)
            v = []
            for source in range(3):
                for part in range(2):
                    x = load(part, source, rows, t).astype(F32)
                    if shift == "y":
                        above = load(part, source, rows, (t + 1) % tiles).astype(F32)
                        x = pltpu.roll(jnp.where(lane < NZ, above, x), NZ, 1)
                    elif shift == "z":
                        following = jnp.where(lane % NZ == NZ - 1, lane + 1 - NZ, lane + 1)
                        x = jnp.take_along_axis(x, following, axis=1)
                    v.append(x.reshape(wide))
            for c in range(3):
                real = imag = None
                for s in range(3):
                    ur, ui = u[2 * (3 * c + s)], u[2 * (3 * c + s) + 1]
                    re, im = v[2 * s], v[2 * s + 1]
                    real = ur * re if real is None else real + ur * re
                    real = real - ui * im
                    imag = ur * im if imag is None else imag + ur * im
                    imag = imag + ui * re
                lanes = slice(c * plane + t * LANES, c * plane + (t + 1) * LANES)
                out_ref[rows, lanes] = real.reshape(STEP, LANES).astype(BF16)
                low = pl.ds(pl.multiple_of(modes + block * STEP, STEP), STEP)
                out_ref[low, lanes] = imag.reshape(STEP, LANES).astype(BF16)
            return carry

        lax.fori_loop(0, modes // STEP, body, 0)


def products(hopped, left):
    return dot(hopped, left, NT)


def combine(blocks):
    modes, all_modes = blocks.shape[0] // 2, blocks.shape[1] // 2
    real = blocks[:modes, :all_modes] + blocks[modes:, all_modes:]
    imag = blocks[modes:, :all_modes] - blocks[:modes, all_modes:]
    return real, imag


class Slots:
    def __init__(self, all_modes, slots, directions):
        self.tiles = all_modes // TM
        assert 2 * self.tiles == LANES
        self.half = self.tiles // 2
        self.depth = round_up((self.half + 1) * self.tiles, 2 * LANES)
        self.columns = 2 * TM * TM * directions
        self.groups = LANES // self.columns
        self.per_group = -(-slots // self.groups)
        self.rows = round_up(self.per_group, 8)

    def arrange(self, ownership, devices):
        slots = ownership.shape[0] // devices
        spread = jnp.pad(
            ownership.reshape(devices, slots),
            ((0, 0), (0, self.groups * self.per_group - slots)),
            constant_values=-1,
        ).reshape(devices, self.groups, self.per_group)
        spread = jnp.pad(
            spread, ((0, 0), (0, 0), (0, self.rows - self.per_group)), constant_values=-1
        )
        return spread.reshape(devices, self.groups * self.rows, 1)

    def codes(self):
        lane = iota((1, self.depth), 1)
        first, second = lane // self.tiles, lane % self.tiles
        last = self.tiles - 1
        diagonal = first == self.half
        turned = jnp.logical_or(diagonal, second < first)
        i = jnp.where(diagonal, last - second, jnp.where(turned, last - first, first))
        j = jnp.where(turned, last - second, second)
        pair = i * self.tiles - (i * (i - 1)) // 2 + (j - i)
        known = jnp.logical_and(
            first <= self.half, jnp.logical_not(jnp.logical_and(diagonal, second >= self.half))
        )
        return jnp.where(known, pair, -2)


def store_table(table_ref, fold_ref, base, real, imag, slots):
    all_modes = real.shape[0]
    n, half = slots.tiles, slots.half
    parts = [real.T - real, imag.T + imag]

    def choose(count, width, turned):
        row, column = iota((count, all_modes), 0), iota((count, all_modes), 1)
        r, i = row // width, row % width
        if turned:
            i = n - 1 - i
        return (column == i * TM + r).astype(F32).astype(BF16)

    pick = [choose(TM * half, half, turned) for turned in (False, True)]
    spread = [choose(all_modes, n, turned) for turned in (False, True)]
    row_i = iota((TM * half, all_modes), 0) % half
    lane_j = iota((TM * half, all_modes), 1) % n
    corners = []
    for part in range(2):
        entries = parts[part].astype(BF16)
        straight, turned = [
            dot(dot(pick[k], entries).astype(BF16), spread[k], NT) for k in range(2)
        ]
        folded = jnp.where(lane_j >= row_i, straight, turned)
        for k in range(TM // 2):
            fold_ref[k, part * TM * half : (part + 1) * TM * half, :] = folded[
                :, k * LANES : (k + 1) * LANES
            ]
        diagonal = jnp.where(lane_j == row_i, turned, 0.0)
        for r in range(TM):
            corners.append(
                jnp.sum(diagonal[r * half : (r + 1) * half], axis=0, keepdims=True)
            )
    low = iota((2 * TM, LANES), 1) < n

    def split(even, odd, lanes):
        for pair in range(TM // 2):
            e, o = even[pair], odd[pair]
            top = base + 2 * pair * 2 * TM
            table_ref[top : top + 2 * TM, lanes] = jnp.where(low, e, pltpu.roll(o, n, 1))
            table_ref[top + 2 * TM : top + 4 * TM, lanes] = jnp.where(
                low, pltpu.roll(e, n, 1), o
            )

    halves = [slice(k * LANES, (k + 1) * LANES) for k in range(TM // 2)]
    for two in range(half // 2):
        even = [fold_ref[k, pl.ds(2 * two, 2 * TM, stride=half), :] for k in range(TM // 2)]
        odd = [fold_ref[k, pl.ds(2 * two + 1, 2 * TM, stride=half), :] for k in range(TM // 2)]
        split(even, odd, slice(two * LANES, (two + 1) * LANES))
    corner = jnp.concatenate(corners, 0)
    nothing = jnp.zeros((2 * TM, LANES), F32)
    start = half * n
    split([corner[:, h] for h in halves], [nothing] * len(halves), slice(start, start + LANES))
    rest = slots.depth - start - LANES
    if rest:
        table_ref[base : base + 2 * TM * TM, start + LANES :] = jnp.zeros(
            (2 * TM * TM, rest), F32
        )


def send_tiles(out_ref, owner_ref, table, slots, directions):
    block = 2 * TM * TM
    row, column = iota((LANES, slots.columns), 0), iota((LANES, slots.columns), 1)
    entry = row % slots.columns
    direction, inside = entry // block, entry % block
    u = inside % TM
    part_r = inside // TM
    order = column == direction * block + u * (2 * TM) + part_r
    table = dot(order.astype(F32).astype(BF16), table).astype(BF16)
    codes = slots.codes()
    lane_group = iota((slots.rows, LANES), 1) // slots.columns

    def body(step, carry):
        for device in (2 * step, 2 * step + 1):
            owners = owner_ref[device]
            chosen = (owners == codes).astype(F32).astype(BF16)
            picked = dot(chosen, table, NT)
            packed = picked[: slots.rows]
            for group in range(1, slots.groups):
                piece = picked[group * slots.rows : (group + 1) * slots.rows]
                packed = jnp.where(lane_group == group, piece, packed)
            out_ref[device] = packed.astype(BF16)
        return carry

    lax.fori_loop(0, out_ref.shape[0] // 2, body, 0)


def links_kernel(seed_ref, where_ref, out_ref):
    _, _, tiles, _ = out_ref.shape
    site = iota((tiles, LANES), 0) * LANES + iota((tiles, LANES), 1)
    site = site + where_ref[0] * (tiles * LANES)
    for d in range(3):
        store_links(out_ref.at[d], seed_ref[d], site)


def split_kernel(whole_ref, *refs):
    parts, sems = refs[:CHUNKS], refs[CHUNKS]
    count = parts[0].shape[0]
    copies = [
        pltpu.make_async_copy(whole_ref.at[pl.ds(q * count, count)], parts[q], sems.at[q])
        for q in range(CHUNKS)
    ]
    for copy in copies:
        copy.start()
    for copy in copies:
        copy.wait()


def left_kernel(planar_ref, left_ref):
    _, _, all_modes, plane = planar_ref.shape
    for c in range(3):
        for part in range(2):
            left_ref[
                part * all_modes : (part + 1) * all_modes, c * plane : (c + 1) * plane
            ] = planar_ref[c, part]


def hop_kernel(d, shift, vector_ref, links_ref, out_ref):
    _, _, modes, plane = vector_ref.shape

    def load(part, colour, rows, t):
        return vector_ref[colour, part, rows, t * LANES : (t + 1) * LANES]

    hop(load, out_ref, links_ref.at[d], modes, plane, shift)


def table_kernel(slots, blocks_ref, out_ref, table_ref, fold_ref):
    real, imag = combine(blocks_ref[...])
    store_table(table_ref, fold_ref, 0, real, imag, slots)
    out_ref[...] = table_ref[...].astype(BF16)


def send_kernel(slots, directions, owner_ref, *refs):
    tables, out_ref = refs[:directions], refs[directions]
    table = jnp.concatenate([t[...] for t in tables], 0)
    send_tiles(out_ref, owner_ref, table, slots, directions)


def last_kernel(slots, owner_ref, *refs):
    chunks = [combine(r[...]) for r in refs[:CHUNKS]]
    sent_ref, table_ref, fold_ref = refs[CHUNKS:]
    real = jnp.concatenate([c[0] for c in chunks], 0)
    imag = jnp.concatenate([c[1] for c in chunks], 0)
    store_table(table_ref, fold_ref, 0, real, imag, slots)
    send_tiles(sent_ref, owner_ref, table_ref[...].astype(BF16), slots, 1)


def finish_kernel(normalise, slots_x, slots_yz, x_ref, yz_ref, out_ref):
    here = out_ref.shape[0]
    start = 0
    for slots, ref in ((slots_x, x_ref), (slots_yz, yz_ref)):
        total = ref[0].astype(F32)
        for device in range(1, ref.shape[0]):
            total = total + ref[device].astype(F32)
        total = total * normalise
        for group in range(slots.groups):
            first = group * slots.per_group
            count = min(slots.per_group, here - first)
            out_ref[first : first + count, start : start + slots.columns] = total[
                :count, group * slots.columns : (group + 1) * slots.columns
            ]
        start += slots.columns


def params(mib):
    return pltpu.CompilerParams(vmem_limit_bytes=mib * 1024 * 1024)


def cost(flops, moved):
    return pl.CostEstimate(flops=flops, bytes_accessed=moved, transcendentals=0)


def per_device(eigvecs, link_seed, ownership):
    modes, _, _, layers, plane = eigvecs.shape
    assert layers == 1
    devices = lax.axis_size("sx")
    here = ownership.shape[0] // devices
    part_modes = modes // CHUNKS
    depth = 3 * plane
    tiles = plane // LANES
    slots_x = Slots(modes, here, 1)
    slots_yz = Slots(modes, here, 2)
    vmem = pl.BlockSpec(memory_space=pltpu.VMEM)
    anywhere = pl.BlockSpec(memory_space=pl.ANY)
    smem = pl.BlockSpec(memory_space=pltpu.SMEM)

    route = [(i, (i - 1) % devices) for i in range(devices)]
    raw = eigvecs.transpose(0, 2, 3, 1, 4).reshape(3 * modes, 2, plane)
    parts = pl.pallas_call(
        split_kernel,
        name="split_modes",
        out_shape=[jax.ShapeDtypeStruct((3 * part_modes, 2, plane), BF16)] * CHUNKS,
        in_specs=[anywhere],
        out_specs=[anywhere] * CHUNKS,
        scratch_shapes=[pltpu.SemaphoreType.DMA((CHUNKS,))],
        cost_estimate=cost(0, 6 * 2**20),
    )(raw)
    upper = [lax.ppermute(part, "sx", route) for part in parts]
    planar = eigvecs.reshape(modes, 2, 3, plane).transpose(2, 1, 0, 3)

    where = lax.axis_index("sx").reshape(1).astype(jnp.int32)
    flops = 4 * modes * modes * depth * 2

    links = pl.pallas_call(
        links_kernel,
        name="links",
        out_shape=jax.ShapeDtypeStruct((3, 18, tiles, LANES), F32),
        in_specs=[smem, smem],
        out_specs=vmem,
        compiler_params=params(8),
        cost_estimate=cost(2**20, 2**18),
    )(link_seed, where)
    left = pl.pallas_call(
        left_kernel,
        name="left_side",
        out_shape=jax.ShapeDtypeStruct((2 * modes, depth), BF16),
        in_specs=[vmem],
        out_specs=vmem,
        compiler_params=params(16),
        cost_estimate=cost(0, 6 * 2**20),
    )(planar)

    table_scratch = [
        pltpu.VMEM((slots_x.columns, slots_x.depth), F32),
        pltpu.VMEM((TM // 2, modes, LANES), F32),
    ]
    def hopped(vectors, d, shift):
        rows = 2 * vectors.shape[2]
        return pl.pallas_call(
            functools.partial(hop_kernel, d, shift),
            name="hop_" + "xyz"[d],
            out_shape=jax.ShapeDtypeStruct((rows, depth), BF16),
            in_specs=[vmem, vmem],
            out_specs=vmem,
            compiler_params=params(16),
            cost_estimate=cost(rows * depth * 12, 2 * rows * depth * 2),
        )(vectors, links)

    tables = [
        pl.pallas_call(
            functools.partial(table_kernel, slots_x),
            name="table_" + shift,
            out_shape=jax.ShapeDtypeStruct((slots_x.columns, slots_x.depth), BF16),
            in_specs=[vmem],
            out_specs=vmem,
            scratch_shapes=table_scratch,
            compiler_params=params(16),
            cost_estimate=cost(2**28, 2**20),
        )(products(hopped(planar, d, shift), left))
        for d, shift in ((1, "y"), (2, "z"))
    ]
    sent_yz = pl.pallas_call(
        functools.partial(send_kernel, slots_yz, 2),
        name="send_inner",
        out_shape=jax.ShapeDtypeStruct((devices, slots_yz.rows, LANES), BF16),
        in_specs=[vmem] * 3,
        out_specs=vmem,
        compiler_params=params(24),
        cost_estimate=cost(flops, 2**20),
    )(slots_yz.arrange(ownership, devices), *tables)
    received_yz = lax.all_to_all(sent_yz, "sx", 0, 0)

    blocks = []
    for q in range(CHUNKS):
        vectors = upper[q].reshape(part_modes, 3, 2, plane).transpose(1, 2, 0, 3)
        blocks.append(products(hopped(vectors, 0, None), left))
    sent_x = pl.pallas_call(
        functools.partial(last_kernel, slots_x),
        name="send_outer",
        out_shape=jax.ShapeDtypeStruct((devices, slots_x.rows, LANES), BF16),
        in_specs=[vmem] * (1 + CHUNKS),
        out_specs=vmem,
        scratch_shapes=table_scratch,
        compiler_params=params(24),
        cost_estimate=cost(flops, 8 * 2**20),
    )(slots_x.arrange(ownership, devices), *blocks)
    received_x = lax.all_to_all(sent_x, "sx", 0, 0)

    extent_x = layers * devices
    normalise = 1.0 / math.sqrt(12.0 * extent_x * plane)
    return pl.pallas_call(
        functools.partial(finish_kernel, normalise, slots_x, slots_yz),
        name="sum_of_devices",
        out_shape=jax.ShapeDtypeStruct((here, slots_x.columns + slots_yz.columns), F32),
        in_specs=[vmem, vmem],
        out_specs=vmem,
        compiler_params=params(32),
    )(received_x, received_yz)


def solution(mesh):
    return jax.shard_map(
        per_device,
        mesh=mesh,
        in_specs=(P("cfg", None, None, "sx", None), P("cfg"), P()),
        out_specs=P(("cfg", "sx"), None),
        check_vma=False,
    )
```

```python
import functools
import math

import jax
import jax.numpy as jnp
from jax import lax
from jax.experimental import pallas as pl
from jax.experimental.pallas import tpu as pltpu
from jax.sharding import PartitionSpec as P

TM = 4
NZ = 64
LANES = 128
MODULUS = 46337
CHUNKS = 4
STEP = 32
AT_ONCE = 8
F32 = jnp.float32
BF16 = jnp.bfloat16
NT = (((1,), (1,)), ((), ()))


def dot(left, right, dims=(((1,), (0,)), ((), ()))):
    return lax.dot_general(left, right, dims, preferred_element_type=F32)


def iota(shape, axis):
    return lax.broadcasted_iota(jnp.int32, shape, axis)


def round_up(value, step):
    return -(-value // step) * step


def divide(value):
    quotient = (value.astype(F32) * (1.0 / MODULUS)).astype(jnp.int32)
    rest = value - quotient * MODULUS
    below, above = rest < 0, rest >= MODULUS
    rest = jnp.where(below, rest + MODULUS, jnp.where(above, rest - MODULUS, rest))
    quotient = jnp.where(below, quotient - 1, jnp.where(above, quotient + 1, quotient))
    return quotient, rest


def link_angles(seed, site):
    high, low = divide(site)
    mixed = divide(seed * seed + low)[1]
    mixed = divide(mixed * mixed + high * 977 + 31)[1]
    angles = []
    for index in range(7):
        g = divide(mixed + (5171 * index + 1))[1]
        g = divide(g * g + low)[1]
        g = divide(g * g + 12345)[1]
        angles.append(g.astype(F32) * (2.0 * math.pi / MODULUS) - math.pi)
    return angles


def store_links(u_ref, seed, site):
    a = link_angles(seed, site)
    ca, sa = jnp.cos(a[0]), jnp.sin(a[0])
    cb, sb = jnp.cos(a[1]), jnp.sin(a[1])
    cg, sg = jnp.cos(a[2]), jnp.sin(a[2])
    rotation = [
        [ca * cb * cg - sa * sg, -ca * cb * sg - sa * cg, ca * sb],
        [sa * cb * cg + ca * sg, -sa * cb * sg + ca * cg, sa * sb],
        [-sb * cg, sb * sg, cb],
    ]
    left = [a[3], a[4], -a[3] - a[4]]
    right = [a[5], a[6], -a[5] - a[6]]
    for c in range(3):
        for s in range(3):
            phase = left[c] + right[s]
            u_ref[2 * (3 * c + s)] = rotation[c][s] * jnp.cos(phase)
            u_ref[2 * (3 * c + s) + 1] = rotation[c][s] * jnp.sin(phase)


def hop(load, out_ref, u_ref, first, modes, all_modes, plane):
    wide = (STEP // 8, 8, LANES)
    for t in range(plane // LANES):
        u = [jnp.broadcast_to(u_ref[k, t : t + 1, :], (8, LANES)) for k in range(18)]

        def body(block, carry, t=t, u=u):
            rows = pl.ds(pl.multiple_of(block * STEP, STEP), STEP)
            v = [
                load(part, source, rows, t).astype(F32).reshape(wide)
                for source in range(3)
                for part in range(2)
            ]
            for c in range(3):
                real = imag = None
                for s in range(3):
                    ur, ui = u[2 * (3 * c + s)], u[2 * (3 * c + s) + 1]
                    re, im = v[2 * s], v[2 * s + 1]
                    real = ur * re if real is None else real + ur * re
                    real = real - ui * im
                    imag = ur * im if imag is None else imag + ur * im
                    imag = imag + ui * re
                lanes = slice(c * plane + t * LANES, c * plane + (t + 1) * LANES)
                for part, value in ((0, real), (1, imag)):
                    low = part * all_modes + first + block * STEP
                    out_ref[pl.ds(pl.multiple_of(low, STEP), STEP), lanes] = value.reshape(
                        STEP, LANES
                    ).astype(BF16)
            return carry

        lax.fori_loop(0, modes // STEP, body, 0)


def hop_planar(vector_ref, out_ref, u_ref, first, all_modes):
    _, _, modes, plane = vector_ref.shape

    def load(part, colour, rows, t):
        return vector_ref[colour, part, rows, t * LANES : (t + 1) * LANES]

    hop(load, out_ref, u_ref, first, modes, all_modes, plane)


class Slots:
    def __init__(self, all_modes, slots):
        self.tiles = all_modes // TM
        assert 2 * self.tiles == LANES
        self.half = self.tiles // 2
        self.depth = round_up((self.half + 1) * self.tiles, 2 * LANES)
        self.columns = 2 * TM * TM
        self.groups = LANES // self.columns
        self.per_group = -(-slots // self.groups)
        self.rows = round_up(self.per_group, 8)
        self.all_rows = self.groups * self.rows

    def arrange(self, ownership, devices):
        slots = ownership.shape[0] // devices
        spread = jnp.pad(
            ownership.reshape(devices, slots),
            ((0, 0), (0, self.groups * self.per_group - slots)),
            constant_values=-1,
        ).reshape(devices, self.groups, self.per_group)
        spread = jnp.pad(
            spread, ((0, 0), (0, 0), (0, self.rows - self.per_group)), constant_values=-1
        )
        return spread.reshape(devices, self.all_rows, 1)

    def codes(self):
        lane = iota((1, self.depth), 1)
        first, second = lane // self.tiles, lane % self.tiles
        last = self.tiles - 1
        diagonal = first == self.half
        turned = jnp.logical_or(diagonal, second < first)
        i = jnp.where(diagonal, last - second, jnp.where(turned, last - first, first))
        j = jnp.where(turned, last - second, second)
        pair = i * self.tiles - (i * (i - 1)) // 2 + (j - i)
        known = jnp.logical_and(
            first <= self.half, jnp.logical_not(jnp.logical_and(diagonal, second >= self.half))
        )
        return jnp.where(known, pair, -2)


def store_table(table_ref, fold_ref, real, imag, slots):
    all_modes = real.shape[0]
    n, half = slots.tiles, slots.half
    parts = [real - real.T, imag + imag.T]

    def choose(count, width, turned):
        row, column = iota((count, all_modes), 0), iota((count, all_modes), 1)
        r, i = row // width, row % width
        if turned:
            i = n - 1 - i
        return (column == i * TM + r).astype(F32).astype(BF16)

    pick = [choose(TM * half, half, turned) for turned in (False, True)]
    spread = [choose(all_modes, n, turned) for turned in (False, True)]
    row_i = iota((TM * half, all_modes), 0) % half
    lane_j = iota((TM * half, all_modes), 1) % n
    corners = []
    for part in range(2):
        entries = parts[part].astype(BF16)
        straight, turned = [
            dot(dot(pick[k], entries).astype(BF16), spread[k], NT) for k in range(2)
        ]
        folded = jnp.where(lane_j >= row_i, straight, turned)
        for k in range(TM // 2):
            fold_ref[k, part * TM * half : (part + 1) * TM * half, :] = folded[
                :, k * LANES : (k + 1) * LANES
            ]
        diagonal = jnp.where(lane_j == row_i, turned, 0.0)
        for r in range(TM):
            corners.append(
                jnp.sum(diagonal[r * half : (r + 1) * half], axis=0, keepdims=True)
            )
    low = iota((2 * TM, LANES), 1) < n

    def split(even, odd, lanes):
        for pair in range(TM // 2):
            e, o = even[pair], odd[pair]
            top = 2 * pair * 2 * TM
            table_ref[top : top + 2 * TM, lanes] = jnp.where(low, e, pltpu.roll(o, n, 1))
            table_ref[top + 2 * TM : top + 4 * TM, lanes] = jnp.where(
                low, pltpu.roll(e, n, 1), o
            )

    halves = [slice(k * LANES, (k + 1) * LANES) for k in range(TM // 2)]
    for two in range(half // 2):
        even = [fold_ref[k, pl.ds(2 * two, 2 * TM, stride=half), :] for k in range(TM // 2)]
        odd = [fold_ref[k, pl.ds(2 * two + 1, 2 * TM, stride=half), :] for k in range(TM // 2)]
        split(even, odd, slice(two * LANES, (two + 1) * LANES))
    corner = jnp.concatenate(corners, 0)
    nothing = jnp.zeros((2 * TM, LANES), F32)
    start = half * n
    split([corner[:, h] for h in halves], [nothing] * len(halves), slice(start, start + LANES))
    rest = slots.depth - start - LANES
    if rest:
        table_ref[:, start + LANES :] = jnp.zeros(
            (2 * TM * TM, rest), F32
        )


def send_tiles(out_ref, owner_ref, tables, chosen_ref, slots):
    row, column = iota((LANES, slots.columns), 0), iota((LANES, slots.columns), 1)
    entry = row % slots.columns
    order = column == (entry % TM) * (2 * TM) + entry // TM
    order = order.astype(F32).astype(BF16)
    table = jnp.concatenate([dot(order, t).astype(BF16) for t in tables], 0)
    tiles = slots.depth // LANES
    codes = slots.codes()
    codes = [
        jnp.broadcast_to(codes[:, t * LANES : (t + 1) * LANES], (16, LANES)).astype(jnp.int16)
        for t in range(tiles)
    ]
    one, zero = jnp.ones((16, LANES), BF16), jnp.zeros((16, LANES), BF16)
    lane_group = iota((slots.rows, LANES), 1) // slots.columns
    rows = slots.all_rows

    def body(step, carry):
        for k in range(AT_ONCE):
            owners = jnp.broadcast_to(owner_ref[step * AT_ONCE + k], (rows, LANES))
            owners = owners.astype(jnp.int16)
            for top in range(0, rows, 16):
                mine = owners[top : top + 16]
                for t in range(tiles):
                    chosen_ref[
                        k * rows + top : k * rows + top + 16, t * LANES : (t + 1) * LANES
                    ] = jnp.where(mine == codes[t], one, zero)
        picked = dot(chosen_ref[...], table, NT)
        for k in range(AT_ONCE):
            for d in range(len(tables)):
                pieces = [
                    picked[
                        k * rows + g * slots.rows : k * rows + (g + 1) * slots.rows,
                        d * LANES : (d + 1) * LANES,
                    ]
                    for g in range(slots.groups)
                ]
                packed = pieces[0]
                for g in range(1, slots.groups):
                    packed = jnp.where(lane_group == g, pieces[g], packed)
                out_ref[step * AT_ONCE + k, d] = packed.astype(BF16)
        return carry

    lax.fori_loop(0, out_ref.shape[0] // AT_ONCE, body, 0)


def links_kernel(seed_ref, where_ref, out_ref):
    _, _, tiles, _ = out_ref.shape
    plane = tiles * LANES
    place = iota((tiles, LANES), 0) * LANES + iota((tiles, LANES), 1)
    before_y = jnp.where(place < NZ, place + (plane - NZ), place - NZ)
    before_z = jnp.where(place % NZ == 0, place + (NZ - 1), place - 1)
    for d, source in enumerate((place, before_y, before_z)):
        store_links(out_ref.at[d], seed_ref[d], source + where_ref[0] * plane)


def load_kernel(whole_ref, *refs):
    parts, sems = refs[:CHUNKS], refs[CHUNKS]
    count = parts[0].shape[0]
    copies = [
        pltpu.make_async_copy(whole_ref.at[pl.ds(q * count, count)], parts[q], sems.at[q])
        for q in range(CHUNKS)
    ]
    for copy in copies:
        copy.start()
    for copy in copies:
        copy.wait()


def left_kernel(*refs):
    parts = refs[:CHUNKS]
    left_ref, left_y_ref, left_z_ref = refs[CHUNKS:]
    _, _, part_modes, plane = parts[0].shape
    all_modes = part_modes * CHUNKS
    for q in range(CHUNKS):
        for c in range(3):
            for part in range(2):
                start = part * all_modes + q * part_modes
                left_ref[start : start + part_modes, c * plane : (c + 1) * plane] = parts[q][
                    c, part
                ]
    wide = 2 * LANES
    source, target = iota((wide, wide), 0), iota((wide, wide), 1)
    halves = (source == (target // LANES) * LANES + (target + NZ) % LANES).astype(F32)
    halves = halves.astype(BF16)
    before = jnp.where(target % NZ == 0, target + (NZ - 1), target - 1)
    behind = (source == before).astype(F32).astype(BF16)
    low = iota((2 * all_modes, LANES), 1) < NZ
    for c in range(3):
        swapped = []
        for start in range(c * plane, (c + 1) * plane, wide):
            piece = left_ref[:, start : start + wide]
            left_z_ref[:, start : start + wide] = dot(piece, behind).astype(BF16)
            both = dot(piece, halves)
            swapped += [both[:, :LANES], both[:, LANES:]]
        for t in range(plane // LANES):
            lanes = slice(c * plane + t * LANES, c * plane + (t + 1) * LANES)
            left_y_ref[:, lanes] = jnp.where(low, swapped[t - 1], swapped[t]).astype(BF16)


def inner_kernel(slots, d, links_ref, left_ref, *refs):
    parts = refs[:CHUNKS]
    out_ref, hop_ref, table_ref, fold_ref = refs[CHUNKS:]
    part_modes = parts[0].shape[2]
    n = part_modes * CHUNKS
    for q in range(CHUNKS):
        hop_planar(parts[q], hop_ref, links_ref.at[d], q * part_modes, n)
    blocks = dot(left_ref[...], hop_ref[...], NT)
    real = blocks[:n, :n] + blocks[n:, n:]
    imag = blocks[:n, n:] - blocks[n:, :n]
    store_table(table_ref, fold_ref, real, imag, slots)
    out_ref[...] = table_ref[...].astype(BF16)


def send_kernel(slots, directions, owner_ref, *refs):
    tables, (out_ref, chosen_ref) = refs[:directions], refs[directions:]
    send_tiles(out_ref, owner_ref, [t[...] for t in tables], chosen_ref, slots)


def outer_chunk(vector_ref, links_ref, left_ref, hop_ref):
    modes = vector_ref.shape[2]
    n = left_ref.shape[0] // 2
    hop_planar(vector_ref, hop_ref, links_ref.at[0], 0, modes)
    blocks = dot(left_ref[...], hop_ref[...], NT)
    straight, crossed = blocks[:n], pltpu.roll(blocks[n:], modes, 1)
    low = iota(straight.shape, 1) < modes
    return jnp.where(low, straight + crossed, straight - crossed)


def outer_kernel(vector_ref, links_ref, left_ref, out_ref, hop_ref):
    out_ref[...] = outer_chunk(vector_ref, links_ref, left_ref, hop_ref)


def last_kernel(slots, owner_ref, vector_ref, links_ref, left_ref, *refs):
    before = [r[...] for r in refs[: CHUNKS - 1]]
    out_ref, hop_ref, table_ref, fold_ref, chosen_ref = refs[CHUNKS - 1 :]
    chunks = before + [outer_chunk(vector_ref, links_ref, left_ref, hop_ref)]
    modes = vector_ref.shape[2]
    low = iota(chunks[0].shape, 1) < modes
    real, imag = [], []
    for even, odd in zip(chunks[::2], chunks[1::2]):
        real.append(jnp.where(low, even, pltpu.roll(odd, modes, 1)))
        imag.append(jnp.where(low, pltpu.roll(even, modes, 1), odd))
    store_table(
        table_ref, fold_ref, jnp.concatenate(real, 1), jnp.concatenate(imag, 1), slots
    )
    send_tiles(out_ref, owner_ref, [table_ref[...].astype(BF16)], chosen_ref, slots)


def total_kernel(in_ref, out_ref):
    total = in_ref[0].astype(F32)
    for device in range(1, in_ref.shape[0]):
        total = total + in_ref[device].astype(F32)
    out_ref[...] = total


def finish_kernel(normalise, slots, x_ref, inner_ref, out_ref):
    here = out_ref.shape[0]
    total = x_ref[0, 0].astype(F32)
    for device in range(1, x_ref.shape[0]):
        total = total + x_ref[device, 0].astype(F32)
    for d, value in enumerate((total, inner_ref[0], inner_ref[1])):
        value = value * normalise
        for group in range(slots.groups):
            first = group * slots.per_group
            count = min(slots.per_group, here - first)
            out_ref[first : first + count, d * slots.columns : (d + 1) * slots.columns] = value[
                :count, group * slots.columns : (group + 1) * slots.columns
            ]


def params(mib):
    return pltpu.CompilerParams(vmem_limit_bytes=mib * 1024 * 1024)


def cost(flops, moved):
    return pl.CostEstimate(flops=flops, bytes_accessed=moved, transcendentals=0)


def per_device(eigvecs, link_seed, ownership):
    modes, _, _, layers, plane = eigvecs.shape
    assert layers == 1
    devices = lax.axis_size("sx")
    here = ownership.shape[0] // devices
    part_modes = modes // CHUNKS
    assert 2 * part_modes == LANES
    depth = 3 * plane
    tiles = plane // LANES
    slots = Slots(modes, here)
    vmem = pl.BlockSpec(memory_space=pltpu.VMEM)
    smem = pl.BlockSpec(memory_space=pltpu.SMEM)
    anywhere = pl.BlockSpec(memory_space=pl.ANY)

    raw = eigvecs.transpose(0, 2, 3, 1, 4).reshape(3 * modes, 2, plane)
    raw_parts = pl.pallas_call(
        load_kernel,
        name="load_modes",
        out_shape=[jax.ShapeDtypeStruct((3 * part_modes, 2, plane), BF16)] * CHUNKS,
        in_specs=[anywhere],
        out_specs=[vmem] * CHUNKS,
        scratch_shapes=[pltpu.SemaphoreType.DMA((CHUNKS,))],
        compiler_params=params(16),
        cost_estimate=cost(0, 6 * 2**20),
    )(raw)
    route = [(i, (i - 1) % devices) for i in range(devices)]
    parts = [p.reshape(part_modes, 3, 2, plane).transpose(1, 2, 0, 3) for p in raw_parts]
    upper = [lax.ppermute(part, "sx", route) for part in parts]

    where = lax.axis_index("sx").reshape(1).astype(jnp.int32)
    owners = slots.arrange(ownership, devices)
    flops = 4 * modes * modes * depth * 2

    links = pl.pallas_call(
        links_kernel,
        name="links",
        out_shape=jax.ShapeDtypeStruct((3, 18, tiles, LANES), F32),
        in_specs=[smem, smem],
        out_specs=vmem,
        compiler_params=params(8),
        cost_estimate=cost(2**20, 2**18),
    )(link_seed, where)
    left, left_y, left_z = pl.pallas_call(
        left_kernel,
        name="left_sides",
        out_shape=[jax.ShapeDtypeStruct((2 * modes, depth), BF16)] * 3,
        in_specs=[vmem] * CHUNKS,
        out_specs=[vmem] * 3,
        compiler_params=params(16),
        cost_estimate=cost(flops, 12 * 2**20),
    )(*parts)

    table_scratch = [
        pltpu.VMEM((slots.columns, slots.depth), F32),
        pltpu.VMEM((TM // 2, modes, LANES), F32),
    ]
    chosen_scratch = [pltpu.VMEM((AT_ONCE * slots.all_rows, slots.depth), BF16)]
    tables = [
        pl.pallas_call(
            functools.partial(inner_kernel, slots, d),
            name="direction_" + "xyz"[d],
            out_shape=jax.ShapeDtypeStruct((slots.columns, slots.depth), BF16),
            in_specs=[vmem] * (2 + CHUNKS),
            out_specs=vmem,
            scratch_shapes=[pltpu.VMEM((2 * modes, depth), BF16)] + table_scratch,
            compiler_params=params(16),
            cost_estimate=cost(2 * flops, 4 * 2**20),
        )(links, side, *parts)
        for d, side in ((1, left_y), (2, left_z))
    ]
    sent_inner = pl.pallas_call(
        functools.partial(send_kernel, slots, 2),
        name="send_inner",
        out_shape=jax.ShapeDtypeStruct((devices, 2, slots.rows, LANES), BF16),
        in_specs=[vmem] * 3,
        out_specs=vmem,
        scratch_shapes=chosen_scratch,
        compiler_params=params(24),
        cost_estimate=cost(flops, 2**20),
    )(owners, *tables)
    received_inner = lax.all_to_all(sent_inner, "sx", 0, 0)
    total_inner = pl.pallas_call(
        total_kernel,
        name="sum_inner",
        out_shape=jax.ShapeDtypeStruct((2, slots.rows, LANES), F32),
        in_specs=[vmem],
        out_specs=vmem,
        compiler_params=params(8),
        cost_estimate=cost(2**20, 2**20),
    )(received_inner)

    hop_scratch = [pltpu.VMEM((2 * part_modes, depth), BF16)]
    before = [
        pl.pallas_call(
            outer_kernel,
            name="direction_x",
            out_shape=jax.ShapeDtypeStruct((modes, LANES), F32),
            in_specs=[vmem] * 3,
            out_specs=vmem,
            scratch_shapes=hop_scratch,
            compiler_params=params(8),
            cost_estimate=cost(flops // CHUNKS, 4 * 2**20),
        )(upper[q], links, left)
        for q in range(CHUNKS - 1)
    ]
    sent_x = pl.pallas_call(
        functools.partial(last_kernel, slots),
        name="send_outer",
        out_shape=jax.ShapeDtypeStruct((devices, 1, slots.rows, LANES), BF16),
        in_specs=[vmem] * (3 + CHUNKS),
        out_specs=vmem,
        scratch_shapes=hop_scratch + table_scratch + chosen_scratch,
        compiler_params=params(24),
        cost_estimate=cost(flops, 8 * 2**20),
    )(owners, upper[-1], links, left, *before)
    received_x = lax.all_to_all(sent_x, "sx", 0, 0)

    extent_x = layers * devices
    normalise = 1.0 / math.sqrt(12.0 * extent_x * plane)
    return pl.pallas_call(
        functools.partial(finish_kernel, normalise, slots),
        name="sum_outer",
        out_shape=jax.ShapeDtypeStruct((here, 3 * slots.columns), F32),
        in_specs=[vmem, vmem],
        out_specs=vmem,
        compiler_params=params(8),
    )(received_x, total_inner)


def solution(mesh):
    return jax.shard_map(
        per_device,
        mesh=mesh,
        in_specs=(P("cfg", None, None, "sx", None), P("cfg"), P()),
        out_specs=P(("cfg", "sx"), None),
        check_vma=False,
    )
```

```python
import functools
import math

import jax
import jax.numpy as jnp
from jax import lax
from jax.experimental import pallas as pl
from jax.experimental.pallas import tpu as pltpu
from jax.sharding import PartitionSpec as P

TM = 4
NZ = 64
LANES = 128
MODULUS = 46337
CHUNKS = 4
STEP = 32
AT_ONCE = 8
F32 = jnp.float32
BF16 = jnp.bfloat16
NT = (((1,), (1,)), ((), ()))


def dot(left, right, dims=(((1,), (0,)), ((), ()))):
    return lax.dot_general(left, right, dims, preferred_element_type=F32)


def iota(shape, axis):
    return lax.broadcasted_iota(jnp.int32, shape, axis)


def round_up(value, step):
    return -(-value // step) * step


def divide(value):
    quotient = (value.astype(F32) * (1.0 / MODULUS)).astype(jnp.int32)
    rest = value - quotient * MODULUS
    below, above = rest < 0, rest >= MODULUS
    rest = jnp.where(below, rest + MODULUS, jnp.where(above, rest - MODULUS, rest))
    quotient = jnp.where(below, quotient - 1, jnp.where(above, quotient + 1, quotient))
    return quotient, rest


def link_angles(seed, site):
    high, low = divide(site)
    mixed = divide(seed * seed + low)[1]
    mixed = divide(mixed * mixed + high * 977 + 31)[1]
    angles = []
    for index in range(7):
        g = divide(mixed + (5171 * index + 1))[1]
        g = divide(g * g + low)[1]
        g = divide(g * g + 12345)[1]
        angles.append(g.astype(F32) * (2.0 * math.pi / MODULUS) - math.pi)
    return angles


def store_links(u_ref, seed, site):
    a = link_angles(seed, site)
    ca, sa = jnp.cos(a[0]), jnp.sin(a[0])
    cb, sb = jnp.cos(a[1]), jnp.sin(a[1])
    cg, sg = jnp.cos(a[2]), jnp.sin(a[2])
    rotation = [
        [ca * cb * cg - sa * sg, -ca * cb * sg - sa * cg, ca * sb],
        [sa * cb * cg + ca * sg, -sa * cb * sg + ca * cg, sa * sb],
        [-sb * cg, sb * sg, cb],
    ]
    left = [a[3], a[4], -a[3] - a[4]]
    right = [a[5], a[6], -a[5] - a[6]]
    for c in range(3):
        for s in range(3):
            phase = left[c] + right[s]
            u_ref[2 * (3 * c + s)] = rotation[c][s] * jnp.cos(phase)
            u_ref[2 * (3 * c + s) + 1] = rotation[c][s] * jnp.sin(phase)


def hop(vector_ref, out_ref, u_ref, first, count):
    all_modes, plane = vector_ref.shape[0] // 2, vector_ref.shape[1] // 3
    wide = (STEP // 8, 8, LANES)
    for t in range(plane // LANES):
        u = [jnp.broadcast_to(u_ref[k, t : t + 1, :], (8, LANES)) for k in range(18)]

        def body(block, carry, t=t, u=u):
            rows = [
                pl.ds(pl.multiple_of(part * all_modes + first + block * STEP, STEP), STEP)
                for part in range(2)
            ]
            lanes = [slice(c * plane + t * LANES, c * plane + (t + 1) * LANES) for c in range(3)]
            v = [
                [vector_ref[rows[part], lanes[c]].astype(F32).reshape(wide) for part in range(2)]
                for c in range(3)
            ]
            for c in range(3):
                real = imag = None
                for s in range(3):
                    ur, ui = u[2 * (3 * c + s)], u[2 * (3 * c + s) + 1]
                    re, im = v[s]
                    real = ur * re if real is None else real + ur * re
                    real = real - ui * im
                    imag = ur * im if imag is None else imag + ur * im
                    imag = imag + ui * re
                for part, value in ((0, real), (1, imag)):
                    out_ref[rows[part], lanes[c]] = value.reshape(STEP, LANES).astype(BF16)
            return carry

        lax.fori_loop(0, count // STEP, body, 0)


def products(left_ref, hop_ref):
    n = left_ref.shape[0] // 2
    with_real = dot(left_ref[...], hop_ref[:n, :], NT)
    with_imag = dot(left_ref[...], hop_ref[n:, :], NT)
    return with_real[:n] + with_imag[n:], with_imag[:n] - with_real[n:]


class Slots:
    def __init__(self, all_modes, slots):
        self.tiles = all_modes // TM
        assert 2 * self.tiles == LANES
        self.half = self.tiles // 2
        self.depth = round_up((self.half + 1) * self.tiles, 2 * LANES)
        self.columns = 2 * TM * TM
        self.groups = LANES // self.columns
        self.per_group = -(-slots // self.groups)
        self.rows = round_up(self.per_group, 8)
        self.all_rows = self.groups * self.rows

    def arrange(self, ownership, devices):
        slots = ownership.shape[0] // devices
        spread = jnp.pad(
            ownership.reshape(devices, slots),
            ((0, 0), (0, self.groups * self.per_group - slots)),
            constant_values=-1,
        ).reshape(devices, self.groups, self.per_group)
        spread = jnp.pad(
            spread, ((0, 0), (0, 0), (0, self.rows - self.per_group)), constant_values=-1
        )
        return spread.reshape(devices, self.all_rows, 1)

    def codes(self):
        lane = iota((1, self.depth), 1)
        first, second = lane // self.tiles, lane % self.tiles
        last = self.tiles - 1
        diagonal = first == self.half
        turned = jnp.logical_or(diagonal, second < first)
        i = jnp.where(diagonal, last - second, jnp.where(turned, last - first, first))
        j = jnp.where(turned, last - second, second)
        pair = i * self.tiles - (i * (i - 1)) // 2 + (j - i)
        known = jnp.logical_and(
            first <= self.half, jnp.logical_not(jnp.logical_and(diagonal, second >= self.half))
        )
        return jnp.where(known, pair, -2)


def store_table(table_ref, fold_ref, real, imag, slots):
    all_modes = real.shape[0]
    n, half = slots.tiles, slots.half
    parts = [real - real.T, imag + imag.T]

    def choose(count, width, turned):
        row, column = iota((count, all_modes), 0), iota((count, all_modes), 1)
        r, i = row // width, row % width
        if turned:
            i = n - 1 - i
        return (column == i * TM + r).astype(F32).astype(BF16)

    pick = [choose(TM * half, half, turned) for turned in (False, True)]
    spread = [choose(all_modes, n, turned) for turned in (False, True)]
    row_i = iota((TM * half, all_modes), 0) % half
    lane_j = iota((TM * half, all_modes), 1) % n
    corners = []
    for part in range(2):
        entries = parts[part].astype(BF16)
        straight, turned = [
            dot(dot(pick[k], entries).astype(BF16), spread[k], NT) for k in range(2)
        ]
        folded = jnp.where(lane_j >= row_i, straight, turned)
        for k in range(TM // 2):
            fold_ref[k, part * TM * half : (part + 1) * TM * half, :] = folded[
                :, k * LANES : (k + 1) * LANES
            ]
        diagonal = jnp.where(lane_j == row_i, turned, 0.0)
        for r in range(TM):
            corners.append(
                jnp.sum(diagonal[r * half : (r + 1) * half], axis=0, keepdims=True)
            )
    low = iota((2 * TM, LANES), 1) < n

    def split(even, odd, lanes):
        for pair in range(TM // 2):
            e, o = even[pair], odd[pair]
            top = 2 * pair * 2 * TM
            table_ref[top : top + 2 * TM, lanes] = jnp.where(low, e, pltpu.roll(o, n, 1))
            table_ref[top + 2 * TM : top + 4 * TM, lanes] = jnp.where(
                low, pltpu.roll(e, n, 1), o
            )

    halves = [slice(k * LANES, (k + 1) * LANES) for k in range(TM // 2)]
    for two in range(half // 2):
        even = [fold_ref[k, pl.ds(2 * two, 2 * TM, stride=half), :] for k in range(TM // 2)]
        odd = [fold_ref[k, pl.ds(2 * two + 1, 2 * TM, stride=half), :] for k in range(TM // 2)]
        split(even, odd, slice(two * LANES, (two + 1) * LANES))
    corner = jnp.concatenate(corners, 0)
    nothing = jnp.zeros((2 * TM, LANES), F32)
    start = half * n
    split([corner[:, h] for h in halves], [nothing] * len(halves), slice(start, start + LANES))
    rest = slots.depth - start - LANES
    if rest:
        table_ref[:, start + LANES :] = jnp.zeros(
            (2 * TM * TM, rest), F32
        )


def send_tiles(out_ref, owner_ref, tables, chosen_ref, slots):
    row, column = iota((LANES, slots.columns), 0), iota((LANES, slots.columns), 1)
    entry = row % slots.columns
    order = column == (entry % TM) * (2 * TM) + entry // TM
    order = order.astype(F32).astype(BF16)
    table = jnp.concatenate([dot(order, t).astype(BF16) for t in tables], 0)
    tiles = slots.depth // LANES
    codes = slots.codes()
    codes = [
        jnp.broadcast_to(codes[:, t * LANES : (t + 1) * LANES], (16, LANES)).astype(jnp.int16)
        for t in range(tiles)
    ]
    one, zero = jnp.ones((16, LANES), BF16), jnp.zeros((16, LANES), BF16)
    lane_group = iota((slots.rows, LANES), 1) // slots.columns
    rows = slots.all_rows

    def body(step, carry):
        for k in range(AT_ONCE):
            owners = jnp.broadcast_to(owner_ref[step * AT_ONCE + k], (rows, LANES))
            owners = owners.astype(jnp.int16)
            for top in range(0, rows, 16):
                mine = owners[top : top + 16]
                for t in range(tiles):
                    chosen_ref[
                        k * rows + top : k * rows + top + 16, t * LANES : (t + 1) * LANES
                    ] = jnp.where(mine == codes[t], one, zero)
        picked = dot(chosen_ref[...], table, NT)
        for k in range(AT_ONCE):
            for d in range(len(tables)):
                pieces = [
                    picked[
                        k * rows + g * slots.rows : k * rows + (g + 1) * slots.rows,
                        d * LANES : (d + 1) * LANES,
                    ]
                    for g in range(slots.groups)
                ]
                packed = pieces[0]
                for g in range(1, slots.groups):
                    packed = jnp.where(lane_group == g, pieces[g], packed)
                out_ref[step * AT_ONCE + k, d] = packed.astype(BF16)
        return carry

    lax.fori_loop(0, out_ref.shape[0] // AT_ONCE, body, 0)


def store_all_links(links_ref, seed_ref, x):
    _, _, tiles, _ = links_ref.shape
    plane = tiles * LANES
    place = iota((tiles, LANES), 0) * LANES + iota((tiles, LANES), 1)
    before_y = jnp.where(place < NZ, place + (plane - NZ), place - NZ)
    before_z = jnp.where(place % NZ == 0, place + (NZ - 1), place - 1)
    for d, source in enumerate((place, before_y, before_z)):
        store_links(links_ref.at[d], seed_ref[d], source + x * plane)


def load_modes(planar_hbm, out_ref, sems, first, count):
    _, _, modes, plane = planar_hbm.shape
    copies = [
        pltpu.make_async_copy(
            planar_hbm.at[c, part, pl.ds(first, count)],
            out_ref.at[
                pl.ds(part * modes + first, count), pl.ds(c * plane, plane)
            ],
            sems.at[2 * c + part],
        )
        for c in range(3)
        for part in range(2)
    ]
    for copy in copies:
        copy.start()
    return copies


def wait_all(copies):
    for copy in copies:
        copy.wait()


def store_left_y(out_ref, left_ref, plane):
    wide = 2 * LANES
    source, target = iota((wide, wide), 0), iota((wide, wide), 1)
    halves = source == (target // LANES) * LANES + (target + NZ) % LANES
    halves = halves.astype(F32).astype(BF16)
    low = iota((left_ref.shape[0], LANES), 1) < NZ
    for c in range(3):
        swapped = []
        for start in range(c * plane, (c + 1) * plane, wide):
            both = dot(left_ref[:, start : start + wide], halves)
            swapped += [both[:, :LANES], both[:, LANES:]]
        for t in range(plane // LANES):
            lanes = slice(c * plane + t * LANES, c * plane + (t + 1) * LANES)
            out_ref[:, lanes] = jnp.where(low, swapped[t - 1], swapped[t]).astype(BF16)


def store_left_z(out_ref, left_ref, plane):
    wide = 2 * LANES
    source, target = iota((wide, wide), 0), iota((wide, wide), 1)
    before = jnp.where(target % NZ == 0, target + (NZ - 1), target - 1)
    behind = (source == before).astype(F32).astype(BF16)
    for start in range(0, 3 * plane, wide):
        piece = dot(left_ref[:, start : start + wide], behind)
        out_ref[:, start : start + wide] = piece.astype(BF16)


def inner_kernel(
    slots,
    seed_ref,
    where_ref,
    owner_ref,
    planar_hbm,
    out_ref,
    links_x_ref,
    vector_ref,
    left_ref,
    hop_ref,
    links_ref,
    table_ref,
    fold_ref,
    chosen_ref,
    sems,
):
    _, _, modes, plane = planar_hbm.shape
    copies = load_modes(planar_hbm, vector_ref, sems, 0, modes)
    store_all_links(links_ref, seed_ref, where_ref[0])
    links_x_ref[...] = links_ref[0]
    wait_all(copies)
    tables = []
    for d, store_left in ((1, store_left_y), (2, store_left_z)):
        store_left(left_ref, vector_ref, plane)
        hop(vector_ref, hop_ref, links_ref.at[d], 0, modes)
        real, imag = products(left_ref, hop_ref)
        store_table(table_ref.at[d - 1], fold_ref, real, imag, slots)
        tables.append(table_ref.at[d - 1])
    send_tiles(out_ref, owner_ref, [t[...].astype(BF16) for t in tables], chosen_ref, slots)


def outer_kernel(
    slots,
    owner_ref,
    links_ref,
    upper_hbm,
    planar_hbm,
    out_ref,
    vector_ref,
    left_ref,
    hop_ref,
    table_ref,
    fold_ref,
    chosen_ref,
    sems,
):
    _, _, modes, plane = planar_hbm.shape
    part = modes // CHUNKS
    arriving = [
        load_modes(upper_hbm, vector_ref, sems.at[q], q * part, part) for q in range(CHUNKS)
    ]
    own = load_modes(planar_hbm, left_ref, sems.at[CHUNKS], 0, modes)
    for q in range(CHUNKS):
        wait_all(arriving[q])
        hop(vector_ref, hop_ref, links_ref, q * part, part)
    wait_all(own)
    real, imag = products(left_ref, hop_ref)
    store_table(table_ref, fold_ref, real, imag, slots)
    send_tiles(out_ref, owner_ref, [table_ref[...].astype(BF16)], chosen_ref, slots)


def total_kernel(in_ref, out_ref):
    total = in_ref[0].astype(F32)
    for device in range(1, in_ref.shape[0]):
        total = total + in_ref[device].astype(F32)
    out_ref[...] = total


def finish_kernel(normalise, slots, x_ref, inner_ref, out_ref):
    here = out_ref.shape[0]
    total = x_ref[0, 0].astype(F32)
    for device in range(1, x_ref.shape[0]):
        total = total + x_ref[device, 0].astype(F32)
    for d, value in enumerate((total, inner_ref[0], inner_ref[1])):
        value = value * normalise
        for group in range(slots.groups):
            first = group * slots.per_group
            count = min(slots.per_group, here - first)
            out_ref[first : first + count, d * slots.columns : (d + 1) * slots.columns] = value[
                :count, group * slots.columns : (group + 1) * slots.columns
            ]


def params(mib):
    return pltpu.CompilerParams(vmem_limit_bytes=mib * 1024 * 1024)


def cost(flops, moved):
    return pl.CostEstimate(flops=flops, bytes_accessed=moved, transcendentals=0)


def per_device(eigvecs, link_seed, ownership):
    modes, _, _, layers, plane = eigvecs.shape
    assert layers == 1
    devices = lax.axis_size("sx")
    here = ownership.shape[0] // devices
    depth = 3 * plane
    tiles = plane // LANES
    slots = Slots(modes, here)
    vmem = pl.BlockSpec(memory_space=pltpu.VMEM)
    smem = pl.BlockSpec(memory_space=pltpu.SMEM)
    anywhere = pl.BlockSpec(memory_space=pl.ANY)

    planar = eigvecs.reshape(modes, 2, 3, plane).transpose(2, 1, 0, 3)
    planar = lax.optimization_barrier(planar)
    route = [(i, (i - 1) % devices) for i in range(devices)]
    upper = lax.ppermute(planar, "sx", route)

    where = lax.axis_index("sx").reshape(1).astype(jnp.int32)
    owners = slots.arrange(ownership, devices)
    flops = 4 * modes * modes * depth * 2
    wide = pltpu.VMEM((2 * modes, depth), BF16)
    table = (slots.columns, slots.depth)
    fold_scratch = pltpu.VMEM((TM // 2, modes, LANES), F32)
    chosen_scratch = pltpu.VMEM((AT_ONCE * slots.all_rows, slots.depth), BF16)

    sent_inner, links_x = pl.pallas_call(
        functools.partial(inner_kernel, slots),
        name="inner_directions",
        out_shape=(
            jax.ShapeDtypeStruct((devices, 2, slots.rows, LANES), BF16),
            jax.ShapeDtypeStruct((18, tiles, LANES), F32),
        ),
        in_specs=[smem, smem, vmem, anywhere],
        out_specs=(vmem, vmem),
        scratch_shapes=[
            wide,
            wide,
            wide,
            pltpu.VMEM((3, 18, tiles, LANES), F32),
            pltpu.VMEM((2,) + table, F32),
            fold_scratch,
            chosen_scratch,
            pltpu.SemaphoreType.DMA((6,)),
        ],
        compiler_params=params(40),
        cost_estimate=cost(6 * flops, 8 * 2**20),
    )(link_seed, where, owners, planar)
    received_inner = lax.all_to_all(sent_inner, "sx", 0, 0)
    total_inner = pl.pallas_call(
        total_kernel,
        name="sum_inner",
        out_shape=jax.ShapeDtypeStruct((2, slots.rows, LANES), F32),
        in_specs=[vmem],
        out_specs=vmem,
        compiler_params=params(8),
        cost_estimate=cost(2**20, 2**20),
    )(received_inner)

    sent_x = pl.pallas_call(
        functools.partial(outer_kernel, slots),
        name="outer_direction",
        out_shape=jax.ShapeDtypeStruct((devices, 1, slots.rows, LANES), BF16),
        in_specs=[vmem, vmem, anywhere, anywhere],
        out_specs=vmem,
        scratch_shapes=[
            wide,
            wide,
            wide,
            pltpu.VMEM(table, F32),
            fold_scratch,
            chosen_scratch,
            pltpu.SemaphoreType.DMA((CHUNKS + 1, 6)),
        ],
        compiler_params=params(40),
        cost_estimate=cost(3 * flops, 8 * 2**20),
    )(owners, links_x, upper, planar)
    received_x = lax.all_to_all(sent_x, "sx", 0, 0)

    extent_x = layers * devices
    normalise = 1.0 / math.sqrt(12.0 * extent_x * plane)
    return pl.pallas_call(
        functools.partial(finish_kernel, normalise, slots),
        name="sum_outer",
        out_shape=jax.ShapeDtypeStruct((here, 3 * slots.columns), F32),
        in_specs=[vmem, vmem],
        out_specs=vmem,
        compiler_params=params(8),
    )(received_x, total_inner)


def solution(mesh):
    return jax.shard_map(
        per_device,
        mesh=mesh,
        in_specs=(P("cfg", None, None, "sx", None), P("cfg"), P()),
        out_specs=P(("cfg", "sx"), None),
        check_vma=False,
    )
```

```python
import functools
import math

import jax
import jax.numpy as jnp
from jax import lax
from jax.experimental import pallas as pl
from jax.experimental.pallas import tpu as pltpu
from jax.sharding import PartitionSpec as P

TM = 4
NZ = 64
LANES = 128
MODULUS = 46337
CHUNKS = 4
STEP = 32
F32 = jnp.float32
BF16 = jnp.bfloat16
NT = (((1,), (1,)), ((), ()))


def dot(left, right, dims=(((1,), (0,)), ((), ()))):
    return lax.dot_general(left, right, dims, preferred_element_type=F32)


def iota(shape, axis):
    return lax.broadcasted_iota(jnp.int32, shape, axis)


def round_up(value, step):
    return -(-value // step) * step


def divide(value):
    quotient = (value.astype(F32) * (1.0 / MODULUS)).astype(jnp.int32)
    rest = value - quotient * MODULUS
    below, above = rest < 0, rest >= MODULUS
    rest = jnp.where(below, rest + MODULUS, jnp.where(above, rest - MODULUS, rest))
    quotient = jnp.where(below, quotient - 1, jnp.where(above, quotient + 1, quotient))
    return quotient, rest


def link_angles(seed, site):
    high, low = divide(site)
    mixed = divide(seed * seed + low)[1]
    mixed = divide(mixed * mixed + high * 977 + 31)[1]
    angles = []
    for index in range(7):
        g = divide(mixed + (5171 * index + 1))[1]
        g = divide(g * g + low)[1]
        g = divide(g * g + 12345)[1]
        angles.append(g.astype(F32) * (2.0 * math.pi / MODULUS) - math.pi)
    return angles


def store_links(u_ref, seed, site):
    a = link_angles(seed, site)
    ca, sa = jnp.cos(a[0]), jnp.sin(a[0])
    cb, sb = jnp.cos(a[1]), jnp.sin(a[1])
    cg, sg = jnp.cos(a[2]), jnp.sin(a[2])
    rotation = [
        [ca * cb * cg - sa * sg, -ca * cb * sg - sa * cg, ca * sb],
        [sa * cb * cg + ca * sg, -sa * cb * sg + ca * cg, sa * sb],
        [-sb * cg, sb * sg, cb],
    ]
    left = [a[3], a[4], -a[3] - a[4]]
    right = [a[5], a[6], -a[5] - a[6]]
    for c in range(3):
        for s in range(3):
            phase = left[c] + right[s]
            u_ref[2 * (3 * c + s)] = rotation[c][s] * jnp.cos(phase)
            u_ref[2 * (3 * c + s) + 1] = rotation[c][s] * jnp.sin(phase)


def hop(vector_ref, out_ref, u_ref, first, count):
    all_modes, plane = vector_ref.shape[0] // 2, vector_ref.shape[1] // 3
    wide = (STEP // 8, 8, LANES)
    for t in range(plane // LANES):
        u = [jnp.broadcast_to(u_ref[k, t : t + 1, :], (8, LANES)) for k in range(18)]

        def body(block, carry, t=t, u=u):
            rows = [
                pl.ds(pl.multiple_of(part * all_modes + first + block * STEP, STEP), STEP)
                for part in range(2)
            ]
            lanes = [slice(c * plane + t * LANES, c * plane + (t + 1) * LANES) for c in range(3)]
            v = [
                [vector_ref[rows[part], lanes[c]].astype(F32).reshape(wide) for part in range(2)]
                for c in range(3)
            ]
            for c in range(3):
                real = imag = None
                for s in range(3):
                    ur, ui = u[2 * (3 * c + s)], u[2 * (3 * c + s) + 1]
                    re, im = v[s]
                    real = ur * re if real is None else real + ur * re
                    real = real - ui * im
                    imag = ur * im if imag is None else imag + ur * im
                    imag = imag + ui * re
                for part, value in ((0, real), (1, imag)):
                    out_ref[rows[part], lanes[c]] = value.reshape(STEP, LANES).astype(BF16)
            return carry

        lax.fori_loop(0, count // STEP, body, 0)


def products(left_ref, hop_ref):
    n = left_ref.shape[0] // 2
    with_real = dot(left_ref[...], hop_ref[:n, :], NT)
    with_imag = dot(left_ref[...], hop_ref[n:, :], NT)
    return with_real[:n] + with_imag[n:], with_imag[:n] - with_real[n:]


class Slots:
    LOW = 2 * LANES

    def __init__(self, all_modes, slots):
        self.tiles = all_modes // TM
        assert 2 * self.tiles == LANES
        self.half = self.tiles // 2
        self.columns = 2 * TM * TM
        self.high = self.half * self.tiles // self.LOW
        assert self.high * self.columns == self.LOW
        self.depth = self.LOW + LANES
        self.groups = LANES // self.columns
        self.per_group = -(-slots // self.groups)
        self.rows = round_up(self.per_group, 8)
        self.all_rows = round_up(self.groups * self.rows, 16)
        assert self.all_rows == self.groups * self.rows

    def codes(self, pair):
        n = self.tiles

        def start(i):
            return i * n - (i * (i - 1)) // 2

        inside = ((2 * n + 1) ** 2 - 8 * pair).astype(F32)
        i = ((2 * n + 1 - jnp.sqrt(inside)) * 0.5).astype(jnp.int32)
        i = jnp.where(start(i) > pair, i - 1, i)
        i = jnp.where(start(i + 1) <= pair, i + 1, i)
        j = i + pair - start(i)
        first = i < self.half
        place = jnp.where(first, i * n + j, (n - 1 - i) * n + (n - 1 - j))
        corner = jnp.logical_and(jnp.logical_not(first), i == j)
        high = jnp.where(corner, 0, place // self.LOW)
        low = jnp.where(corner, self.LOW + (n - 1 - i), place % self.LOW)
        return high * 512 + low

    def arrange(self, codes):
        devices, slots = codes.shape
        spread = jnp.pad(
            codes, ((0, 0), (0, self.groups * self.per_group - slots)), constant_values=-1
        ).reshape(devices, self.groups, self.per_group)
        spread = jnp.pad(
            spread, ((0, 0), (0, 0), (0, self.rows - self.per_group)), constant_values=-1
        )
        return spread.reshape(devices, self.all_rows).T


def store_table(table_ref, fold_ref, real, imag, slots):
    all_modes = real.shape[0]
    n, half = slots.tiles, slots.half
    parts = [real - real.T, imag + imag.T]

    def choose(count, width, turned):
        row, column = iota((count, all_modes), 0), iota((count, all_modes), 1)
        r, i = row // width, row % width
        if turned:
            i = n - 1 - i
        return (column == i * TM + r).astype(F32).astype(BF16)

    pick = [choose(TM * half, half, turned) for turned in (False, True)]
    spread = [choose(all_modes, n, turned) for turned in (False, True)]
    row_i = iota((TM * half, all_modes), 0) % half
    lane_j = iota((TM * half, all_modes), 1) % n
    corners = []
    for part in range(2):
        entries = parts[part].astype(BF16)
        straight, turned = [
            dot(dot(pick[k], entries).astype(BF16), spread[k], NT) for k in range(2)
        ]
        folded = jnp.where(lane_j >= row_i, straight, turned)
        for k in range(TM // 2):
            fold_ref[k, part * TM * half : (part + 1) * TM * half, :] = folded[
                :, k * LANES : (k + 1) * LANES
            ]
        diagonal = jnp.where(lane_j == row_i, turned, 0.0)
        for r in range(TM):
            corners.append(
                jnp.sum(diagonal[r * half : (r + 1) * half], axis=0, keepdims=True)
            )
    low = iota((2 * TM, LANES), 1) < n

    def split(even, odd, high, lanes):
        for pair in range(TM // 2):
            e, o = even[pair], odd[pair]
            top = high * slots.columns + 2 * pair * 2 * TM
            table_ref[top : top + 2 * TM, lanes] = jnp.where(low, e, pltpu.roll(o, n, 1))
            table_ref[top + 2 * TM : top + 4 * TM, lanes] = jnp.where(
                low, pltpu.roll(e, n, 1), o
            )

    halves = [slice(k * LANES, (k + 1) * LANES) for k in range(TM // 2)]
    for two in range(half // 2):
        even = [fold_ref[k, pl.ds(2 * two, 2 * TM, stride=half), :] for k in range(TM // 2)]
        odd = [fold_ref[k, pl.ds(2 * two + 1, 2 * TM, stride=half), :] for k in range(TM // 2)]
        at = two * LANES % slots.LOW
        split(even, odd, two * LANES // slots.LOW, slice(at, at + LANES))
    corner = jnp.concatenate(corners, 0)
    nothing = jnp.zeros((2 * TM, LANES), F32)
    table_ref[:, slots.LOW :] = jnp.zeros((slots.LOW, LANES), F32)
    split([corner[:, h] for h in halves], [nothing] * len(halves), 0, slice(slots.LOW, slots.depth))


def pick_tiles(emit, owner_ref, tables, chosen_ref, slots):
    inside, column = iota((slots.LOW, LANES), 0) % slots.columns, iota((slots.LOW, LANES), 1)
    entry = (inside % (2 * TM)) * TM + inside // (2 * TM)
    fold = (column % slots.columns == entry).astype(F32).astype(BF16)
    rows = slots.all_rows
    lane16 = iota((16, LANES), 1)
    lanes = [
        (lane16 + t * LANES).astype(jnp.int16) for t in range(slots.depth // LANES)
    ]
    one, zero = jnp.ones((16, LANES), BF16), jnp.zeros((16, LANES), BF16)
    lane_group = iota((slots.rows, LANES), 1) // slots.columns
    high_group = iota((rows, LANES), 1) // slots.columns
    count = owner_ref.shape[1] // 2
    for half in range(2):
        high = []
        for k in range(count):
            n = half * count + k
            code = jnp.broadcast_to(owner_ref[:, n : n + 1], (rows, LANES))
            high.append(code >> 9)
            low = (code & 511).astype(jnp.int16)
            for top in range(0, rows, 16):
                for t in range(slots.depth // LANES):
                    chosen_ref[
                        half, k * rows + top : k * rows + top + 16, t * LANES : (t + 1) * LANES
                    ] = jnp.where(low[top : top + 16] == lanes[t], one, zero)
        for d, table in enumerate(tables):
            parts = dot(chosen_ref[half], table, NT)
            masked = jnp.concatenate(
                [
                    jnp.concatenate(
                        [
                            jnp.where(
                                high[k] == high_group + side * slots.groups,
                                parts[k * rows : (k + 1) * rows, side * LANES : (side + 1) * LANES],
                                0.0,
                            )
                            for side in range(2)
                        ],
                        1,
                    ).astype(BF16)
                    for k in range(count)
                ],
                0,
            )
            picked = dot(masked, fold)
            for k in range(count):
                top = k * rows
                packed = picked[top : top + slots.rows]
                for g in range(1, slots.groups):
                    piece = picked[top + g * slots.rows : top + (g + 1) * slots.rows]
                    packed = jnp.where(lane_group == g, piece, packed)
                emit(half * count + k, d, packed.astype(BF16))


def store_all_links(links_ref, seed_ref, x):
    _, _, tiles, _ = links_ref.shape
    plane = tiles * LANES
    place = iota((tiles, LANES), 0) * LANES + iota((tiles, LANES), 1)
    before_y = jnp.where(place < NZ, place + (plane - NZ), place - NZ)
    before_z = jnp.where(place % NZ == 0, place + (NZ - 1), place - 1)
    for d, source in enumerate((place, before_y, before_z)):
        store_links(links_ref.at[d], seed_ref[d], source + x * plane)


def load_modes(planar_hbm, out_ref, sems, first, count):
    _, _, modes, plane = planar_hbm.shape
    copies = [
        pltpu.make_async_copy(
            planar_hbm.at[c, part, pl.ds(first, count)],
            out_ref.at[
                pl.ds(part * modes + first, count), pl.ds(c * plane, plane)
            ],
            sems.at[2 * c + part],
        )
        for c in range(3)
        for part in range(2)
    ]
    for copy in copies:
        copy.start()
    return copies


def wait_all(copies):
    for copy in copies:
        copy.wait()


def store_left_y(out_ref, left_ref, plane):
    wide = 2 * LANES
    source, target = iota((wide, wide), 0), iota((wide, wide), 1)
    halves = source == (target // LANES) * LANES + (target + NZ) % LANES
    halves = halves.astype(F32).astype(BF16)
    low = iota((left_ref.shape[0], LANES), 1) < NZ
    for c in range(3):
        swapped = []
        for start in range(c * plane, (c + 1) * plane, wide):
            both = dot(left_ref[:, start : start + wide], halves)
            swapped += [both[:, :LANES], both[:, LANES:]]
        for t in range(plane // LANES):
            lanes = slice(c * plane + t * LANES, c * plane + (t + 1) * LANES)
            out_ref[:, lanes] = jnp.where(low, swapped[t - 1], swapped[t]).astype(BF16)


def store_left_z(out_ref, left_ref, plane):
    wide = 2 * LANES
    source, target = iota((wide, wide), 0), iota((wide, wide), 1)
    before = jnp.where(target % NZ == 0, target + (NZ - 1), target - 1)
    behind = (source == before).astype(F32).astype(BF16)
    for start in range(0, 3 * plane, wide):
        piece = dot(left_ref[:, start : start + wide], behind)
        out_ref[:, start : start + wide] = piece.astype(BF16)


def inner_kernel(
    slots,
    seed_ref,
    where_ref,
    owner_ref,
    planar_hbm,
    out_ref,
    links_x_ref,
    vector_ref,
    left_ref,
    hop_ref,
    links_ref,
    table_ref,
    fold_ref,
    chosen_ref,
    sems,
):
    _, _, modes, plane = planar_hbm.shape
    copies = load_modes(planar_hbm, vector_ref, sems, 0, modes)
    store_all_links(links_ref, seed_ref, where_ref[0])
    links_x_ref[...] = links_ref[0]
    wait_all(copies)
    tables = []
    for d, store_left in ((1, store_left_y), (2, store_left_z)):
        store_left(left_ref, vector_ref, plane)
        hop(vector_ref, hop_ref, links_ref.at[d], 0, modes)
        real, imag = products(left_ref, hop_ref)
        store_table(table_ref.at[d - 1], fold_ref, real, imag, slots)
        tables.append(table_ref.at[d - 1])

    def emit(n, d, packed):
        out_ref[n, d] = packed

    pick_tiles(emit, owner_ref, [t[...].astype(BF16) for t in tables], chosen_ref, slots)


def outer_kernel(
    slots,
    owner_ref,
    links_ref,
    upper_hbm,
    planar_hbm,
    *refs,
):
    near = len(refs) - 8
    sent_hbm, refs = refs[:near], refs[near:]
    vector_ref, left_ref, hop_ref, table_ref, fold_ref, chosen_ref, stage_ref, sems = refs
    _, _, modes, plane = planar_hbm.shape
    part = modes // CHUNKS
    arriving = [
        load_modes(upper_hbm, vector_ref, sems.at[q], q * part, part) for q in range(CHUNKS)
    ]
    own = load_modes(planar_hbm, left_ref, sems.at[CHUNKS], 0, modes)
    for q in range(CHUNKS):
        wait_all(arriving[q])
        hop(vector_ref, hop_ref, links_ref, q * part, part)
    wait_all(own)
    real, imag = products(left_ref, hop_ref)
    store_table(table_ref, fold_ref, real, imag, slots)
    per = stage_ref.shape[0] // near
    leaving = []

    def emit(n, d, packed):
        stage_ref[n] = packed
        k = n // per
        if n % per == per - 1:
            copy = pltpu.make_async_copy(
                stage_ref.at[pl.ds(k * per, per)], sent_hbm[k], sems.at[CHUNKS + 1, k]
            )
            copy.start()
            leaving.append(copy)

    pick_tiles(emit, owner_ref, [table_ref[...].astype(BF16)], chosen_ref, slots)
    wait_all(leaving)


def near_sum_kernel(where_ref, *refs):
    far = refs[0].shape[0]
    sources, outs = refs[:-far], refs[-far:]
    here = where_ref[0] // len(sources)
    for m in range(far):
        block = lax.rem(here + m, far)
        total = sources[0][block].astype(F32)
        for source in sources[1:]:
            total = total + source[block].astype(F32)
        outs[m][...] = total


def total_kernel(in_ref, out_ref):
    total = in_ref[0].astype(F32)
    for device in range(1, in_ref.shape[0]):
        total = total + in_ref[device].astype(F32)
    out_ref[...] = total


def finish_kernel(normalise, slots, *refs):
    sources, inner_ref, out_ref = refs[:-2], refs[-2], refs[-1]
    here = out_ref.shape[0]
    total = sources[0][...]
    for source in sources[1:]:
        total = total + source[...]
    for d, value in enumerate((total, inner_ref[0], inner_ref[1])):
        value = value * normalise
        for group in range(slots.groups):
            first = group * slots.per_group
            count = min(slots.per_group, here - first)
            out_ref[first : first + count, d * slots.columns : (d + 1) * slots.columns] = value[
                :count, group * slots.columns : (group + 1) * slots.columns
            ]


def params(mib):
    return pltpu.CompilerParams(vmem_limit_bytes=mib * 1024 * 1024)


def cost(flops, moved):
    return pl.CostEstimate(flops=flops, bytes_accessed=moved, transcendentals=0)


def per_device(eigvecs, link_seed, ownership):
    modes, _, _, layers, plane = eigvecs.shape
    assert layers == 1
    devices = lax.axis_size("sx")
    here = ownership.shape[0] // devices
    depth = 3 * plane
    tiles = plane // LANES
    slots = Slots(modes, here)
    vmem = pl.BlockSpec(memory_space=pltpu.VMEM)
    smem = pl.BlockSpec(memory_space=pltpu.SMEM)
    anywhere = pl.BlockSpec(memory_space=pl.ANY)

    planar = eigvecs.reshape(modes, 2, 3, plane).transpose(2, 1, 0, 3)
    planar = lax.optimization_barrier(planar)
    route = [(i, (i - 1) % devices) for i in range(devices)]
    upper = lax.ppermute(planar, "sx", route)

    where = lax.axis_index("sx").reshape(1).astype(jnp.int32)
    codes = slots.codes(ownership).reshape(devices, here)
    owners = slots.arrange(codes)
    near = 1
    while near * near < devices:
        near *= 2
    far = devices // near
    turned = jnp.roll(codes.reshape(far, near, here), -(where[0] % near), 1)
    owners_x = slots.arrange(turned.transpose(1, 0, 2).reshape(devices, here))
    flops = 4 * modes * modes * depth * 2
    wide = pltpu.VMEM((2 * modes, depth), BF16)
    table = (slots.LOW, slots.depth)
    fold_scratch = pltpu.VMEM((TM // 2, modes, LANES), F32)
    chosen_scratch = pltpu.VMEM((2, devices // 2 * slots.all_rows, slots.depth), BF16)

    sent_inner, links_x = pl.pallas_call(
        functools.partial(inner_kernel, slots),
        name="inner_directions",
        out_shape=(
            jax.ShapeDtypeStruct((devices, 2, slots.rows, LANES), BF16),
            jax.ShapeDtypeStruct((18, tiles, LANES), F32),
        ),
        in_specs=[smem, smem, vmem, anywhere],
        out_specs=(vmem, vmem),
        scratch_shapes=[
            wide,
            wide,
            wide,
            pltpu.VMEM((3, 18, tiles, LANES), F32),
            pltpu.VMEM((2,) + table, F32),
            fold_scratch,
            chosen_scratch,
            pltpu.SemaphoreType.DMA((6,)),
        ],
        compiler_params=params(40),
        cost_estimate=cost(6 * flops, 8 * 2**20),
    )(link_seed, where, owners, planar)
    received_inner = lax.all_to_all(sent_inner, "sx", 0, 0)
    total_inner = pl.pallas_call(
        total_kernel,
        name="sum_inner",
        out_shape=jax.ShapeDtypeStruct((2, slots.rows, LANES), F32),
        in_specs=[vmem],
        out_specs=vmem,
        compiler_params=params(8),
        cost_estimate=cost(2**20, 2**20),
    )(received_inner)

    sent_x = pl.pallas_call(
        functools.partial(outer_kernel, slots),
        name="outer_direction",
        out_shape=[jax.ShapeDtypeStruct((far, slots.rows, LANES), BF16)] * near,
        in_specs=[vmem, vmem, anywhere, anywhere],
        out_specs=[anywhere] * near,
        scratch_shapes=[
            wide,
            wide,
            wide,
            pltpu.VMEM(table, F32),
            fold_scratch,
            chosen_scratch,
            pltpu.VMEM((devices, slots.rows, LANES), BF16),
            pltpu.SemaphoreType.DMA((CHUNKS + 2, max(6, near))),
        ],
        compiler_params=params(32),
        cost_estimate=cost(3 * flops, 8 * 2**20),
    )(owners_x, links_x, upper, planar)

    def onward(step, block, size, inner):
        def target(i):
            index = i // inner % size
            return i + ((index + step) % size - index) * inner

        return lax.ppermute(block, "sx", [(i, target(i)) for i in range(devices)])

    gathered = [sent_x[0]] + [onward(k, sent_x[k], near, 1) for k in range(1, near)]
    halfway = pl.pallas_call(
        near_sum_kernel,
        name="sum_near",
        out_shape=[jax.ShapeDtypeStruct((slots.rows, LANES), F32)] * far,
        in_specs=[smem] + [vmem] * near,
        out_specs=[vmem] * far,
        compiler_params=params(8),
        cost_estimate=cost(2**20, 2**20),
    )(where, *gathered)
    arrived = [halfway[0]] + [onward(m, halfway[m], far, near) for m in range(1, far)]

    extent_x = layers * devices
    normalise = 1.0 / math.sqrt(12.0 * extent_x * plane)
    return pl.pallas_call(
        functools.partial(finish_kernel, normalise, slots),
        name="sum_far",
        out_shape=jax.ShapeDtypeStruct((here, 3 * slots.columns), F32),
        in_specs=[vmem] * (far + 1),
        out_specs=vmem,
        compiler_params=params(8),
    )(*arrived, total_inner)


def solution(mesh):
    return jax.shard_map(
        per_device,
        mesh=mesh,
        in_specs=(P("cfg", None, None, "sx", None), P("cfg"), P()),
        out_specs=P(("cfg", "sx"), None),
        check_vma=False,
    )
```

```python
import functools
import math

import jax
import jax.numpy as jnp
from jax import lax
from jax.experimental import pallas as pl
from jax.experimental.pallas import tpu as pltpu
from jax.sharding import PartitionSpec as P

TM = 4
NZ = 64
LANES = 128
MODULUS = 46337
STEP = 32
F32 = jnp.float32
BF16 = jnp.bfloat16
NT = (((1,), (1,)), ((), ()))


def dot(left, right, dims=(((1,), (0,)), ((), ()))):
    return lax.dot_general(left, right, dims, preferred_element_type=F32)


def iota(shape, axis):
    return lax.broadcasted_iota(jnp.int32, shape, axis)


def round_up(value, step):
    return -(-value // step) * step


def divide(value):
    quotient = (value.astype(F32) * (1.0 / MODULUS)).astype(jnp.int32)
    rest = value - quotient * MODULUS
    below, above = rest < 0, rest >= MODULUS
    rest = jnp.where(below, rest + MODULUS, jnp.where(above, rest - MODULUS, rest))
    quotient = jnp.where(below, quotient - 1, jnp.where(above, quotient + 1, quotient))
    return quotient, rest


def link_angles(seed, site):
    high, low = divide(site)
    mixed = divide(seed * seed + low)[1]
    mixed = divide(mixed * mixed + high * 977 + 31)[1]
    angles = []
    for index in range(7):
        g = divide(mixed + (5171 * index + 1))[1]
        g = divide(g * g + low)[1]
        g = divide(g * g + 12345)[1]
        angles.append(g.astype(F32) * (2.0 * math.pi / MODULUS) - math.pi)
    return angles


def store_links(u_ref, seed, site):
    a = link_angles(seed, site)
    ca, sa = jnp.cos(a[0]), jnp.sin(a[0])
    cb, sb = jnp.cos(a[1]), jnp.sin(a[1])
    cg, sg = jnp.cos(a[2]), jnp.sin(a[2])
    rotation = [
        [ca * cb * cg - sa * sg, -ca * cb * sg - sa * cg, ca * sb],
        [sa * cb * cg + ca * sg, -sa * cb * sg + ca * cg, sa * sb],
        [-sb * cg, sb * sg, cb],
    ]
    left = [a[3], a[4], -a[3] - a[4]]
    right = [a[5], a[6], -a[5] - a[6]]
    for c in range(3):
        for s in range(3):
            phase = left[c] + right[s]
            u_ref[2 * (3 * c + s)] = rotation[c][s] * jnp.cos(phase)
            u_ref[2 * (3 * c + s) + 1] = rotation[c][s] * jnp.sin(phase)


def hop(vector_ref, out_ref, u_ref, first, count):
    all_modes, plane = vector_ref.shape[0] // 2, vector_ref.shape[1] // 3
    wide = (STEP // 8, 8, LANES)
    for t in range(plane // LANES):
        u = [jnp.broadcast_to(u_ref[k, t : t + 1, :], (8, LANES)) for k in range(18)]

        def body(block, carry, t=t, u=u):
            rows = [
                pl.ds(pl.multiple_of(part * all_modes + first + block * STEP, STEP), STEP)
                for part in range(2)
            ]
            lanes = [slice(c * plane + t * LANES, c * plane + (t + 1) * LANES) for c in range(3)]
            v = [
                [vector_ref[rows[part], lanes[c]].astype(F32).reshape(wide) for part in range(2)]
                for c in range(3)
            ]
            for c in range(3):
                real = imag = None
                for s in range(3):
                    ur, ui = u[2 * (3 * c + s)], u[2 * (3 * c + s) + 1]
                    re, im = v[s]
                    real = ur * re if real is None else real + ur * re
                    real = real - ui * im
                    imag = ur * im if imag is None else imag + ur * im
                    imag = imag + ui * re
                for part, value in ((0, real), (1, imag)):
                    out_ref[rows[part], lanes[c]] = value.reshape(STEP, LANES).astype(BF16)
            return carry

        lax.fori_loop(0, count // STEP, body, 0)


def products(left_ref, hop_ref):
    n, modes = left_ref.shape[0] // 2, hop_ref.shape[0] // 2
    by_real = dot(left_ref[:n, :], hop_ref[...], NT)
    by_imag = dot(left_ref[n:, :], hop_ref[...], NT)
    if modes % LANES:
        crossed = pltpu.roll(by_imag, modes, 1)
        low = iota(crossed.shape, 1) < modes
        return jnp.where(low, by_real + crossed, by_real - crossed)
    real = by_real[:, :modes] + by_imag[:, modes:]
    imag = by_real[:, modes:] - by_imag[:, :modes]
    return real, imag


class Slots:
    LOW = 2 * LANES

    def __init__(self, all_modes, slots):
        self.tiles = all_modes // TM
        assert 2 * self.tiles == LANES
        self.half = self.tiles // 2
        self.columns = 2 * TM * TM
        self.high = self.half * self.tiles // self.LOW
        assert self.high * self.columns == self.LOW
        self.depth = self.LOW + LANES
        self.groups = LANES // self.columns
        self.per_group = -(-slots // self.groups)
        self.rows = round_up(self.per_group, 8)
        self.all_rows = round_up(self.groups * self.rows, 16)
        assert self.all_rows == self.groups * self.rows

    def codes(self, pair):
        n = self.tiles

        def start(i):
            return i * n - (i * (i - 1)) // 2

        inside = ((2 * n + 1) ** 2 - 8 * pair).astype(F32)
        i = ((2 * n + 1 - jnp.sqrt(inside)) * 0.5).astype(jnp.int32)
        i = jnp.where(start(i) > pair, i - 1, i)
        i = jnp.where(start(i + 1) <= pair, i + 1, i)
        j = i + pair - start(i)
        first = i < self.half
        place = jnp.where(first, i * n + j, (n - 1 - i) * n + (n - 1 - j))
        corner = jnp.logical_and(jnp.logical_not(first), i == j)
        high = jnp.where(corner, 0, place // self.LOW)
        low = jnp.where(corner, self.LOW + (n - 1 - i), place % self.LOW)
        return high * 512 + low

    def arrange(self, codes):
        devices, slots = codes.shape
        spread = jnp.pad(
            codes, ((0, 0), (0, self.groups * self.per_group - slots)), constant_values=-1
        ).reshape(devices, self.groups, self.per_group)
        spread = jnp.pad(
            spread, ((0, 0), (0, 0), (0, self.rows - self.per_group)), constant_values=-1
        )
        return spread.reshape(devices, self.all_rows).T


def store_table(table_ref, fold_ref, real, imag, slots):
    all_modes = real.shape[0]
    n, half = slots.tiles, slots.half
    parts = [real - real.T, imag + imag.T]

    def choose(count, width, turned):
        row, column = iota((count, all_modes), 0), iota((count, all_modes), 1)
        r, i = row // width, row % width
        if turned:
            i = n - 1 - i
        return (column == i * TM + r).astype(F32).astype(BF16)

    pick = [choose(TM * half, half, turned) for turned in (False, True)]
    spread = [choose(all_modes, n, turned) for turned in (False, True)]
    row_i = iota((TM * half, all_modes), 0) % half
    lane_j = iota((TM * half, all_modes), 1) % n
    corners = []
    for part in range(2):
        entries = parts[part].astype(BF16)
        straight, turned = [
            dot(dot(pick[k], entries).astype(BF16), spread[k], NT) for k in range(2)
        ]
        folded = jnp.where(lane_j >= row_i, straight, turned)
        for k in range(TM // 2):
            fold_ref[k, part * TM * half : (part + 1) * TM * half, :] = folded[
                :, k * LANES : (k + 1) * LANES
            ]
        diagonal = jnp.where(lane_j == row_i, turned, 0.0)
        for r in range(TM):
            corners.append(
                jnp.sum(diagonal[r * half : (r + 1) * half], axis=0, keepdims=True)
            )
    low = iota((2 * TM, LANES), 1) < n

    def split(even, odd, high, lanes):
        for pair in range(TM // 2):
            e, o = even[pair], odd[pair]
            top = high * slots.columns + 2 * pair * 2 * TM
            table_ref[top : top + 2 * TM, lanes] = jnp.where(low, e, pltpu.roll(o, n, 1))
            table_ref[top + 2 * TM : top + 4 * TM, lanes] = jnp.where(
                low, pltpu.roll(e, n, 1), o
            )

    halves = [slice(k * LANES, (k + 1) * LANES) for k in range(TM // 2)]
    for two in range(half // 2):
        even = [fold_ref[k, pl.ds(2 * two, 2 * TM, stride=half), :] for k in range(TM // 2)]
        odd = [fold_ref[k, pl.ds(2 * two + 1, 2 * TM, stride=half), :] for k in range(TM // 2)]
        at = two * LANES % slots.LOW
        split(even, odd, two * LANES // slots.LOW, slice(at, at + LANES))
    corner = jnp.concatenate(corners, 0)
    nothing = jnp.zeros((2 * TM, LANES), F32)
    table_ref[:, slots.LOW :] = jnp.zeros((slots.LOW, LANES), F32)
    split([corner[:, h] for h in halves], [nothing] * len(halves), 0, slice(slots.LOW, slots.depth))


def pick_tiles(emit, owner_ref, tables, chosen_ref, slots):
    inside, column = iota((slots.LOW, LANES), 0) % slots.columns, iota((slots.LOW, LANES), 1)
    entry = (inside % (2 * TM)) * TM + inside // (2 * TM)
    fold = (column % slots.columns == entry).astype(F32).astype(BF16)
    rows = slots.all_rows
    lane16 = iota((16, LANES), 1)
    lanes = [
        (lane16 + t * LANES).astype(jnp.int16) for t in range(slots.depth // LANES)
    ]
    one, zero = jnp.ones((16, LANES), BF16), jnp.zeros((16, LANES), BF16)
    lane_group = iota((slots.rows, LANES), 1) // slots.columns
    high_group = iota((rows, LANES), 1) // slots.columns
    count = owner_ref.shape[1] // 2
    for half in range(2):
        high = []
        for k in range(count):
            n = half * count + k
            code = jnp.broadcast_to(owner_ref[:, n : n + 1], (rows, LANES))
            high.append(code >> 9)
            low = (code & 511).astype(jnp.int16)
            for top in range(0, rows, 16):
                for t in range(slots.depth // LANES):
                    chosen_ref[
                        half, k * rows + top : k * rows + top + 16, t * LANES : (t + 1) * LANES
                    ] = jnp.where(low[top : top + 16] == lanes[t], one, zero)
        for d, table in enumerate(tables):
            parts = dot(chosen_ref[half], table, NT)
            masked = jnp.concatenate(
                [
                    jnp.concatenate(
                        [
                            jnp.where(
                                high[k] == high_group + side * slots.groups,
                                parts[k * rows : (k + 1) * rows, side * LANES : (side + 1) * LANES],
                                0.0,
                            )
                            for side in range(2)
                        ],
                        1,
                    ).astype(BF16)
                    for k in range(count)
                ],
                0,
            )
            picked = dot(masked, fold)
            for k in range(count):
                top = k * rows
                packed = picked[top : top + slots.rows]
                for g in range(1, slots.groups):
                    piece = picked[top + g * slots.rows : top + (g + 1) * slots.rows]
                    packed = jnp.where(lane_group == g, piece, packed)
                emit(half * count + k, d, packed.astype(BF16))


def store_all_links(links_ref, seed_ref, x):
    _, _, tiles, _ = links_ref.shape
    plane = tiles * LANES
    place = iota((tiles, LANES), 0) * LANES + iota((tiles, LANES), 1)
    before_y = jnp.where(place < NZ, place + (plane - NZ), place - NZ)
    before_z = jnp.where(place % NZ == 0, place + (NZ - 1), place - 1)
    for d, source in enumerate((place, before_y, before_z)):
        store_links(links_ref.at[d], seed_ref[d], source + x * plane)


def load_modes(planar_hbm, out_ref, sems, first):
    _, _, count, plane = planar_hbm.shape
    modes = out_ref.shape[0] // 2
    copies = [
        pltpu.make_async_copy(
            planar_hbm.at[c, part],
            out_ref.at[pl.ds(part * modes + first, count), pl.ds(c * plane, plane)],
            sems.at[2 * c + part],
        )
        for c in range(3)
        for part in range(2)
    ]
    for copy in copies:
        copy.start()
    return copies


def load_all(parts, out_ref, sems):
    quarter = out_ref.shape[0] // 8
    copies = []
    for k, (first, _) in enumerate(chunks_of(4 * quarter)):
        copies += load_modes(parts[k], out_ref, sems.at[k], first)
    return copies


def wait_all(copies):
    for copy in copies:
        copy.wait()


def store_left_y(out_ref, left_ref, plane):
    wide = 2 * LANES
    source, target = iota((wide, wide), 0), iota((wide, wide), 1)
    halves = source == (target // LANES) * LANES + (target + NZ) % LANES
    halves = halves.astype(F32).astype(BF16)
    low = iota((left_ref.shape[0], LANES), 1) < NZ
    for c in range(3):
        swapped = []
        for start in range(c * plane, (c + 1) * plane, wide):
            both = dot(left_ref[:, start : start + wide], halves)
            swapped += [both[:, :LANES], both[:, LANES:]]
        for t in range(plane // LANES):
            lanes = slice(c * plane + t * LANES, c * plane + (t + 1) * LANES)
            out_ref[:, lanes] = jnp.where(low, swapped[t - 1], swapped[t]).astype(BF16)


def store_left_z(out_ref, left_ref, plane):
    wide = 2 * LANES
    source, target = iota((wide, wide), 0), iota((wide, wide), 1)
    before = jnp.where(target % NZ == 0, target + (NZ - 1), target - 1)
    behind = (source == before).astype(F32).astype(BF16)
    for start in range(0, 3 * plane, wide):
        piece = dot(left_ref[:, start : start + wide], behind)
        out_ref[:, start : start + wide] = piece.astype(BF16)


def load_kernel(first, whole_hbm, *refs):
    out_ref, sem = refs[-2:]
    copy = pltpu.make_async_copy(whole_hbm.at[pl.ds(first, out_ref.shape[0])], out_ref, sem)
    copy.start()
    copy.wait()


def inner_kernel(
    slots,
    seed_ref,
    where_ref,
    owner_ref,
    first_hbm,
    second_hbm,
    third_hbm,
    out_ref,
    links_x_ref,
    vector_ref,
    left_ref,
    hop_ref,
    links_ref,
    table_ref,
    fold_ref,
    chosen_ref,
    sems,
):
    modes, plane = vector_ref.shape[0] // 2, vector_ref.shape[1] // 3
    copies = load_all((first_hbm, second_hbm, third_hbm), vector_ref, sems)
    store_all_links(links_ref, seed_ref, where_ref[0])
    links_x_ref[...] = links_ref[0]
    wait_all(copies)
    tables = []
    for d, store_left in ((1, store_left_y), (2, store_left_z)):
        store_left(left_ref, vector_ref, plane)
        hop(vector_ref, hop_ref, links_ref.at[d], 0, modes)
        real, imag = products(left_ref, hop_ref)
        store_table(table_ref.at[d - 1], fold_ref, real, imag, slots)
        tables.append(table_ref.at[d - 1])

    def emit(n, d, packed):
        out_ref[n, d] = packed

    pick_tiles(emit, owner_ref, [t[...].astype(BF16) for t in tables], chosen_ref, slots)


def outer_chunk(links_ref, upper_hbm, own_hbm, vector_ref, left_ref, hop_ref, sems):
    arriving = load_modes(upper_hbm, vector_ref, sems.at[3], 0)
    own = load_all(own_hbm, left_ref, sems)
    wait_all(arriving)
    hop(vector_ref, hop_ref, links_ref, 0, vector_ref.shape[0] // 2)
    wait_all(own)
    return products(left_ref, hop_ref)


def narrow_kernel(links_ref, upper_hbm, a, b, c, out_ref, *scratch):
    out_ref[...] = outer_chunk(links_ref, upper_hbm, (a, b, c), *scratch)


def wide_kernel(links_ref, upper_hbm, a, b, c, out_ref, *scratch):
    out_ref[0], out_ref[1] = outer_chunk(links_ref, upper_hbm, (a, b, c), *scratch)


def last_kernel(
    slots,
    owner_ref,
    narrow_ref,
    wide_ref,
    links_ref,
    upper_hbm,
    a,
    b,
    c,
    out_ref,
    vector_ref,
    left_ref,
    hop_ref,
    sems,
    table_ref,
    fold_ref,
    chosen_ref,
):
    first = narrow_ref[...]
    last = outer_chunk(links_ref, upper_hbm, (a, b, c), vector_ref, left_ref, hop_ref, sems)
    modes = last.shape[1] // 2
    low = iota(last.shape, 1) < modes
    real = jnp.where(low, first, pltpu.roll(last, modes, 1))
    imag = jnp.where(low, pltpu.roll(first, modes, 1), last)
    real = jnp.concatenate([real, wide_ref[0]], 1)
    imag = jnp.concatenate([imag, wide_ref[1]], 1)
    store_table(table_ref, fold_ref, real, imag, slots)
    near = out_ref.shape[0]

    def emit(n, d, packed):
        out_ref[n % near, n // near] = packed

    pick_tiles(emit, owner_ref, [table_ref[...].astype(BF16)], chosen_ref, slots)


def total_kernel(in_ref, out_ref):
    total = in_ref[0].astype(F32)
    for device in range(1, in_ref.shape[0]):
        total = total + in_ref[device].astype(F32)
    out_ref[...] = total


def finish_kernel(normalise, slots, far_ref, inner_ref, out_ref):
    here = out_ref.shape[0]
    total = far_ref[0]
    for device in range(1, far_ref.shape[0]):
        total = total + far_ref[device]
    for d, value in enumerate((total, inner_ref[0], inner_ref[1])):
        value = value * normalise
        for group in range(slots.groups):
            first = group * slots.per_group
            count = min(slots.per_group, here - first)
            out_ref[first : first + count, d * slots.columns : (d + 1) * slots.columns] = value[
                :count, group * slots.columns : (group + 1) * slots.columns
            ]


def params(mib):
    return pltpu.CompilerParams(vmem_limit_bytes=mib * 1024 * 1024)


def cost(flops, moved):
    return pl.CostEstimate(flops=flops, bytes_accessed=moved, transcendentals=0)


def chunks_of(modes):
    quarter = modes // 4
    return ((0, quarter), (2 * quarter, 2 * quarter), (quarter, quarter))


def per_device(eigvecs, link_seed, ownership):
    modes, _, _, layers, plane = eigvecs.shape
    assert layers == 1
    devices = lax.axis_size("sx")
    here = ownership.shape[0] // devices
    depth = 3 * plane
    tiles = plane // LANES
    slots = Slots(modes, here)
    vmem = pl.BlockSpec(memory_space=pltpu.VMEM)
    smem = pl.BlockSpec(memory_space=pltpu.SMEM)
    anywhere = pl.BlockSpec(memory_space=pl.ANY)

    raw = eigvecs.transpose(0, 2, 3, 1, 4).reshape(3 * modes, 2, plane)
    route = [(i, (i - 1) % devices) for i in range(devices)]
    own, upper = [], []
    for first, count in chunks_of(modes):
        part = pl.pallas_call(
            functools.partial(load_kernel, 3 * first),
            name="load_modes",
            out_shape=jax.ShapeDtypeStruct((3 * count, 2, plane), BF16),
            in_specs=[anywhere] * (1 + len(own[-1:])),
            out_specs=vmem,
            scratch_shapes=[pltpu.SemaphoreType.DMA],
            compiler_params=params(8),
            cost_estimate=cost(0, 12 * count * plane),
        )(raw, *own[-1:])
        part = part.reshape(count, 3, 2, plane).transpose(1, 2, 0, 3)
        own.append(part)
        upper.append(lax.ppermute(part, "sx", route))

    where = lax.axis_index("sx").reshape(1).astype(jnp.int32)
    owners = slots.arrange(slots.codes(ownership).reshape(devices, here))
    near = 1
    while near * near < devices:
        near *= 2
    far = devices // near
    flops = 4 * modes * modes * depth * 2
    wide = pltpu.VMEM((2 * modes, depth), BF16)
    table = (slots.LOW, slots.depth)
    fold_scratch = pltpu.VMEM((TM // 2, modes, LANES), F32)
    chosen_scratch = pltpu.VMEM((2, devices // 2 * slots.all_rows, slots.depth), BF16)

    sent_inner, links_x = pl.pallas_call(
        functools.partial(inner_kernel, slots),
        name="inner_directions",
        out_shape=(
            jax.ShapeDtypeStruct((devices, 2, slots.rows, LANES), BF16),
            jax.ShapeDtypeStruct((18, tiles, LANES), F32),
        ),
        in_specs=[smem, smem, vmem] + [anywhere] * 3,
        out_specs=(vmem, vmem),
        scratch_shapes=[
            wide,
            wide,
            wide,
            pltpu.VMEM((3, 18, tiles, LANES), F32),
            pltpu.VMEM((2,) + table, F32),
            fold_scratch,
            chosen_scratch,
            pltpu.SemaphoreType.DMA((3, 6)),
        ],
        compiler_params=params(40),
        cost_estimate=cost(6 * flops, 8 * 2**20),
    )(link_seed, where, owners, *own)
    received_inner = lax.all_to_all(sent_inner, "sx", 0, 0)
    total_inner = pl.pallas_call(
        total_kernel,
        name="sum_inner",
        out_shape=jax.ShapeDtypeStruct((2, slots.rows, LANES), F32),
        in_specs=[vmem],
        out_specs=vmem,
        compiler_params=params(8),
        cost_estimate=cost(2**20, 2**20),
    )(received_inner)

    def outer(kernel, name, size, out_shape, before, upper_part, more):
        return pl.pallas_call(
            kernel,
            name=name,
            out_shape=out_shape,
            in_specs=[vmem] * (len(before) + 1) + [anywhere] * 4,
            out_specs=vmem,
            scratch_shapes=[
                pltpu.VMEM((2 * size, depth), BF16),
                wide,
                pltpu.VMEM((2 * size, depth), BF16),
                pltpu.SemaphoreType.DMA((4, 6)),
            ]
            + more,
            compiler_params=params(24),
            cost_estimate=cost(flops * size // modes, 8 * 2**20),
        )(*before, links_x, upper_part, *own)

    sizes = [count for _, count in chunks_of(modes)]
    first_x = outer(
        narrow_kernel,
        "outer_first",
        sizes[0],
        jax.ShapeDtypeStruct((modes, LANES), F32),
        [],
        upper[0],
        [],
    )
    second_x = outer(
        wide_kernel,
        "outer_second",
        sizes[1],
        jax.ShapeDtypeStruct((2, modes, sizes[1]), F32),
        [],
        upper[1],
        [],
    )
    sent_x = outer(
        functools.partial(last_kernel, slots),
        "outer_last",
        sizes[2],
        jax.ShapeDtypeStruct((near, far, slots.rows, LANES), BF16),
        [owners, first_x, second_x],
        upper[2],
        [pltpu.VMEM(table, F32), fold_scratch, chosen_scratch],
    )

    near_groups = [[h * near + k for k in range(near)] for h in range(far)]
    far_groups = [[h * near + k for h in range(far)] for k in range(near)]
    gathered = lax.all_to_all(sent_x, "sx", 0, 0, axis_index_groups=near_groups)
    halfway = pl.pallas_call(
        total_kernel,
        name="sum_near",
        out_shape=jax.ShapeDtypeStruct((far, slots.rows, LANES), F32),
        in_specs=[vmem],
        out_specs=vmem,
        compiler_params=params(8),
        cost_estimate=cost(2**20, 2**20),
    )(gathered)
    arrived = lax.all_to_all(halfway, "sx", 0, 0, axis_index_groups=far_groups)

    extent_x = layers * devices
    normalise = 1.0 / math.sqrt(12.0 * extent_x * plane)
    return pl.pallas_call(
        functools.partial(finish_kernel, normalise, slots),
        name="sum_far",
        out_shape=jax.ShapeDtypeStruct((here, 3 * slots.columns), F32),
        in_specs=[vmem, vmem],
        out_specs=vmem,
        compiler_params=params(8),
    )(arrived, total_inner)


def solution(mesh):
    return jax.shard_map(
        per_device,
        mesh=mesh,
        in_specs=(P("cfg", None, None, "sx", None), P("cfg"), P()),
        out_specs=P(("cfg", "sx"), None),
        check_vma=False,
    )
```

```python
import functools
import math

import jax
import jax.numpy as jnp
from jax import lax
from jax.experimental import pallas as pl
from jax.experimental.pallas import tpu as pltpu
from jax.sharding import PartitionSpec as P

TM = 4
NZ = 64
LANES = 128
MODULUS = 46337
STEP = 32
F32 = jnp.float32
BF16 = jnp.bfloat16
NT = (((1,), (1,)), ((), ()))


def dot(left, right, dims=(((1,), (0,)), ((), ()))):
    return lax.dot_general(left, right, dims, preferred_element_type=F32)


def iota(shape, axis):
    return lax.broadcasted_iota(jnp.int32, shape, axis)


def round_up(value, step):
    return -(-value // step) * step


def divide(value):
    quotient = (value.astype(F32) * (1.0 / MODULUS)).astype(jnp.int32)
    rest = value - quotient * MODULUS
    below, above = rest < 0, rest >= MODULUS
    rest = jnp.where(below, rest + MODULUS, jnp.where(above, rest - MODULUS, rest))
    quotient = jnp.where(below, quotient - 1, jnp.where(above, quotient + 1, quotient))
    return quotient, rest


def link_angles(seed, site):
    high, low = divide(site)
    mixed = divide(seed * seed + low)[1]
    mixed = divide(mixed * mixed + high * 977 + 31)[1]
    angles = []
    for index in range(7):
        g = divide(mixed + (5171 * index + 1))[1]
        g = divide(g * g + low)[1]
        g = divide(g * g + 12345)[1]
        angles.append(g.astype(F32) * (2.0 * math.pi / MODULUS) - math.pi)
    return angles


def store_links(u_ref, seed, site):
    a = link_angles(seed, site)
    ca, sa = jnp.cos(a[0]), jnp.sin(a[0])
    cb, sb = jnp.cos(a[1]), jnp.sin(a[1])
    cg, sg = jnp.cos(a[2]), jnp.sin(a[2])
    rotation = [
        [ca * cb * cg - sa * sg, -ca * cb * sg - sa * cg, ca * sb],
        [sa * cb * cg + ca * sg, -sa * cb * sg + ca * cg, sa * sb],
        [-sb * cg, sb * sg, cb],
    ]
    left = [a[3], a[4], -a[3] - a[4]]
    right = [a[5], a[6], -a[5] - a[6]]
    for c in range(3):
        for s in range(3):
            phase = left[c] + right[s]
            u_ref[2 * (3 * c + s)] = rotation[c][s] * jnp.cos(phase)
            u_ref[2 * (3 * c + s) + 1] = rotation[c][s] * jnp.sin(phase)


def hop(vector_ref, out_ref, u_ref, first, count):
    all_modes, plane = vector_ref.shape[0] // 2, vector_ref.shape[1] // 3
    wide = (STEP // 8, 8, LANES)
    for t in range(plane // LANES):
        u = [jnp.broadcast_to(u_ref[k, t : t + 1, :], (8, LANES)) for k in range(18)]

        def body(block, carry, t=t, u=u):
            rows = [
                pl.ds(pl.multiple_of(part * all_modes + first + block * STEP, STEP), STEP)
                for part in range(2)
            ]
            lanes = [slice(c * plane + t * LANES, c * plane + (t + 1) * LANES) for c in range(3)]
            v = [
                [vector_ref[rows[part], lanes[c]].astype(F32).reshape(wide) for part in range(2)]
                for c in range(3)
            ]
            for c in range(3):
                real = imag = None
                for s in range(3):
                    ur, ui = u[2 * (3 * c + s)], u[2 * (3 * c + s) + 1]
                    re, im = v[s]
                    real = ur * re if real is None else real + ur * re
                    real = real - ui * im
                    imag = ur * im if imag is None else imag + ur * im
                    imag = imag + ui * re
                for part, value in ((0, real), (1, imag)):
                    out_ref[rows[part], lanes[c]] = value.reshape(STEP, LANES).astype(BF16)
            return carry

        lax.fori_loop(0, count // STEP, body, 0)


def products(left_ref, hop_ref):
    n, modes = left_ref.shape[0] // 2, hop_ref.shape[0] // 2
    by_real = dot(left_ref[:n, :], hop_ref[...], NT)
    by_imag = dot(left_ref[n:, :], hop_ref[...], NT)
    if modes % LANES:
        crossed = pltpu.roll(by_imag, modes, 1)
        low = iota(crossed.shape, 1) < modes
        return jnp.where(low, by_real + crossed, by_real - crossed)
    real = by_real[:, :modes] + by_imag[:, modes:]
    imag = by_real[:, modes:] - by_imag[:, :modes]
    return real, imag


class Slots:
    LOW = 2 * LANES

    def __init__(self, all_modes, slots):
        self.tiles = all_modes // TM
        assert 2 * self.tiles == LANES
        self.half = self.tiles // 2
        self.columns = 2 * TM * TM
        self.high = self.half * self.tiles // self.LOW
        assert self.high * self.columns == self.LOW
        self.depth = self.LOW + LANES
        self.groups = LANES // self.columns
        self.per_group = -(-slots // self.groups)
        self.rows = round_up(self.per_group, 8)
        self.all_rows = round_up(self.groups * self.rows, 16)
        assert self.all_rows == self.groups * self.rows

    def codes(self, pair):
        n = self.tiles

        def start(i):
            return i * n - (i * (i - 1)) // 2

        inside = ((2 * n + 1) ** 2 - 8 * pair).astype(F32)
        i = ((2 * n + 1 - jnp.sqrt(inside)) * 0.5).astype(jnp.int32)
        i = jnp.where(start(i) > pair, i - 1, i)
        i = jnp.where(start(i + 1) <= pair, i + 1, i)
        j = i + pair - start(i)
        first = i < self.half
        place = jnp.where(first, i * n + j, (n - 1 - i) * n + (n - 1 - j))
        corner = jnp.logical_and(jnp.logical_not(first), i == j)
        high = jnp.where(corner, 0, place // self.LOW)
        low = jnp.where(corner, self.LOW + (n - 1 - i), place % self.LOW)
        return high * 512 + low

    def arrange(self, codes):
        devices, slots = codes.shape
        spread = jnp.pad(
            codes, ((0, 0), (0, self.groups * self.per_group - slots)), constant_values=-1
        ).reshape(devices, self.groups, self.per_group)
        spread = jnp.pad(
            spread, ((0, 0), (0, 0), (0, self.rows - self.per_group)), constant_values=-1
        )
        return spread.reshape(devices, self.all_rows).T


def store_table(table_ref, fold_ref, real, imag, slots):
    all_modes = real.shape[0]
    n, half = slots.tiles, slots.half
    parts = [real - real.T, imag + imag.T]

    def choose(count, width, turned):
        row, column = iota((count, all_modes), 0), iota((count, all_modes), 1)
        r, i = row // width, row % width
        if turned:
            i = n - 1 - i
        return (column == i * TM + r).astype(F32).astype(BF16)

    pick = [choose(TM * half, half, turned) for turned in (False, True)]
    spread = [choose(all_modes, n, turned) for turned in (False, True)]
    row_i = iota((TM * half, all_modes), 0) % half
    lane_j = iota((TM * half, all_modes), 1) % n
    corners = []
    for part in range(2):
        entries = parts[part].astype(BF16)
        straight, turned = [
            dot(dot(pick[k], entries).astype(BF16), spread[k], NT) for k in range(2)
        ]
        folded = jnp.where(lane_j >= row_i, straight, turned)
        for k in range(TM // 2):
            fold_ref[k, part * TM * half : (part + 1) * TM * half, :] = folded[
                :, k * LANES : (k + 1) * LANES
            ]
        diagonal = jnp.where(lane_j == row_i, turned, 0.0)
        for r in range(TM):
            corners.append(
                jnp.sum(diagonal[r * half : (r + 1) * half], axis=0, keepdims=True)
            )
    low = iota((2 * TM, LANES), 1) < n

    def split(even, odd, high, lanes):
        for pair in range(TM // 2):
            e, o = even[pair], odd[pair]
            top = high * slots.columns + 2 * pair * 2 * TM
            table_ref[top : top + 2 * TM, lanes] = jnp.where(low, e, pltpu.roll(o, n, 1))
            table_ref[top + 2 * TM : top + 4 * TM, lanes] = jnp.where(
                low, pltpu.roll(e, n, 1), o
            )

    halves = [slice(k * LANES, (k + 1) * LANES) for k in range(TM // 2)]
    for two in range(half // 2):
        even = [fold_ref[k, pl.ds(2 * two, 2 * TM, stride=half), :] for k in range(TM // 2)]
        odd = [fold_ref[k, pl.ds(2 * two + 1, 2 * TM, stride=half), :] for k in range(TM // 2)]
        at = two * LANES % slots.LOW
        split(even, odd, two * LANES // slots.LOW, slice(at, at + LANES))
    corner = jnp.concatenate(corners, 0)
    nothing = jnp.zeros((2 * TM, LANES), F32)
    table_ref[:, slots.LOW :] = jnp.zeros((slots.LOW, LANES), F32)
    split([corner[:, h] for h in halves], [nothing] * len(halves), 0, slice(slots.LOW, slots.depth))


def pick_tiles(emit, owner_ref, tables, chosen_ref, slots):
    inside, column = iota((slots.LOW, LANES), 0) % slots.columns, iota((slots.LOW, LANES), 1)
    entry = (inside % (2 * TM)) * TM + inside // (2 * TM)
    fold = (column % slots.columns == entry).astype(F32).astype(BF16)
    rows = slots.all_rows
    lane16 = iota((16, LANES), 1)
    lanes = [
        (lane16 + t * LANES).astype(jnp.int16) for t in range(slots.depth // LANES)
    ]
    one, zero = jnp.ones((16, LANES), BF16), jnp.zeros((16, LANES), BF16)
    lane_group = iota((slots.rows, LANES), 1) // slots.columns
    high_group = iota((rows, LANES), 1) // slots.columns
    count = owner_ref.shape[1] // 2
    for half in range(2):
        high = []
        for k in range(count):
            n = half * count + k
            code = jnp.broadcast_to(owner_ref[:, n : n + 1], (rows, LANES))
            high.append(code >> 9)
            low = (code & 511).astype(jnp.int16)
            for top in range(0, rows, 16):
                for t in range(slots.depth // LANES):
                    chosen_ref[
                        half, k * rows + top : k * rows + top + 16, t * LANES : (t + 1) * LANES
                    ] = jnp.where(low[top : top + 16] == lanes[t], one, zero)
        for d, table in enumerate(tables):
            parts = dot(chosen_ref[half], table, NT)
            masked = jnp.concatenate(
                [
                    jnp.concatenate(
                        [
                            jnp.where(
                                high[k] == high_group + side * slots.groups,
                                parts[k * rows : (k + 1) * rows, side * LANES : (side + 1) * LANES],
                                0.0,
                            )
                            for side in range(2)
                        ],
                        1,
                    ).astype(BF16)
                    for k in range(count)
                ],
                0,
            )
            picked = dot(masked, fold)
            for k in range(count):
                top = k * rows
                packed = picked[top : top + slots.rows]
                for g in range(1, slots.groups):
                    piece = picked[top + g * slots.rows : top + (g + 1) * slots.rows]
                    packed = jnp.where(lane_group == g, piece, packed)
                emit(half * count + k, d, packed)


def store_all_links(links_ref, seed_ref, x):
    _, _, tiles, _ = links_ref.shape
    plane = tiles * LANES
    place = iota((tiles, LANES), 0) * LANES + iota((tiles, LANES), 1)
    before_y = jnp.where(place < NZ, place + (plane - NZ), place - NZ)
    before_z = jnp.where(place % NZ == 0, place + (NZ - 1), place - 1)
    for d, source in enumerate((place, before_y, before_z)):
        store_links(links_ref.at[d], seed_ref[d], source + x * plane)


def load_modes(planar_hbm, out_ref, sems, first):
    _, _, count, plane = planar_hbm.shape
    modes = out_ref.shape[0] // 2
    copies = [
        pltpu.make_async_copy(
            planar_hbm.at[c, part],
            out_ref.at[pl.ds(part * modes + first, count), pl.ds(c * plane, plane)],
            sems.at[2 * c + part],
        )
        for c in range(3)
        for part in range(2)
    ]
    for copy in copies:
        copy.start()
    return copies


def load_all(parts, out_ref, sems):
    quarter = out_ref.shape[0] // 8
    copies = []
    for k, (first, _) in enumerate(chunks_of(4 * quarter)):
        copies += load_modes(parts[k], out_ref, sems.at[k], first)
    return copies


def wait_all(copies):
    for copy in copies:
        copy.wait()


def store_left_y(out_ref, left_ref, plane):
    wide = 2 * LANES
    source, target = iota((wide, wide), 0), iota((wide, wide), 1)
    halves = source == (target // LANES) * LANES + (target + NZ) % LANES
    halves = halves.astype(F32).astype(BF16)
    low = iota((left_ref.shape[0], LANES), 1) < NZ
    for c in range(3):
        swapped = []
        for start in range(c * plane, (c + 1) * plane, wide):
            both = dot(left_ref[:, start : start + wide], halves)
            swapped += [both[:, :LANES], both[:, LANES:]]
        for t in range(plane // LANES):
            lanes = slice(c * plane + t * LANES, c * plane + (t + 1) * LANES)
            out_ref[:, lanes] = jnp.where(low, swapped[t - 1], swapped[t]).astype(BF16)


def store_left_z(out_ref, left_ref, plane):
    wide = 2 * LANES
    source, target = iota((wide, wide), 0), iota((wide, wide), 1)
    before = jnp.where(target % NZ == 0, target + (NZ - 1), target - 1)
    behind = (source == before).astype(F32).astype(BF16)
    for start in range(0, 3 * plane, wide):
        piece = dot(left_ref[:, start : start + wide], behind)
        out_ref[:, start : start + wide] = piece.astype(BF16)


def load_kernel(starts, whole_hbm, *refs):
    parts, sems = refs[:-1], refs[-1]
    copies = [
        pltpu.make_async_copy(whole_hbm.at[pl.ds(start, part.shape[0])], part, sems.at[k])
        for k, (start, part) in enumerate(zip(starts, parts))
    ]
    for copy in copies:
        copy.start()
    wait_all(copies)


def inner_kernel(
    slots,
    seed_ref,
    where_ref,
    owner_ref,
    first_hbm,
    last_hbm,
    out_ref,
    links_x_ref,
    vector_ref,
    left_ref,
    hop_ref,
    links_ref,
    table_ref,
    fold_ref,
    chosen_ref,
    sems,
):
    modes, plane = vector_ref.shape[0] // 2, vector_ref.shape[1] // 3
    copies = load_all((first_hbm, last_hbm), vector_ref, sems)
    store_all_links(links_ref, seed_ref, where_ref[0])
    links_x_ref[...] = links_ref[0]
    wait_all(copies)
    tables = []
    for d, store_left in ((1, store_left_y), (2, store_left_z)):
        store_left(left_ref, vector_ref, plane)
        hop(vector_ref, hop_ref, links_ref.at[d], 0, modes)
        real, imag = products(left_ref, hop_ref)
        store_table(table_ref.at[d - 1], fold_ref, real, imag, slots)
        tables.append(table_ref.at[d - 1])

    def emit(n, d, packed):
        out_ref[n, d] = packed.astype(BF16)

    pick_tiles(emit, owner_ref, [t[...].astype(BF16) for t in tables], chosen_ref, slots)


def outer_chunk(links_ref, upper_hbm, own_hbm, vector_ref, left_ref, hop_ref, sems):
    arriving = load_modes(upper_hbm, vector_ref, sems.at[2], 0)
    own = load_all(own_hbm, left_ref, sems)
    wait_all(arriving)
    hop(vector_ref, hop_ref, links_ref, 0, vector_ref.shape[0] // 2)
    wait_all(own)
    return products(left_ref, hop_ref)


def first_kernel(after_hbm, links_ref, upper_hbm, a, b, out_ref, *scratch):
    del after_hbm
    out_ref[...] = outer_chunk(links_ref, upper_hbm, (a, b), *scratch)


def last_kernel(
    slots,
    after_hbm,
    where_ref,
    owner_ref,
    first_ref,
    links_ref,
    upper_hbm,
    a,
    b,
    kept_ref,
    sent_ref,
    vector_ref,
    left_ref,
    hop_ref,
    sems,
    table_ref,
    fold_ref,
    chosen_ref,
    stage_ref,
):
    del after_hbm
    last = outer_chunk(links_ref, upper_hbm, (a, b), vector_ref, left_ref, hop_ref, sems)
    quarter = last.shape[1] // 2
    low = iota(last.shape, 1) < quarter
    first = first_ref[...]
    turned = pltpu.roll(first, quarter, 1)
    tile = [slice(k * LANES, (k + 1) * LANES) for k in range(3)]
    real = [first[:, tile[0]], jnp.where(low, first[:, tile[1]], pltpu.roll(last, quarter, 1))]
    imag = [turned[:, tile[2]], jnp.where(low, turned[:, tile[0]], last)]
    store_table(
        table_ref, fold_ref, jnp.concatenate(real, 1), jnp.concatenate(imag, 1), slots
    )
    half = kept_ref.shape[0]

    def emit(n, d, packed):
        away = n ^ where_ref[0]
        stage_ref[(away & 1) * half + (away >> 1)] = packed

    pick_tiles(emit, owner_ref, [table_ref[...].astype(BF16)], chosen_ref, slots)
    kept_ref[...] = stage_ref[:half]
    sent_ref[...] = stage_ref[half:].astype(sent_ref.dtype)


def halve_kernel(kept_in_ref, came_ref, kept_ref, sent_ref):
    for block in range(kept_ref.shape[0]):
        kept_ref[block] = kept_in_ref[2 * block] + came_ref[2 * block].astype(F32)
        other = kept_in_ref[2 * block + 1] + came_ref[2 * block + 1].astype(F32)
        sent_ref[block] = other.astype(sent_ref.dtype)


def total_kernel(in_ref, out_ref):
    total = in_ref[0].astype(F32)
    for device in range(1, in_ref.shape[0]):
        total = total + in_ref[device].astype(F32)
    out_ref[...] = total


def finish_kernel(normalise, slots, kept_ref, came_ref, inner_ref, out_ref):
    here = out_ref.shape[0]
    total = kept_ref[0] + came_ref[0].astype(F32)
    for d, value in enumerate((total, inner_ref[0], inner_ref[1])):
        value = value * normalise
        for group in range(slots.groups):
            first = group * slots.per_group
            count = min(slots.per_group, here - first)
            out_ref[first : first + count, d * slots.columns : (d + 1) * slots.columns] = value[
                :count, group * slots.columns : (group + 1) * slots.columns
            ]


def params(mib):
    return pltpu.CompilerParams(vmem_limit_bytes=mib * 1024 * 1024)


def cost(flops, moved):
    return pl.CostEstimate(flops=flops, bytes_accessed=moved, transcendentals=0)


def chunks_of(modes):
    quarter = modes // 4
    return ((0, 3 * quarter), (3 * quarter, quarter))


def per_device(eigvecs, link_seed, ownership):
    modes, _, _, layers, plane = eigvecs.shape
    assert layers == 1
    devices = lax.axis_size("sx")
    here = ownership.shape[0] // devices
    depth = 3 * plane
    tiles = plane // LANES
    slots = Slots(modes, here)
    vmem = pl.BlockSpec(memory_space=pltpu.VMEM)
    smem = pl.BlockSpec(memory_space=pltpu.SMEM)
    anywhere = pl.BlockSpec(memory_space=pl.ANY)

    raw = eigvecs.transpose(0, 2, 3, 1, 4).reshape(3 * modes, 2, plane)
    route = [(i, (i - 1) % devices) for i in range(devices)]
    chunks = chunks_of(modes)
    loaded = pl.pallas_call(
        functools.partial(load_kernel, [3 * first for first, _ in chunks]),
        name="load_modes",
        out_shape=[jax.ShapeDtypeStruct((3 * count, 2, plane), BF16) for _, count in chunks],
        in_specs=[anywhere],
        out_specs=[vmem] * len(chunks),
        scratch_shapes=[pltpu.SemaphoreType.DMA((len(chunks),))],
        compiler_params=params(50),
        cost_estimate=cost(0, 12 * modes * plane),
    )(raw)
    own, upper = [], []
    for part, (_, count) in zip(loaded, chunks):
        part = part.reshape(count, 3, 2, plane).transpose(1, 2, 0, 3)
        own.append(part)
        upper.append(lax.ppermute(part, "sx", route))

    where = lax.axis_index("sx").reshape(1).astype(jnp.int32)
    owners = slots.arrange(slots.codes(ownership).reshape(devices, here))
    flops = 4 * modes * modes * depth * 2
    wide = pltpu.VMEM((2 * modes, depth), BF16)
    table = (slots.LOW, slots.depth)
    fold_scratch = pltpu.VMEM((TM // 2, modes, LANES), F32)
    chosen_scratch = pltpu.VMEM((2, devices // 2 * slots.all_rows, slots.depth), BF16)

    sent_inner, links_x = pl.pallas_call(
        functools.partial(inner_kernel, slots),
        name="inner_directions",
        out_shape=(
            jax.ShapeDtypeStruct((devices, 2, slots.rows, LANES), BF16),
            jax.ShapeDtypeStruct((18, tiles, LANES), F32),
        ),
        in_specs=[smem, smem, vmem] + [anywhere] * 2,
        out_specs=(vmem, vmem),
        scratch_shapes=[
            wide,
            wide,
            wide,
            pltpu.VMEM((3, 18, tiles, LANES), F32),
            pltpu.VMEM((2,) + table, F32),
            fold_scratch,
            chosen_scratch,
            pltpu.SemaphoreType.DMA((2, 6)),
        ],
        compiler_params=params(40),
        cost_estimate=cost(6 * flops, 8 * 2**20),
    )(link_seed, where, owners, *own)
    received_inner = lax.all_to_all(sent_inner, "sx", 0, 0)
    total_inner = pl.pallas_call(
        total_kernel,
        name="sum_inner",
        out_shape=jax.ShapeDtypeStruct((2, slots.rows, LANES), F32),
        in_specs=[vmem],
        out_specs=vmem,
        compiler_params=params(8),
        cost_estimate=cost(2**20, 2**20),
    )(received_inner)

    sizes = [count for _, count in chunks]

    def outer_scratch(size):
        return [
            pltpu.VMEM((2 * size, depth), BF16),
            wide,
            pltpu.VMEM((2 * size, depth), BF16),
            pltpu.SemaphoreType.DMA((3, 6)),
        ]

    first_x = pl.pallas_call(
        first_kernel,
        name="outer_first",
        out_shape=jax.ShapeDtypeStruct((modes, 2 * sizes[0]), F32),
        in_specs=[anywhere, vmem] + [anywhere] * 3,
        out_specs=vmem,
        scratch_shapes=outer_scratch(sizes[0]),
        compiler_params=params(24),
        cost_estimate=cost(3 * flops, 8 * 2**20),
    )(sent_inner, links_x, upper[0], *own)

    block = (slots.rows, LANES)
    half = devices // 2
    kept, sent = pl.pallas_call(
        functools.partial(last_kernel, slots),
        name="outer_last",
        out_shape=(
            jax.ShapeDtypeStruct((half,) + block, F32),
            jax.ShapeDtypeStruct((half,) + block, BF16),
        ),
        in_specs=[anywhere, smem] + [vmem] * 3 + [anywhere] * 3,
        out_specs=(vmem, vmem),
        scratch_shapes=outer_scratch(sizes[1])
        + [
            pltpu.VMEM(table, F32),
            fold_scratch,
            chosen_scratch,
            pltpu.VMEM((devices,) + block, F32),
        ],
        compiler_params=params(24),
        cost_estimate=cost(2 * flops, 8 * 2**20),
    )(total_inner, where, owners, first_x, links_x, upper[1], *own)

    bit = 1
    while True:
        came = lax.ppermute(sent, "sx", [(i, i ^ bit) for i in range(devices)])
        bit, half = 2 * bit, half // 2
        if half == 0:
            break
        kept, sent = pl.pallas_call(
            halve_kernel,
            name="halve",
            out_shape=(
                jax.ShapeDtypeStruct((half,) + block, F32),
                jax.ShapeDtypeStruct((half,) + block, BF16 if bit == 2 else F32),
            ),
            in_specs=[vmem, vmem],
            out_specs=(vmem, vmem),
            compiler_params=params(8),
            cost_estimate=cost(2**20, 2**20),
        )(kept, came)
    assert bit == devices

    extent_x = layers * devices
    normalise = 1.0 / math.sqrt(12.0 * extent_x * plane)
    return pl.pallas_call(
        functools.partial(finish_kernel, normalise, slots),
        name="sum_far",
        out_shape=jax.ShapeDtypeStruct((here, 3 * slots.columns), F32),
        in_specs=[vmem] * 3,
        out_specs=vmem,
        compiler_params=params(8),
    )(kept, came, total_inner)


def solution(mesh):
    return jax.shard_map(
        per_device,
        mesh=mesh,
        in_specs=(P("cfg", None, None, "sx", None), P("cfg"), P()),
        out_specs=P(("cfg", "sx"), None),
        check_vma=False,
    )
```

```python
import functools
import math

import jax
import jax.numpy as jnp
from jax import lax
from jax.experimental import pallas as pl
from jax.experimental.pallas import tpu as pltpu
from jax.sharding import PartitionSpec as P

TM = 4
NZ = 64
LANES = 128
MODULUS = 46337
STEP = 32
F32 = jnp.float32
BF16 = jnp.bfloat16
NT = (((1,), (1,)), ((), ()))


def dot(left, right, dims=(((1,), (0,)), ((), ()))):
    return lax.dot_general(left, right, dims, preferred_element_type=F32)


def iota(shape, axis):
    return lax.broadcasted_iota(jnp.int32, shape, axis)


def round_up(value, step):
    return -(-value // step) * step


def divide(value):
    quotient = (value.astype(F32) * (1.0 / MODULUS)).astype(jnp.int32)
    rest = value - quotient * MODULUS
    below, above = rest < 0, rest >= MODULUS
    rest = jnp.where(below, rest + MODULUS, jnp.where(above, rest - MODULUS, rest))
    quotient = jnp.where(below, quotient - 1, jnp.where(above, quotient + 1, quotient))
    return quotient, rest


def link_angles(seed, site):
    high, low = divide(site)
    mixed = divide(seed * seed + low)[1]
    mixed = divide(mixed * mixed + high * 977 + 31)[1]
    angles = []
    for index in range(7):
        g = divide(mixed + (5171 * index + 1))[1]
        g = divide(g * g + low)[1]
        g = divide(g * g + 12345)[1]
        angles.append(g.astype(F32) * (2.0 * math.pi / MODULUS) - math.pi)
    return angles


def store_links(u_ref, seed, site):
    a = link_angles(seed, site)
    ca, sa = jnp.cos(a[0]), jnp.sin(a[0])
    cb, sb = jnp.cos(a[1]), jnp.sin(a[1])
    cg, sg = jnp.cos(a[2]), jnp.sin(a[2])
    rotation = [
        [ca * cb * cg - sa * sg, -ca * cb * sg - sa * cg, ca * sb],
        [sa * cb * cg + ca * sg, -sa * cb * sg + ca * cg, sa * sb],
        [-sb * cg, sb * sg, cb],
    ]
    left = [a[3], a[4], -a[3] - a[4]]
    right = [a[5], a[6], -a[5] - a[6]]
    for c in range(3):
        for s in range(3):
            phase = left[c] + right[s]
            u_ref[2 * (3 * c + s)] = rotation[c][s] * jnp.cos(phase)
            u_ref[2 * (3 * c + s) + 1] = rotation[c][s] * jnp.sin(phase)


def hop(vector_ref, out_ref, u_ref, first, count):
    all_modes, plane = vector_ref.shape[0] // 2, vector_ref.shape[1] // 3
    wide = (STEP // 8, 8, LANES)
    for t in range(plane // LANES):
        u = [jnp.broadcast_to(u_ref[k, t : t + 1, :], (8, LANES)) for k in range(18)]

        def body(block, carry, t=t, u=u):
            rows = [
                pl.ds(pl.multiple_of(part * all_modes + first + block * STEP, STEP), STEP)
                for part in range(2)
            ]
            lanes = [slice(c * plane + t * LANES, c * plane + (t + 1) * LANES) for c in range(3)]
            v = [
                [vector_ref[rows[part], lanes[c]].astype(F32).reshape(wide) for part in range(2)]
                for c in range(3)
            ]
            for c in range(3):
                real = imag = None
                for s in range(3):
                    ur, ui = u[2 * (3 * c + s)], u[2 * (3 * c + s) + 1]
                    re, im = v[s]
                    real = ur * re if real is None else real + ur * re
                    real = real - ui * im
                    imag = ur * im if imag is None else imag + ur * im
                    imag = imag + ui * re
                for part, value in ((0, real), (1, imag)):
                    out_ref[rows[part], lanes[c]] = value.reshape(STEP, LANES).astype(BF16)
            return carry

        lax.fori_loop(0, count // STEP, body, 0)


def products(left_ref, hop_ref):
    n, modes = left_ref.shape[0] // 2, hop_ref.shape[0] // 2
    by_real = dot(left_ref[:n, :], hop_ref[...], NT)
    by_imag = dot(left_ref[n:, :], hop_ref[...], NT)
    if modes % LANES:
        crossed = pltpu.roll(by_imag, modes, 1)
        low = iota(crossed.shape, 1) < modes
        return jnp.where(low, by_real + crossed, by_real - crossed)
    real = by_real[:, :modes] + by_imag[:, modes:]
    imag = by_real[:, modes:] - by_imag[:, :modes]
    return real, imag


class Slots:
    LOW = 2 * LANES

    def __init__(self, all_modes, slots):
        self.tiles = all_modes // TM
        assert 2 * self.tiles == LANES
        self.half = self.tiles // 2
        self.columns = 2 * TM * TM
        self.high = self.half * self.tiles // self.LOW
        assert self.high * self.columns == self.LOW
        self.depth = self.LOW + LANES
        self.groups = LANES // self.columns
        self.per_group = -(-slots // self.groups)
        self.rows = round_up(self.per_group, 8)
        self.all_rows = round_up(self.groups * self.rows, 16)
        assert self.all_rows == self.groups * self.rows

    def codes(self, pair):
        n = self.tiles

        def start(i):
            return i * n - (i * (i - 1)) // 2

        inside = ((2 * n + 1) ** 2 - 8 * pair).astype(F32)
        i = ((2 * n + 1 - jnp.sqrt(inside)) * 0.5).astype(jnp.int32)
        i = jnp.where(start(i) > pair, i - 1, i)
        i = jnp.where(start(i + 1) <= pair, i + 1, i)
        j = i + pair - start(i)
        first = i < self.half
        place = jnp.where(first, i * n + j, (n - 1 - i) * n + (n - 1 - j))
        corner = jnp.logical_and(jnp.logical_not(first), i == j)
        high = jnp.where(corner, 0, place // self.LOW)
        low = jnp.where(corner, self.LOW + (n - 1 - i), place % self.LOW)
        return high * 512 + low

    def arrange(self, codes):
        devices, slots = codes.shape
        spread = jnp.pad(
            codes, ((0, 0), (0, self.groups * self.per_group - slots)), constant_values=-1
        ).reshape(devices, self.groups, self.per_group)
        spread = jnp.pad(
            spread, ((0, 0), (0, 0), (0, self.rows - self.per_group)), constant_values=-1
        )
        return spread.reshape(devices, self.all_rows).T


def store_table(table_ref, fold_ref, real, imag, slots):
    all_modes = real.shape[0]
    n, half = slots.tiles, slots.half
    parts = [real - real.T, imag + imag.T]

    def choose(count, width, turned):
        row, column = iota((count, all_modes), 0), iota((count, all_modes), 1)
        r, i = row // width, row % width
        if turned:
            i = n - 1 - i
        return (column == i * TM + r).astype(F32).astype(BF16)

    pick = [choose(TM * half, half, turned) for turned in (False, True)]
    spread = [choose(all_modes, n, turned) for turned in (False, True)]
    row_i = iota((TM * half, all_modes), 0) % half
    lane_j = iota((TM * half, all_modes), 1) % n
    corners = []
    for part in range(2):
        entries = parts[part].astype(BF16)
        straight, turned = [
            dot(dot(pick[k], entries).astype(BF16), spread[k], NT) for k in range(2)
        ]
        folded = jnp.where(lane_j >= row_i, straight, turned)
        for k in range(TM // 2):
            fold_ref[k, part * TM * half : (part + 1) * TM * half, :] = folded[
                :, k * LANES : (k + 1) * LANES
            ]
        diagonal = jnp.where(lane_j == row_i, turned, 0.0)
        for r in range(TM):
            corners.append(
                jnp.sum(diagonal[r * half : (r + 1) * half], axis=0, keepdims=True)
            )
    low = iota((2 * TM, LANES), 1) < n

    def split(even, odd, high, lanes):
        for pair in range(TM // 2):
            e, o = even[pair], odd[pair]
            top = high * slots.columns + 2 * pair * 2 * TM
            table_ref[top : top + 2 * TM, lanes] = jnp.where(low, e, pltpu.roll(o, n, 1))
            table_ref[top + 2 * TM : top + 4 * TM, lanes] = jnp.where(
                low, pltpu.roll(e, n, 1), o
            )

    halves = [slice(k * LANES, (k + 1) * LANES) for k in range(TM // 2)]
    for two in range(half // 2):
        even = [fold_ref[k, pl.ds(2 * two, 2 * TM, stride=half), :] for k in range(TM // 2)]
        odd = [fold_ref[k, pl.ds(2 * two + 1, 2 * TM, stride=half), :] for k in range(TM // 2)]
        at = two * LANES % slots.LOW
        split(even, odd, two * LANES // slots.LOW, slice(at, at + LANES))
    corner = jnp.concatenate(corners, 0)
    nothing = jnp.zeros((2 * TM, LANES), F32)
    table_ref[:, slots.LOW :] = jnp.zeros((slots.LOW, LANES), F32)
    split([corner[:, h] for h in halves], [nothing] * len(halves), 0, slice(slots.LOW, slots.depth))


def pick_tiles(emit, owner_ref, tables, chosen_ref, slots):
    inside, column = iota((slots.LOW, LANES), 0) % slots.columns, iota((slots.LOW, LANES), 1)
    entry = (inside % (2 * TM)) * TM + inside // (2 * TM)
    fold = (column % slots.columns == entry).astype(F32).astype(BF16)
    rows = slots.all_rows
    lane16 = iota((16, LANES), 1)
    lanes = [
        (lane16 + t * LANES).astype(jnp.int16) for t in range(slots.depth // LANES)
    ]
    one, zero = jnp.ones((16, LANES), BF16), jnp.zeros((16, LANES), BF16)
    lane_group = iota((slots.rows, LANES), 1) // slots.columns
    high_group = iota((rows, LANES), 1) // slots.columns
    count = owner_ref.shape[1] // 2
    for half in range(2):
        high = []
        for k in range(count):
            n = half * count + k
            code = jnp.broadcast_to(owner_ref[:, n : n + 1], (rows, LANES))
            high.append(code >> 9)
            low = (code & 511).astype(jnp.int16)
            for top in range(0, rows, 16):
                for t in range(slots.depth // LANES):
                    chosen_ref[
                        half, k * rows + top : k * rows + top + 16, t * LANES : (t + 1) * LANES
                    ] = jnp.where(low[top : top + 16] == lanes[t], one, zero)
        for d, table in enumerate(tables):
            parts = dot(chosen_ref[half], table, NT)
            masked = jnp.concatenate(
                [
                    jnp.concatenate(
                        [
                            jnp.where(
                                high[k] == high_group + side * slots.groups,
                                parts[k * rows : (k + 1) * rows, side * LANES : (side + 1) * LANES],
                                0.0,
                            )
                            for side in range(2)
                        ],
                        1,
                    ).astype(BF16)
                    for k in range(count)
                ],
                0,
            )
            picked = dot(masked, fold)
            for k in range(count):
                top = k * rows
                packed = picked[top : top + slots.rows]
                for g in range(1, slots.groups):
                    piece = picked[top + g * slots.rows : top + (g + 1) * slots.rows]
                    packed = jnp.where(lane_group == g, piece, packed)
                emit(half * count + k, d, packed)


def store_all_links(links_ref, seed_ref, x):
    _, _, tiles, _ = links_ref.shape
    plane = tiles * LANES
    place = iota((tiles, LANES), 0) * LANES + iota((tiles, LANES), 1)
    before_y = jnp.where(place < NZ, place + (plane - NZ), place - NZ)
    before_z = jnp.where(place % NZ == 0, place + (NZ - 1), place - 1)
    for d, source in enumerate((place, before_y, before_z)):
        store_links(links_ref.at[d], seed_ref[d], source + x * plane)


def load_modes(planar_hbm, out_ref, sems, first):
    _, _, count, plane = planar_hbm.shape
    modes = out_ref.shape[0] // 2
    copies = [
        pltpu.make_async_copy(
            planar_hbm.at[c, part],
            out_ref.at[pl.ds(part * modes + first, count), pl.ds(c * plane, plane)],
            sems.at[2 * c + part],
        )
        for c in range(3)
        for part in range(2)
    ]
    for copy in copies:
        copy.start()
    return copies


def load_all(parts, out_ref, sems):
    quarter = out_ref.shape[0] // 8
    copies = []
    for k, (first, _) in enumerate(chunks_of(4 * quarter)):
        copies += load_modes(parts[k], out_ref, sems.at[k], first)
    return copies


def wait_all(copies):
    for copy in copies:
        copy.wait()


def store_left_y(out_ref, left_ref, plane):
    wide = 2 * LANES
    source, target = iota((wide, wide), 0), iota((wide, wide), 1)
    halves = source == (target // LANES) * LANES + (target + NZ) % LANES
    halves = halves.astype(F32).astype(BF16)
    low = iota((left_ref.shape[0], LANES), 1) < NZ
    for c in range(3):
        swapped = []
        for start in range(c * plane, (c + 1) * plane, wide):
            both = dot(left_ref[:, start : start + wide], halves)
            swapped += [both[:, :LANES], both[:, LANES:]]
        for t in range(plane // LANES):
            lanes = slice(c * plane + t * LANES, c * plane + (t + 1) * LANES)
            out_ref[:, lanes] = jnp.where(low, swapped[t - 1], swapped[t]).astype(BF16)


def store_left_z(out_ref, left_ref, plane):
    wide = 2 * LANES
    source, target = iota((wide, wide), 0), iota((wide, wide), 1)
    before = jnp.where(target % NZ == 0, target + (NZ - 1), target - 1)
    behind = (source == before).astype(F32).astype(BF16)
    for start in range(0, 3 * plane, wide):
        piece = dot(left_ref[:, start : start + wide], behind)
        out_ref[:, start : start + wide] = piece.astype(BF16)


def load_kernel(starts, whole_hbm, *refs):
    parts, sems = refs[:-1], refs[-1]
    copies = [
        pltpu.make_async_copy(whole_hbm.at[pl.ds(start, part.shape[0])], part, sems.at[k])
        for k, (start, part) in enumerate(zip(starts, parts))
    ]
    for copy in copies:
        copy.start()
    wait_all(copies)


def place_of(n, here, near, far):
    return lax.rem(n % near + near - lax.rem(here, near), near) * far + n // near


def inner_kernel(
    slots,
    grid,
    seed_ref,
    where_ref,
    owner_ref,
    first_hbm,
    last_hbm,
    out_ref,
    links_x_ref,
    vector_ref,
    left_ref,
    hop_ref,
    links_ref,
    table_ref,
    fold_ref,
    chosen_ref,
    sems,
):
    modes, plane = vector_ref.shape[0] // 2, vector_ref.shape[1] // 3
    copies = load_all((first_hbm, last_hbm), vector_ref, sems)
    store_all_links(links_ref, seed_ref, where_ref[0])
    links_x_ref[...] = links_ref[0]
    wait_all(copies)
    tables = []
    for d, store_left in ((1, store_left_y), (2, store_left_z)):
        store_left(left_ref, vector_ref, plane)
        hop(vector_ref, hop_ref, links_ref.at[d], 0, modes)
        real, imag = products(left_ref, hop_ref)
        store_table(table_ref.at[d - 1], fold_ref, real, imag, slots)
        tables.append(table_ref.at[d - 1])

    def emit(n, d, packed):
        out_ref[place_of(n, where_ref[0], *grid), d] = packed.astype(BF16)

    pick_tiles(emit, owner_ref, [t[...].astype(BF16) for t in tables], chosen_ref, slots)


def outer_chunk(links_ref, upper_hbm, own_hbm, vector_ref, left_ref, hop_ref, sems):
    arriving = load_modes(upper_hbm, vector_ref, sems.at[2], 0)
    own = load_all(own_hbm, left_ref, sems)
    wait_all(arriving)
    hop(vector_ref, hop_ref, links_ref, 0, vector_ref.shape[0] // 2)
    wait_all(own)
    return products(left_ref, hop_ref)


def first_kernel(links_ref, upper_hbm, a, b, out_ref, *scratch):
    out_ref[...] = outer_chunk(links_ref, upper_hbm, (a, b), *scratch)


def last_kernel(
    slots,
    grid,
    where_ref,
    owner_ref,
    inner_ref,
    first_ref,
    links_ref,
    upper_hbm,
    a,
    b,
    *refs,
):
    near, far = grid
    sent_hbm, refs = refs[:near], refs[near:]
    vector_ref, left_ref, hop_ref, sems, table_ref, fold_ref, chosen_ref, stage_ref, out_sems = refs
    stage_ref[:, 1:] = inner_ref[...]
    last = outer_chunk(links_ref, upper_hbm, (a, b), vector_ref, left_ref, hop_ref, sems)
    quarter = last.shape[1] // 2
    low = iota(last.shape, 1) < quarter
    first = first_ref[...]
    turned = pltpu.roll(first, quarter, 1)
    tile = [slice(k * LANES, (k + 1) * LANES) for k in range(3)]
    real = [first[:, tile[0]], jnp.where(low, first[:, tile[1]], pltpu.roll(last, quarter, 1))]
    imag = [turned[:, tile[2]], jnp.where(low, turned[:, tile[0]], last)]
    store_table(
        table_ref, fold_ref, jnp.concatenate(real, 1), jnp.concatenate(imag, 1), slots
    )

    def emit(n, d, packed):
        stage_ref[place_of(n, where_ref[0], near, far), 0] = packed.astype(BF16)

    pick_tiles(emit, owner_ref, [table_ref[...].astype(BF16)], chosen_ref, slots)
    leaving = [
        pltpu.make_async_copy(stage_ref.at[pl.ds(k * far, far)], sent_hbm[k], out_sems.at[k])
        for k in range(near)
    ]
    for copy in leaving:
        copy.start()
    wait_all(leaving)


def near_sum_kernel(where_ref, *refs):
    far = refs[0].shape[0]
    sources, outs = refs[:-far], refs[-far:]
    here = where_ref[0] // len(sources)
    for m in range(far):
        block = lax.rem(here + m, far)
        total = sources[0][block].astype(F32)
        for source in sources[1:]:
            total = total + source[block].astype(F32)
        outs[m][...] = total.astype(outs[m].dtype)


def finish_kernel(normalise, slots, *refs):
    sources, out_ref = refs[:-1], refs[-1]
    here = out_ref.shape[0]
    total = sources[0][...]
    for source in sources[1:]:
        total = total + source[...].astype(F32)
    for d in range(3):
        value = total[d]
        value = value * normalise
        for group in range(slots.groups):
            first = group * slots.per_group
            count = min(slots.per_group, here - first)
            out_ref[first : first + count, d * slots.columns : (d + 1) * slots.columns] = value[
                :count, group * slots.columns : (group + 1) * slots.columns
            ]


def params(mib):
    return pltpu.CompilerParams(vmem_limit_bytes=mib * 1024 * 1024)


def cost(flops, moved):
    return pl.CostEstimate(flops=flops, bytes_accessed=moved, transcendentals=0)


def chunks_of(modes):
    quarter = modes // 4
    return ((0, 3 * quarter), (3 * quarter, quarter))


def per_device(eigvecs, link_seed, ownership):
    modes, _, _, layers, plane = eigvecs.shape
    assert layers == 1
    devices = lax.axis_size("sx")
    here = ownership.shape[0] // devices
    depth = 3 * plane
    tiles = plane // LANES
    slots = Slots(modes, here)
    vmem = pl.BlockSpec(memory_space=pltpu.VMEM)
    smem = pl.BlockSpec(memory_space=pltpu.SMEM)
    anywhere = pl.BlockSpec(memory_space=pl.ANY)

    raw = eigvecs.transpose(0, 2, 3, 1, 4).reshape(3 * modes, 2, plane)
    route = [(i, (i - 1) % devices) for i in range(devices)]
    chunks = chunks_of(modes)
    loaded = pl.pallas_call(
        functools.partial(load_kernel, [3 * first for first, _ in chunks]),
        name="load_modes",
        out_shape=[jax.ShapeDtypeStruct((3 * count, 2, plane), BF16) for _, count in chunks],
        in_specs=[anywhere],
        out_specs=[vmem] * len(chunks),
        scratch_shapes=[pltpu.SemaphoreType.DMA((len(chunks),))],
        compiler_params=params(50),
        cost_estimate=cost(0, 12 * modes * plane),
    )(raw)
    own, upper = [], []
    for part, (_, count) in zip(loaded, chunks):
        part = part.reshape(count, 3, 2, plane).transpose(1, 2, 0, 3)
        own.append(part)
        upper.append(lax.ppermute(part, "sx", route))

    where = lax.axis_index("sx").reshape(1).astype(jnp.int32)
    owners = slots.arrange(slots.codes(ownership).reshape(devices, here))
    near = 1
    while near * near < devices:
        near *= 2
    far = devices // near
    assert near * far == devices
    flops = 4 * modes * modes * depth * 2
    wide = pltpu.VMEM((2 * modes, depth), BF16)
    table = (slots.LOW, slots.depth)
    fold_scratch = pltpu.VMEM((TM // 2, modes, LANES), F32)
    chosen_scratch = pltpu.VMEM((2, devices // 2 * slots.all_rows, slots.depth), BF16)

    block = (slots.rows, LANES)
    sent_inner, links_x = pl.pallas_call(
        functools.partial(inner_kernel, slots, (near, far)),
        name="inner_directions",
        out_shape=(
            jax.ShapeDtypeStruct((devices, 2) + block, BF16),
            jax.ShapeDtypeStruct((18, tiles, LANES), F32),
        ),
        in_specs=[smem, smem, vmem] + [anywhere] * 2,
        out_specs=(vmem, vmem),
        scratch_shapes=[
            wide,
            wide,
            wide,
            pltpu.VMEM((3, 18, tiles, LANES), F32),
            pltpu.VMEM((2,) + table, F32),
            fold_scratch,
            chosen_scratch,
            pltpu.SemaphoreType.DMA((2, 6)),
        ],
        compiler_params=params(40),
        cost_estimate=cost(6 * flops, 8 * 2**20),
    )(link_seed, where, owners, *own)
    sizes = [count for _, count in chunks]

    def outer_scratch(size):
        return [
            pltpu.VMEM((2 * size, depth), BF16),
            wide,
            pltpu.VMEM((2 * size, depth), BF16),
            pltpu.SemaphoreType.DMA((3, 6)),
        ]

    first_x = pl.pallas_call(
        first_kernel,
        name="outer_first",
        out_shape=jax.ShapeDtypeStruct((modes, 2 * sizes[0]), F32),
        in_specs=[vmem] + [anywhere] * 3,
        out_specs=vmem,
        scratch_shapes=outer_scratch(sizes[0]),
        compiler_params=params(24),
        cost_estimate=cost(2**20, 2**18),
    )(links_x, upper[0], *own)

    sent = pl.pallas_call(
        functools.partial(last_kernel, slots, (near, far)),
        name="outer_last",
        out_shape=[jax.ShapeDtypeStruct((far, 3) + block, BF16)] * near,
        in_specs=[smem] + [vmem] * 4 + [anywhere] * 3,
        out_specs=[anywhere] * near,
        scratch_shapes=outer_scratch(sizes[1])
        + [
            pltpu.VMEM(table, F32),
            fold_scratch,
            chosen_scratch,
            pltpu.VMEM((devices, 3) + block, BF16),
            pltpu.SemaphoreType.DMA((near,)),
        ],
        compiler_params=params(24),
        cost_estimate=cost(2**20, 2**18),
    )(where, owners, sent_inner, first_x, links_x, upper[1], *own)

    def onward(step, array, size, inner):
        def target(i):
            index = i // inner % size
            return i + ((index + step) % size - index) * inner

        return lax.ppermute(array, "sx", [(i, target(i)) for i in range(devices)])

    gathered = [sent[0]] + [onward(k, sent[k], near, 1) for k in range(1, near)]
    halfway = pl.pallas_call(
        near_sum_kernel,
        name="sum_near",
        out_shape=[
            jax.ShapeDtypeStruct((3,) + block, F32 if m == 0 else BF16) for m in range(far)
        ],
        in_specs=[smem] + [vmem] * near,
        out_specs=[vmem] * far,
        compiler_params=params(8),
        cost_estimate=cost(2**20, 2**20),
    )(where, *gathered)
    arrived = [halfway[0]] + [onward(m, halfway[m], far, near) for m in range(1, far)]

    extent_x = layers * devices
    normalise = 1.0 / math.sqrt(12.0 * extent_x * plane)
    return pl.pallas_call(
        functools.partial(finish_kernel, normalise, slots),
        name="sum_far",
        out_shape=jax.ShapeDtypeStruct((here, 3 * slots.columns), F32),
        in_specs=[vmem] * far,
        out_specs=vmem,
        compiler_params=params(8),
    )(*arrived)


def solution(mesh):
    return jax.shard_map(
        per_device,
        mesh=mesh,
        in_specs=(P("cfg", None, None, "sx", None), P("cfg"), P()),
        out_specs=P(("cfg", "sx"), None),
        check_vma=False,
    )
```

```python
import functools
import math

import jax
import jax.numpy as jnp
from jax import lax
from jax.experimental import pallas as pl
from jax.experimental.pallas import tpu as pltpu
from jax.sharding import PartitionSpec as P

TM = 4
NZ = 64
LANES = 128
MODULUS = 46337
STEP = 32
F32 = jnp.float32
BF16 = jnp.bfloat16
NT = (((1,), (1,)), ((), ()))


def dot(left, right, dims=(((1,), (0,)), ((), ()))):
    return lax.dot_general(left, right, dims, preferred_element_type=F32)


def iota(shape, axis):
    return lax.broadcasted_iota(jnp.int32, shape, axis)


def round_up(value, step):
    return -(-value // step) * step


def divide(value):
    quotient = (value.astype(F32) * (1.0 / MODULUS)).astype(jnp.int32)
    rest = value - quotient * MODULUS
    below, above = rest < 0, rest >= MODULUS
    rest = jnp.where(below, rest + MODULUS, jnp.where(above, rest - MODULUS, rest))
    quotient = jnp.where(below, quotient - 1, jnp.where(above, quotient + 1, quotient))
    return quotient, rest


def link_angles(seed, site):
    high, low = divide(site)
    mixed = divide(seed * seed + low)[1]
    mixed = divide(mixed * mixed + high * 977 + 31)[1]
    angles = []
    for index in range(7):
        g = divide(mixed + (5171 * index + 1))[1]
        g = divide(g * g + low)[1]
        g = divide(g * g + 12345)[1]
        angles.append(g.astype(F32) * (2.0 * math.pi / MODULUS) - math.pi)
    return angles


def store_links(u_ref, seed, site):
    a = link_angles(seed, site)
    ca, sa = jnp.cos(a[0]), jnp.sin(a[0])
    cb, sb = jnp.cos(a[1]), jnp.sin(a[1])
    cg, sg = jnp.cos(a[2]), jnp.sin(a[2])
    rotation = [
        [ca * cb * cg - sa * sg, -ca * cb * sg - sa * cg, ca * sb],
        [sa * cb * cg + ca * sg, -sa * cb * sg + ca * cg, sa * sb],
        [-sb * cg, sb * sg, cb],
    ]
    left = [a[3], a[4], -a[3] - a[4]]
    right = [a[5], a[6], -a[5] - a[6]]
    for c in range(3):
        for s in range(3):
            phase = left[c] + right[s]
            u_ref[2 * (3 * c + s)] = rotation[c][s] * jnp.cos(phase)
            u_ref[2 * (3 * c + s) + 1] = rotation[c][s] * jnp.sin(phase)


def hop(vector_ref, out_ref, u_ref, first, count):
    all_modes, plane = vector_ref.shape[0] // 2, vector_ref.shape[1] // 3
    wide = (STEP // 8, 8, LANES)
    for t in range(plane // LANES):
        u = [jnp.broadcast_to(u_ref[k, t : t + 1, :], (8, LANES)) for k in range(18)]

        def body(block, carry, t=t, u=u):
            rows = [
                pl.ds(pl.multiple_of(part * all_modes + first + block * STEP, STEP), STEP)
                for part in range(2)
            ]
            lanes = [slice(c * plane + t * LANES, c * plane + (t + 1) * LANES) for c in range(3)]
            v = [
                [vector_ref[rows[part], lanes[c]].astype(F32).reshape(wide) for part in range(2)]
                for c in range(3)
            ]
            for c in range(3):
                real = imag = None
                for s in range(3):
                    ur, ui = u[2 * (3 * c + s)], u[2 * (3 * c + s) + 1]
                    re, im = v[s]
                    real = ur * re if real is None else real + ur * re
                    real = real - ui * im
                    imag = ur * im if imag is None else imag + ur * im
                    imag = imag + ui * re
                for part, value in ((0, real), (1, imag)):
                    out_ref[rows[part], lanes[c]] = value.reshape(STEP, LANES).astype(BF16)
            return carry

        lax.fori_loop(0, count // STEP, body, 0)


def products(left_ref, hop_ref):
    n, modes = left_ref.shape[0] // 2, hop_ref.shape[0] // 2
    by_real = dot(left_ref[:n, :], hop_ref[...], NT)
    by_imag = dot(left_ref[n:, :], hop_ref[...], NT)
    if modes % LANES:
        crossed = pltpu.roll(by_imag, modes, 1)
        low = iota(crossed.shape, 1) < modes
        return jnp.where(low, by_real + crossed, by_real - crossed)
    real = by_real[:, :modes] + by_imag[:, modes:]
    imag = by_real[:, modes:] - by_imag[:, :modes]
    return real, imag


class Slots:
    LOW = 2 * LANES

    def __init__(self, all_modes, slots):
        self.tiles = all_modes // TM
        assert 2 * self.tiles == LANES
        self.half = self.tiles // 2
        self.columns = 2 * TM * TM
        self.high = self.half * self.tiles // self.LOW
        assert self.high * self.columns == self.LOW
        self.depth = self.LOW + LANES
        self.groups = LANES // self.columns
        self.per_group = -(-slots // self.groups)
        self.rows = round_up(self.per_group, 8)
        self.all_rows = round_up(self.groups * self.rows, 16)
        assert self.all_rows == self.groups * self.rows

    def codes(self, pair):
        n = self.tiles

        def start(i):
            return i * n - (i * (i - 1)) // 2

        inside = ((2 * n + 1) ** 2 - 8 * pair).astype(F32)
        i = ((2 * n + 1 - jnp.sqrt(inside)) * 0.5).astype(jnp.int32)
        i = jnp.where(start(i) > pair, i - 1, i)
        i = jnp.where(start(i + 1) <= pair, i + 1, i)
        j = i + pair - start(i)
        first = i < self.half
        place = jnp.where(first, i * n + j, (n - 1 - i) * n + (n - 1 - j))
        corner = jnp.logical_and(jnp.logical_not(first), i == j)
        high = jnp.where(corner, 0, place // self.LOW)
        low = jnp.where(corner, self.LOW + (n - 1 - i), place % self.LOW)
        return high * 512 + low

    def arrange(self, codes):
        devices, slots = codes.shape
        spread = jnp.pad(
            codes, ((0, 0), (0, self.groups * self.per_group - slots)), constant_values=-1
        ).reshape(devices, self.groups, self.per_group)
        spread = jnp.pad(
            spread, ((0, 0), (0, 0), (0, self.rows - self.per_group)), constant_values=-1
        )
        return spread.reshape(devices, self.all_rows).T


def store_table(table_ref, fold_ref, real, imag, slots):
    all_modes = real.shape[0]
    n, half = slots.tiles, slots.half
    parts = [real - real.T, imag + imag.T]

    def choose(count, width, turned):
        row, column = iota((count, all_modes), 0), iota((count, all_modes), 1)
        r, i = row // width, row % width
        if turned:
            i = n - 1 - i
        return (column == i * TM + r).astype(F32).astype(BF16)

    pick = [choose(TM * half, half, turned) for turned in (False, True)]
    spread = [choose(all_modes, n, turned) for turned in (False, True)]
    row_i = iota((TM * half, all_modes), 0) % half
    lane_j = iota((TM * half, all_modes), 1) % n
    corners = []
    for part in range(2):
        entries = parts[part].astype(BF16)
        straight, turned = [
            dot(dot(pick[k], entries).astype(BF16), spread[k], NT) for k in range(2)
        ]
        folded = jnp.where(lane_j >= row_i, straight, turned)
        for k in range(TM // 2):
            fold_ref[k, part * TM * half : (part + 1) * TM * half, :] = folded[
                :, k * LANES : (k + 1) * LANES
            ]
        diagonal = jnp.where(lane_j == row_i, turned, 0.0)
        for r in range(TM):
            corners.append(
                jnp.sum(diagonal[r * half : (r + 1) * half], axis=0, keepdims=True)
            )
    low = iota((2 * TM, LANES), 1) < n

    def split(even, odd, high, lanes):
        for pair in range(TM // 2):
            e, o = even[pair], odd[pair]
            top = high * slots.columns + 2 * pair * 2 * TM
            table_ref[top : top + 2 * TM, lanes] = jnp.where(low, e, pltpu.roll(o, n, 1))
            table_ref[top + 2 * TM : top + 4 * TM, lanes] = jnp.where(
                low, pltpu.roll(e, n, 1), o
            )

    halves = [slice(k * LANES, (k + 1) * LANES) for k in range(TM // 2)]
    for two in range(half // 2):
        even = [fold_ref[k, pl.ds(2 * two, 2 * TM, stride=half), :] for k in range(TM // 2)]
        odd = [fold_ref[k, pl.ds(2 * two + 1, 2 * TM, stride=half), :] for k in range(TM // 2)]
        at = two * LANES % slots.LOW
        split(even, odd, two * LANES // slots.LOW, slice(at, at + LANES))
    corner = jnp.concatenate(corners, 0)
    nothing = jnp.zeros((2 * TM, LANES), F32)
    table_ref[:, slots.LOW :] = jnp.zeros((slots.LOW, LANES), F32)
    split([corner[:, h] for h in halves], [nothing] * len(halves), 0, slice(slots.LOW, slots.depth))


def pick_tiles(emit, owner_ref, tables, chosen_ref, slots):
    inside, column = iota((slots.LOW, LANES), 0) % slots.columns, iota((slots.LOW, LANES), 1)
    entry = (inside % (2 * TM)) * TM + inside // (2 * TM)
    fold = (column % slots.columns == entry).astype(F32).astype(BF16)
    rows = slots.all_rows
    lane16 = iota((16, LANES), 1)
    lanes = [
        (lane16 + t * LANES).astype(jnp.int16) for t in range(slots.depth // LANES)
    ]
    one, zero = jnp.ones((16, LANES), BF16), jnp.zeros((16, LANES), BF16)
    lane_group = iota((slots.rows, LANES), 1) // slots.columns
    high_group = iota((rows, LANES), 1) // slots.columns
    count = owner_ref.shape[1] // 2
    for half in range(2):
        high = []
        for k in range(count):
            n = half * count + k
            code = jnp.broadcast_to(owner_ref[:, n : n + 1], (rows, LANES))
            high.append(code >> 9)
            low = (code & 511).astype(jnp.int16)
            for top in range(0, rows, 16):
                for t in range(slots.depth // LANES):
                    chosen_ref[
                        half, k * rows + top : k * rows + top + 16, t * LANES : (t + 1) * LANES
                    ] = jnp.where(low[top : top + 16] == lanes[t], one, zero)
        for d, table in enumerate(tables):
            parts = dot(chosen_ref[half], table, NT)
            masked = jnp.concatenate(
                [
                    jnp.concatenate(
                        [
                            jnp.where(
                                high[k] == high_group + side * slots.groups,
                                parts[k * rows : (k + 1) * rows, side * LANES : (side + 1) * LANES],
                                0.0,
                            )
                            for side in range(2)
                        ],
                        1,
                    ).astype(BF16)
                    for k in range(count)
                ],
                0,
            )
            picked = dot(masked, fold)
            for k in range(count):
                top = k * rows
                packed = picked[top : top + slots.rows]
                for g in range(1, slots.groups):
                    piece = picked[top + g * slots.rows : top + (g + 1) * slots.rows]
                    packed = jnp.where(lane_group == g, piece, packed)
                emit(half * count + k, d, packed)


def store_all_links(links_ref, seed_ref, x):
    _, _, tiles, _ = links_ref.shape
    plane = tiles * LANES
    place = iota((tiles, LANES), 0) * LANES + iota((tiles, LANES), 1)
    before_y = jnp.where(place < NZ, place + (plane - NZ), place - NZ)
    before_z = jnp.where(place % NZ == 0, place + (NZ - 1), place - 1)
    for d, source in enumerate((place, before_y, before_z)):
        store_links(links_ref.at[d], seed_ref[d], source + x * plane)


def load_modes(planar_hbm, out_ref, sems, first):
    _, _, count, plane = planar_hbm.shape
    modes = out_ref.shape[0] // 2
    copies = [
        pltpu.make_async_copy(
            planar_hbm.at[c, part],
            out_ref.at[pl.ds(part * modes + first, count), pl.ds(c * plane, plane)],
            sems.at[2 * c + part],
        )
        for c in range(3)
        for part in range(2)
    ]
    for copy in copies:
        copy.start()
    return copies


def load_all(parts, out_ref, sems):
    quarter = out_ref.shape[0] // 8
    copies = []
    for k, (first, _) in enumerate(chunks_of(4 * quarter)):
        copies += load_modes(parts[k], out_ref, sems.at[k], first)
    return copies


def wait_all(copies):
    for copy in copies:
        copy.wait()


def store_left_y(out_ref, left_ref, plane):
    wide = 2 * LANES
    source, target = iota((wide, wide), 0), iota((wide, wide), 1)
    halves = source == (target // LANES) * LANES + (target + NZ) % LANES
    halves = halves.astype(F32).astype(BF16)
    low = iota((left_ref.shape[0], LANES), 1) < NZ
    for c in range(3):
        swapped = []
        for start in range(c * plane, (c + 1) * plane, wide):
            both = dot(left_ref[:, start : start + wide], halves)
            swapped += [both[:, :LANES], both[:, LANES:]]
        for t in range(plane // LANES):
            lanes = slice(c * plane + t * LANES, c * plane + (t + 1) * LANES)
            out_ref[:, lanes] = jnp.where(low, swapped[t - 1], swapped[t]).astype(BF16)


def store_left_z(out_ref, left_ref, plane):
    wide = 2 * LANES
    source, target = iota((wide, wide), 0), iota((wide, wide), 1)
    before = jnp.where(target % NZ == 0, target + (NZ - 1), target - 1)
    behind = (source == before).astype(F32).astype(BF16)
    for start in range(0, 3 * plane, wide):
        piece = dot(left_ref[:, start : start + wide], behind)
        out_ref[:, start : start + wide] = piece.astype(BF16)


def load_kernel(starts, whole_hbm, *refs):
    parts, sems = refs[-1 - len(starts) : -1], refs[-1]
    copies = [
        pltpu.make_async_copy(whole_hbm.at[pl.ds(start, part.shape[0])], part, sems.at[k])
        for k, (start, part) in enumerate(zip(starts, parts))
    ]
    for copy in copies:
        copy.start()
    wait_all(copies)


def place_of(n, here, near, far):
    return lax.rem(n % near + near - lax.rem(here, near), near) * far + n // near


def inner_kernel(
    slots,
    grid,
    seed_ref,
    where_ref,
    owner_ref,
    a,
    b,
    c,
    *refs,
):
    near, far = grid
    sent, refs = refs[:near], refs[near:]
    links_x_ref, vector_ref, left_ref, hop_ref, links_ref, *refs = refs
    table_ref, fold_ref, chosen_ref, stage_ref, sems = refs
    modes, plane = vector_ref.shape[0] // 2, vector_ref.shape[1] // 3
    copies = load_all((a, b, c), vector_ref, sems)
    store_all_links(links_ref, seed_ref, where_ref[0])
    links_x_ref[...] = links_ref[0]
    wait_all(copies)
    tables = []
    for d, store_left in ((1, store_left_y), (2, store_left_z)):
        store_left(left_ref, vector_ref, plane)
        hop(vector_ref, hop_ref, links_ref.at[d], 0, modes)
        real, imag = products(left_ref, hop_ref)
        store_table(table_ref.at[d - 1], fold_ref, real, imag, slots)
        tables.append(table_ref.at[d - 1])

    def emit(n, d, packed):
        stage_ref[place_of(n, where_ref[0], near, far), d] = packed.astype(BF16)

    pick_tiles(emit, owner_ref, [t[...].astype(BF16) for t in tables], chosen_ref, slots)
    for k in range(near):
        sent[k][...] = stage_ref[k * far : (k + 1) * far]


def outer_chunk(links_ref, upper_hbm, own_hbm, vector_ref, left_ref, hop_ref, sems):
    arriving = load_modes(upper_hbm, vector_ref, sems.at[3], 0)
    own = load_all(own_hbm, left_ref, sems)
    wait_all(arriving)
    hop(vector_ref, hop_ref, links_ref, 0, vector_ref.shape[0] // 2)
    wait_all(own)
    return products(left_ref, hop_ref)


def wide_kernel(links_ref, upper_hbm, a, b, c, out_ref, *scratch):
    out_ref[0], out_ref[1] = outer_chunk(links_ref, upper_hbm, (a, b, c), *scratch)


def narrow_kernel(links_ref, upper_hbm, a, b, c, before_hbm, out_ref, *scratch):
    del before_hbm
    out_ref[...] = outer_chunk(links_ref, upper_hbm, (a, b, c), *scratch)


def last_kernel(
    slots,
    grid,
    where_ref,
    owner_ref,
    first_ref,
    second_ref,
    links_ref,
    upper_hbm,
    a,
    b,
    c,
    *refs,
):
    near, far = grid
    sent_hbm, refs = refs[:near], refs[near:]
    vector_ref, left_ref, hop_ref, sems, table_ref, fold_ref, chosen_ref, stage_ref, out_sems = refs
    last = outer_chunk(links_ref, upper_hbm, (a, b, c), vector_ref, left_ref, hop_ref, sems)
    quarter = last.shape[1] // 2
    low = iota(last.shape, 1) < quarter
    second = second_ref[...]
    real = [first_ref[0], jnp.where(low, second, pltpu.roll(last, quarter, 1))]
    imag = [first_ref[1], jnp.where(low, pltpu.roll(second, quarter, 1), last)]
    store_table(
        table_ref, fold_ref, jnp.concatenate(real, 1), jnp.concatenate(imag, 1), slots
    )

    def emit(n, d, packed):
        stage_ref[place_of(n, where_ref[0], near, far)] = packed.astype(BF16)

    pick_tiles(emit, owner_ref, [table_ref[...].astype(BF16)], chosen_ref, slots)
    leaving = [
        pltpu.make_async_copy(stage_ref.at[pl.ds(k * far, far)], sent_hbm[k], out_sems.at[k])
        for k in range(near)
    ]
    for copy in leaving:
        copy.start()
    wait_all(leaving)


def near_sum_kernel(where_ref, *refs):
    far = refs[0].shape[0]
    sources, outs = refs[:-far], refs[-far:]
    near = len(sources) // 2
    here = where_ref[0] // near

    def total(arrays, block):
        value = arrays[0][block].astype(F32)
        for array in arrays[1:]:
            value = value + array[block].astype(F32)
        return value

    for m in range(far):
        block = lax.rem(here + m, far)
        outs[m][0] = total(sources[:near], block).astype(outs[m].dtype)
        outs[m][1:] = total(sources[near:], block).astype(outs[m].dtype)


def finish_kernel(normalise, slots, *refs):
    sources, out_ref = refs[:-1], refs[-1]
    here = out_ref.shape[0]
    total = sources[0][...]
    for source in sources[1:]:
        total = total + source[...].astype(F32)
    for d in range(3):
        value = total[d]
        value = value * normalise
        for group in range(slots.groups):
            first = group * slots.per_group
            count = min(slots.per_group, here - first)
            out_ref[first : first + count, d * slots.columns : (d + 1) * slots.columns] = value[
                :count, group * slots.columns : (group + 1) * slots.columns
            ]


def params(mib):
    return pltpu.CompilerParams(vmem_limit_bytes=mib * 1024 * 1024)


def cost(flops, moved):
    return pl.CostEstimate(flops=flops, bytes_accessed=moved, transcendentals=0)


def chunks_of(modes):
    quarter = modes // 4
    return ((0, 2 * quarter), (2 * quarter, quarter), (3 * quarter, quarter))


def per_device(eigvecs, link_seed, ownership):
    modes, _, _, layers, plane = eigvecs.shape
    assert layers == 1
    devices = lax.axis_size("sx")
    here = ownership.shape[0] // devices
    depth = 3 * plane
    tiles = plane // LANES
    slots = Slots(modes, here)
    vmem = pl.BlockSpec(memory_space=pltpu.VMEM)
    smem = pl.BlockSpec(memory_space=pltpu.SMEM)
    anywhere = pl.BlockSpec(memory_space=pl.ANY)

    raw = eigvecs.transpose(0, 2, 3, 1, 4).reshape(3 * modes, 2, plane)
    route = [(i, (i - 1) % devices) for i in range(devices)]
    chunks = chunks_of(modes)
    own, upper = [], []
    for some, room in ((chunks[:1], 52), (chunks[1:], 50)):
        loaded = pl.pallas_call(
            functools.partial(load_kernel, [3 * first for first, _ in some]),
            name="load_modes",
            out_shape=[jax.ShapeDtypeStruct((3 * count, 2, plane), BF16) for _, count in some],
            in_specs=[anywhere] * (1 + len(own[-1:])),
            out_specs=[vmem] * len(some),
            scratch_shapes=[pltpu.SemaphoreType.DMA((len(some),))],
            compiler_params=params(room),
            cost_estimate=cost(0, 12 * modes * plane),
        )(raw, *own[-1:])
        for part, (_, count) in zip(loaded, some):
            part = part.reshape(count, 3, 2, plane).transpose(1, 2, 0, 3)
            own.append(part)
            upper.append(lax.ppermute(part, "sx", route))

    where = lax.axis_index("sx").reshape(1).astype(jnp.int32)
    owners = slots.arrange(slots.codes(ownership).reshape(devices, here))
    near = 1
    while near * near < devices:
        near *= 2
    far = devices // near
    assert near * far == devices
    flops = 4 * modes * modes * depth * 2
    wide = pltpu.VMEM((2 * modes, depth), BF16)
    table = (slots.LOW, slots.depth)
    fold_scratch = pltpu.VMEM((TM // 2, modes, LANES), F32)
    chosen_scratch = pltpu.VMEM((2, devices // 2 * slots.all_rows, slots.depth), BF16)

    block = (slots.rows, LANES)
    *sent_inner, links_x = pl.pallas_call(
        functools.partial(inner_kernel, slots, (near, far)),
        name="inner_directions",
        out_shape=[jax.ShapeDtypeStruct((far, 2) + block, BF16)] * near
        + [jax.ShapeDtypeStruct((18, tiles, LANES), F32)],
        in_specs=[smem, smem, vmem] + [anywhere] * 3,
        out_specs=[vmem] * (near + 1),
        scratch_shapes=[
            wide,
            wide,
            wide,
            pltpu.VMEM((3, 18, tiles, LANES), F32),
            pltpu.VMEM((2,) + table, F32),
            fold_scratch,
            chosen_scratch,
            pltpu.VMEM((devices, 2) + block, BF16),
            pltpu.SemaphoreType.DMA((3, 6)),
        ],
        compiler_params=params(40),
        cost_estimate=cost(6 * flops, 8 * 2**20),
    )(link_seed, where, owners, *own)
    sizes = [count for _, count in chunks]

    def outer_scratch(size):
        return [
            pltpu.VMEM((2 * size, depth), BF16),
            wide,
            pltpu.VMEM((2 * size, depth), BF16),
            pltpu.SemaphoreType.DMA((4, 6)),
        ]

    def outer(kernel, name, which, shape, before):
        return pl.pallas_call(
            kernel,
            name=name,
            out_shape=jax.ShapeDtypeStruct(shape, F32),
            in_specs=[vmem] + [anywhere] * (4 + len(before)),
            out_specs=vmem,
            scratch_shapes=outer_scratch(sizes[which]),
            compiler_params=params(24),
            cost_estimate=cost(2**20, 2**18),
        )(links_x, upper[which], *own, *before)

    first_x = outer(wide_kernel, "outer_first", 0, (2, modes, sizes[0]), [])
    second_x = outer(narrow_kernel, "outer_second", 1, (modes, 2 * sizes[1]), [first_x])
    sent = pl.pallas_call(
        functools.partial(last_kernel, slots, (near, far)),
        name="outer_last",
        out_shape=[jax.ShapeDtypeStruct((far,) + block, BF16)] * near,
        in_specs=[smem] + [vmem] * 4 + [anywhere] * 4,
        out_specs=[anywhere] * near,
        scratch_shapes=outer_scratch(sizes[2])
        + [
            pltpu.VMEM(table, F32),
            fold_scratch,
            chosen_scratch,
            pltpu.VMEM((devices,) + block, BF16),
            pltpu.SemaphoreType.DMA((near,)),
        ],
        compiler_params=params(24),
        cost_estimate=cost(2**20, 2**18),
    )(where, owners, first_x, second_x, links_x, upper[2], *own)

    def onward(step, array, size, inner):
        def target(i):
            index = i // inner % size
            return i + ((index + step) % size - index) * inner

        return lax.ppermute(array, "sx", [(i, target(i)) for i in range(devices)])

    gathered = [
        array if k == 0 else onward(k, array, near, 1)
        for arrays in (sent, sent_inner)
        for k, array in enumerate(arrays)
    ]
    halfway = pl.pallas_call(
        near_sum_kernel,
        name="sum_near",
        out_shape=[
            jax.ShapeDtypeStruct((3,) + block, F32 if m == 0 else BF16) for m in range(far)
        ],
        in_specs=[smem] + [vmem] * (2 * near),
        out_specs=[vmem] * far,
        compiler_params=params(8),
        cost_estimate=cost(2**20, 2**20),
    )(where, *gathered)
    arrived = [halfway[0]] + [onward(m, halfway[m], far, near) for m in range(1, far)]

    extent_x = layers * devices
    normalise = 1.0 / math.sqrt(12.0 * extent_x * plane)
    return pl.pallas_call(
        functools.partial(finish_kernel, normalise, slots),
        name="sum_far",
        out_shape=jax.ShapeDtypeStruct((here, 3 * slots.columns), F32),
        in_specs=[vmem] * far,
        out_specs=vmem,
        compiler_params=params(8),
    )(*arrived)


def solution(mesh):
    return jax.shard_map(
        per_device,
        mesh=mesh,
        in_specs=(P("cfg", None, None, "sx", None), P("cfg"), P()),
        out_specs=P(("cfg", "sx"), None),
        check_vma=False,
    )
```

```python
import functools
import math

import jax
import jax.numpy as jnp
from jax import lax
from jax.experimental import pallas as pl
from jax.experimental.pallas import tpu as pltpu
from jax.sharding import PartitionSpec as P

TM = 4
NZ = 64
LANES = 128
MODULUS = 46337
STEP = 32
PIECES = 4
F32 = jnp.float32
BF16 = jnp.bfloat16
NT = (((1,), (1,)), ((), ()))


def dot(left, right, dims=(((1,), (0,)), ((), ()))):
    return lax.dot_general(left, right, dims, preferred_element_type=F32)


def iota(shape, axis):
    return lax.broadcasted_iota(jnp.int32, shape, axis)


def round_up(value, step):
    return -(-value // step) * step


def divide(value):
    quotient = (value.astype(F32) * (1.0 / MODULUS)).astype(jnp.int32)
    rest = value - quotient * MODULUS
    below, above = rest < 0, rest >= MODULUS
    rest = jnp.where(below, rest + MODULUS, jnp.where(above, rest - MODULUS, rest))
    quotient = jnp.where(below, quotient - 1, jnp.where(above, quotient + 1, quotient))
    return quotient, rest


def link_angles(seed, site):
    high, low = divide(site)
    mixed = divide(seed * seed + low)[1]
    mixed = divide(mixed * mixed + high * 977 + 31)[1]
    angles = []
    for index in range(7):
        g = divide(mixed + (5171 * index + 1))[1]
        g = divide(g * g + low)[1]
        g = divide(g * g + 12345)[1]
        angles.append(g.astype(F32) * (2.0 * math.pi / MODULUS) - math.pi)
    return angles


def store_links(u_ref, seed, site):
    a = link_angles(seed, site)
    ca, sa = jnp.cos(a[0]), jnp.sin(a[0])
    cb, sb = jnp.cos(a[1]), jnp.sin(a[1])
    cg, sg = jnp.cos(a[2]), jnp.sin(a[2])
    rotation = [
        [ca * cb * cg - sa * sg, -ca * cb * sg - sa * cg, ca * sb],
        [sa * cb * cg + ca * sg, -sa * cb * sg + ca * cg, sa * sb],
        [-sb * cg, sb * sg, cb],
    ]
    def phases(first, second):
        c1, s1, c2, s2 = jnp.cos(first), jnp.sin(first), jnp.cos(second), jnp.sin(second)
        return [(c1, s1), (c2, s2), (c1 * c2 - s1 * s2, -(s1 * c2 + c1 * s2))]

    left, right = phases(a[3], a[4]), phases(a[5], a[6])
    for c in range(3):
        for s in range(3):
            (cl, sl), (cr, sr) = left[c], right[s]
            u_ref[2 * (3 * c + s)] = rotation[c][s] * (cl * cr - sl * sr)
            u_ref[2 * (3 * c + s) + 1] = rotation[c][s] * (sl * cr + cl * sr)


def hop(vector_ref, out_ref, u_ref, first, count):
    all_modes, plane = vector_ref.shape[0] // 2, vector_ref.shape[1] // 3
    wide = (STEP // 8, 8, LANES)
    for t in range(plane // LANES):
        u = [jnp.broadcast_to(u_ref[k, t : t + 1, :], (8, LANES)) for k in range(18)]

        def body(block, carry, t=t, u=u):
            rows = [
                pl.ds(pl.multiple_of(part * all_modes + first + block * STEP, STEP), STEP)
                for part in range(2)
            ]
            lanes = [slice(c * plane + t * LANES, c * plane + (t + 1) * LANES) for c in range(3)]
            v = [
                [vector_ref[rows[part], lanes[c]].astype(F32).reshape(wide) for part in range(2)]
                for c in range(3)
            ]
            for c in range(3):
                real = imag = None
                for s in range(3):
                    ur, ui = u[2 * (3 * c + s)], u[2 * (3 * c + s) + 1]
                    re, im = v[s]
                    real = ur * re if real is None else real + ur * re
                    real = real - ui * im
                    imag = ur * im if imag is None else imag + ur * im
                    imag = imag + ui * re
                for part, value in ((0, real), (1, imag)):
                    out_ref[rows[part], lanes[c]] = value.reshape(STEP, LANES).astype(BF16)
            return carry

        lax.fori_loop(0, count // STEP, body, 0)


def products(left_ref, hop_ref):
    n, modes = left_ref.shape[0] // 2, hop_ref.shape[0] // 2
    by_real = dot(left_ref[:n, :], hop_ref[...], NT)
    by_imag = dot(left_ref[n:, :], hop_ref[...], NT)
    if modes % LANES:
        crossed = pltpu.roll(by_imag, modes, 1)
        low = iota(crossed.shape, 1) < modes
        return jnp.where(low, by_real + crossed, by_real - crossed)
    real = by_real[:, :modes] + by_imag[:, modes:]
    imag = by_real[:, modes:] - by_imag[:, :modes]
    return real, imag


class Slots:
    LOW = 2 * LANES

    def __init__(self, all_modes, slots):
        self.tiles = all_modes // TM
        assert 2 * self.tiles == LANES
        self.half = self.tiles // 2
        self.columns = 2 * TM * TM
        self.high = self.half * self.tiles // self.LOW
        assert self.high * self.columns == self.LOW
        self.depth = self.LOW + LANES
        self.groups = LANES // self.columns
        self.per_group = -(-slots // self.groups)
        self.rows = round_up(self.per_group, 8)
        self.all_rows = round_up(self.groups * self.rows, 16)
        assert self.all_rows == self.groups * self.rows

    def codes(self, pair):
        n = self.tiles

        def start(i):
            return i * n - (i * (i - 1)) // 2

        inside = ((2 * n + 1) ** 2 - 8 * pair).astype(F32)
        i = ((2 * n + 1 - jnp.sqrt(inside)) * 0.5).astype(jnp.int32)
        i = jnp.where(start(i) > pair, i - 1, i)
        i = jnp.where(start(i + 1) <= pair, i + 1, i)
        j = i + pair - start(i)
        first = i < self.half
        place = jnp.where(first, i * n + j, (n - 1 - i) * n + (n - 1 - j))
        corner = jnp.logical_and(jnp.logical_not(first), i == j)
        high = jnp.where(corner, 0, place // self.LOW)
        low = jnp.where(corner, self.LOW + (n - 1 - i), place % self.LOW)
        return high * 512 + low

    def arrange(self, codes):
        devices, slots = codes.shape
        spread = jnp.pad(
            codes, ((0, 0), (0, self.groups * self.per_group - slots)), constant_values=-1
        ).reshape(devices, self.groups, self.per_group)
        spread = jnp.pad(
            spread, ((0, 0), (0, 0), (0, self.rows - self.per_group)), constant_values=-1
        )
        return spread.reshape(devices, self.all_rows).T


def store_table(table_ref, fold_ref, real, imag, slots):
    all_modes = real.shape[0]
    n, half = slots.tiles, slots.half
    parts = [real - real.T, imag + imag.T]

    def choose(count, width, turned):
        row, column = iota((count, all_modes), 0), iota((count, all_modes), 1)
        r, i = row // width, row % width
        if turned:
            i = n - 1 - i
        return (column == i * TM + r).astype(F32).astype(BF16)

    pick = [choose(TM * half, half, turned) for turned in (False, True)]
    spread = [choose(all_modes, n, turned) for turned in (False, True)]
    row_i = iota((TM * half, all_modes), 0) % half
    lane_j = iota((TM * half, all_modes), 1) % n
    corners = []
    for part in range(2):
        entries = parts[part].astype(BF16)
        straight, turned = [
            dot(dot(pick[k], entries).astype(BF16), spread[k], NT) for k in range(2)
        ]
        folded = jnp.where(lane_j >= row_i, straight, turned)
        for k in range(TM // 2):
            fold_ref[k, part * TM * half : (part + 1) * TM * half, :] = folded[
                :, k * LANES : (k + 1) * LANES
            ]
        diagonal = jnp.where(lane_j == row_i, turned, 0.0)
        for r in range(TM):
            corners.append(
                jnp.sum(diagonal[r * half : (r + 1) * half], axis=0, keepdims=True)
            )
    low = iota((2 * TM, LANES), 1) < n

    def split(even, odd, high, lanes):
        for pair in range(TM // 2):
            e, o = even[pair], odd[pair]
            top = high * slots.columns + 2 * pair * 2 * TM
            table_ref[top : top + 2 * TM, lanes] = jnp.where(low, e, pltpu.roll(o, n, 1))
            table_ref[top + 2 * TM : top + 4 * TM, lanes] = jnp.where(
                low, pltpu.roll(e, n, 1), o
            )

    halves = [slice(k * LANES, (k + 1) * LANES) for k in range(TM // 2)]
    for two in range(half // 2):
        even = [fold_ref[k, pl.ds(2 * two, 2 * TM, stride=half), :] for k in range(TM // 2)]
        odd = [fold_ref[k, pl.ds(2 * two + 1, 2 * TM, stride=half), :] for k in range(TM // 2)]
        at = two * LANES % slots.LOW
        split(even, odd, two * LANES // slots.LOW, slice(at, at + LANES))
    corner = jnp.concatenate(corners, 0)
    nothing = jnp.zeros((2 * TM, LANES), F32)
    table_ref[:, slots.LOW :] = jnp.zeros((slots.LOW, LANES), F32)
    split([corner[:, h] for h in halves], [nothing] * len(halves), 0, slice(slots.LOW, slots.depth))


def pick_tiles(emit, owner_ref, tables, chosen_ref, slots):
    inside, column = iota((slots.LOW, LANES), 0) % slots.columns, iota((slots.LOW, LANES), 1)
    entry = (inside % (2 * TM)) * TM + inside // (2 * TM)
    fold = (column % slots.columns == entry).astype(F32).astype(BF16)
    rows = slots.all_rows
    lane16 = iota((16, LANES), 1)
    lanes = [
        (lane16 + t * LANES).astype(jnp.int16) for t in range(slots.depth // LANES)
    ]
    one, zero = jnp.ones((16, LANES), BF16), jnp.zeros((16, LANES), BF16)
    lane_group = iota((slots.rows, LANES), 1) // slots.columns
    high_group = iota((rows, LANES), 1) // slots.columns
    count = owner_ref.shape[1] // 2
    for half in range(2):
        high = []
        for k in range(count):
            n = half * count + k
            code = jnp.broadcast_to(owner_ref[:, n : n + 1], (rows, LANES))
            high.append(code >> 9)
            low = (code & 511).astype(jnp.int16)
            for top in range(0, rows, 16):
                for t in range(slots.depth // LANES):
                    chosen_ref[
                        half, k * rows + top : k * rows + top + 16, t * LANES : (t + 1) * LANES
                    ] = jnp.where(low[top : top + 16] == lanes[t], one, zero)
        for d, table in enumerate(tables):
            parts = dot(chosen_ref[half], table, NT)
            masked = jnp.concatenate(
                [
                    jnp.concatenate(
                        [
                            jnp.where(
                                high[k] == high_group + side * slots.groups,
                                parts[k * rows : (k + 1) * rows, side * LANES : (side + 1) * LANES],
                                0.0,
                            )
                            for side in range(2)
                        ],
                        1,
                    ).astype(BF16)
                    for k in range(count)
                ],
                0,
            )
            picked = dot(masked, fold)
            for k in range(count):
                top = k * rows
                packed = picked[top : top + slots.rows]
                for g in range(1, slots.groups):
                    piece = picked[top + g * slots.rows : top + (g + 1) * slots.rows]
                    packed = jnp.where(lane_group == g, piece, packed)
                emit(half * count + k, d, packed)


def store_all_links(links_ref, seed_ref, x):
    _, _, tiles, _ = links_ref.shape
    plane = tiles * LANES
    place = iota((tiles, LANES), 0) * LANES + iota((tiles, LANES), 1)
    before_y = jnp.where(place < NZ, place + (plane - NZ), place - NZ)
    before_z = jnp.where(place % NZ == 0, place + (NZ - 1), place - 1)
    for d, source in enumerate((place, before_y, before_z)):
        store_links(links_ref.at[d], seed_ref[d], source + x * plane)


def load_modes(planar_hbm, out_ref, sems, first):
    _, _, count, plane = planar_hbm.shape
    modes = out_ref.shape[0] // 2
    copies = [
        pltpu.make_async_copy(
            planar_hbm.at[c, part],
            out_ref.at[pl.ds(part * modes + first, count), pl.ds(c * plane, plane)],
            sems.at[2 * c + part],
        )
        for c in range(3)
        for part in range(2)
    ]
    for copy in copies:
        copy.start()
    return copies


def load_all(parts, out_ref, sems):
    quarter = out_ref.shape[0] // 8
    copies = []
    for k, (first, _) in enumerate(chunks_of(4 * quarter)):
        copies += load_modes(parts[k], out_ref, sems.at[k], first)
    return copies


def wait_all(copies):
    for copy in copies:
        copy.wait()


def store_left_y(out_ref, left_ref, plane):
    wide = 2 * LANES
    source, target = iota((wide, wide), 0), iota((wide, wide), 1)
    halves = source == (target // LANES) * LANES + (target + NZ) % LANES
    halves = halves.astype(F32).astype(BF16)
    low = iota((left_ref.shape[0], LANES), 1) < NZ
    for c in range(3):
        swapped = []
        for start in range(c * plane, (c + 1) * plane, wide):
            both = dot(left_ref[:, start : start + wide], halves)
            swapped += [both[:, :LANES], both[:, LANES:]]
        for t in range(plane // LANES):
            lanes = slice(c * plane + t * LANES, c * plane + (t + 1) * LANES)
            out_ref[:, lanes] = jnp.where(low, swapped[t - 1], swapped[t]).astype(BF16)


def store_left_z(out_ref, left_ref, plane):
    wide = 2 * LANES
    source, target = iota((wide, wide), 0), iota((wide, wide), 1)
    before = jnp.where(target % NZ == 0, target + (NZ - 1), target - 1)
    behind = (source == before).astype(F32).astype(BF16)
    for start in range(0, 3 * plane, wide):
        piece = dot(left_ref[:, start : start + wide], behind)
        out_ref[:, start : start + wide] = piece.astype(BF16)


def load_kernel(starts, whole_hbm, *refs):
    parts, sems = refs[-1 - len(starts) : -1], refs[-1]
    copies = []
    for k, (start, part) in enumerate(zip(starts, parts)):
        count = part.shape[0] // PIECES
        for piece in range(PIECES):
            copies.append(
                pltpu.make_async_copy(
                    whole_hbm.at[pl.ds(start + piece * count, count)],
                    part.at[pl.ds(piece * count, count)],
                    sems.at[k, piece],
                )
            )
    for copy in copies:
        copy.start()
    wait_all(copies)


def place_of(n, here, near, far):
    return lax.rem(n % near + near - lax.rem(here, near), near) * far + n // near


def inner_kernel(
    slots,
    grid,
    seed_ref,
    where_ref,
    owner_ref,
    a,
    b,
    c,
    *refs,
):
    near, far = grid
    sent, refs = refs[:near], refs[near:]
    links_x_ref, own_hbm, vector_ref, left_ref, hop_ref, links_ref, *refs = refs
    table_ref, fold_ref, chosen_ref, stage_ref, sems, own_sem = refs
    modes, plane = vector_ref.shape[0] // 2, vector_ref.shape[1] // 3
    copies = load_all((a, b, c), vector_ref, sems)
    store_all_links(links_ref, seed_ref, where_ref[0])
    links_x_ref[...] = links_ref[0]
    wait_all(copies)
    own = pltpu.make_async_copy(vector_ref, own_hbm, own_sem)
    own.start()
    tables = []
    for d, store_left in ((1, store_left_y), (2, store_left_z)):
        store_left(left_ref, vector_ref, plane)
        hop(vector_ref, hop_ref, links_ref.at[d], 0, modes)
        real, imag = products(left_ref, hop_ref)
        store_table(table_ref.at[d - 1], fold_ref, real, imag, slots)
        tables.append(table_ref.at[d - 1])

    def emit(n, d, packed):
        stage_ref[place_of(n, where_ref[0], near, far), d] = packed.astype(BF16)

    pick_tiles(emit, owner_ref, [t[...].astype(BF16) for t in tables], chosen_ref, slots)
    for k in range(near):
        sent[k][...] = stage_ref[k * far : (k + 1) * far]
    own.wait()


def outer_chunk(links_ref, upper_hbm, own_hbm, vector_ref, left_ref, hop_ref, sems):
    arriving = load_modes(upper_hbm, vector_ref, sems.at[0], 0)
    count = left_ref.shape[0] // PIECES
    own = [
        pltpu.make_async_copy(
            own_hbm.at[pl.ds(piece * count, count)],
            left_ref.at[pl.ds(piece * count, count)],
            sems.at[1, piece],
        )
        for piece in range(PIECES)
    ]
    for copy in own:
        copy.start()
    wait_all(arriving)
    hop(vector_ref, hop_ref, links_ref, 0, vector_ref.shape[0] // 2)
    wait_all(own)
    return products(left_ref, hop_ref)


def wide_kernel(links_ref, upper_hbm, own_hbm, out_ref, *scratch):
    out_ref[0], out_ref[1] = outer_chunk(links_ref, upper_hbm, own_hbm, *scratch)


def narrow_kernel(links_ref, upper_hbm, own_hbm, before_hbm, out_ref, *scratch):
    del before_hbm
    out_ref[...] = outer_chunk(links_ref, upper_hbm, own_hbm, *scratch)


def last_kernel(
    slots,
    grid,
    where_ref,
    owner_ref,
    first_ref,
    second_ref,
    links_ref,
    upper_hbm,
    own_hbm,
    *refs,
):
    near, far = grid
    sent_hbm, refs = refs[:near], refs[near:]
    vector_ref, left_ref, hop_ref, sems, table_ref, fold_ref, chosen_ref, stage_ref, out_sems = refs
    last = outer_chunk(links_ref, upper_hbm, own_hbm, vector_ref, left_ref, hop_ref, sems)
    quarter = last.shape[1] // 2
    low = iota(last.shape, 1) < quarter
    second = second_ref[...]
    real = [first_ref[0], jnp.where(low, second, pltpu.roll(last, quarter, 1))]
    imag = [first_ref[1], jnp.where(low, pltpu.roll(second, quarter, 1), last)]
    store_table(
        table_ref, fold_ref, jnp.concatenate(real, 1), jnp.concatenate(imag, 1), slots
    )

    def emit(n, d, packed):
        stage_ref[place_of(n, where_ref[0], near, far)] = packed.astype(BF16)

    pick_tiles(emit, owner_ref, [table_ref[...].astype(BF16)], chosen_ref, slots)
    leaving = [
        pltpu.make_async_copy(stage_ref.at[pl.ds(k * far, far)], sent_hbm[k], out_sems.at[k])
        for k in range(near)
    ]
    for copy in leaving:
        copy.start()
    wait_all(leaving)


def near_sum_kernel(where_ref, *refs):
    far = refs[0].shape[0]
    sources, outs = refs[:-far], refs[-far:]
    near = len(sources) // 2
    here = where_ref[0] // near

    def total(arrays, block):
        value = arrays[0][block].astype(F32)
        for array in arrays[1:]:
            value = value + array[block].astype(F32)
        return value

    for m in range(far):
        block = lax.rem(here + m, far)
        outs[m][0] = total(sources[:near], block).astype(outs[m].dtype)
        outs[m][1:] = total(sources[near:], block).astype(outs[m].dtype)


def finish_kernel(normalise, slots, *refs):
    sources, out_ref = refs[:-1], refs[-1]
    here = out_ref.shape[0]
    total = sources[0][...]
    for source in sources[1:]:
        total = total + source[...].astype(F32)
    for d in range(3):
        value = total[d]
        value = value * normalise
        for group in range(slots.groups):
            first = group * slots.per_group
            count = min(slots.per_group, here - first)
            out_ref[first : first + count, d * slots.columns : (d + 1) * slots.columns] = value[
                :count, group * slots.columns : (group + 1) * slots.columns
            ]


def params(mib):
    return pltpu.CompilerParams(vmem_limit_bytes=mib * 1024 * 1024)


def cost(flops, moved):
    return pl.CostEstimate(flops=flops, bytes_accessed=moved, transcendentals=0)


def chunks_of(modes):
    quarter = modes // 4
    return ((0, 2 * quarter), (2 * quarter, quarter), (3 * quarter, quarter))


def per_device(eigvecs, link_seed, ownership):
    modes, _, _, layers, plane = eigvecs.shape
    assert layers == 1
    devices = lax.axis_size("sx")
    here = ownership.shape[0] // devices
    depth = 3 * plane
    tiles = plane // LANES
    slots = Slots(modes, here)
    vmem = pl.BlockSpec(memory_space=pltpu.VMEM)
    smem = pl.BlockSpec(memory_space=pltpu.SMEM)
    anywhere = pl.BlockSpec(memory_space=pl.ANY)

    raw = eigvecs.transpose(0, 2, 3, 1, 4).reshape(3 * modes, 2, plane)
    route = [(i, (i - 1) % devices) for i in range(devices)]
    chunks = chunks_of(modes)
    own, upper = [], []
    for some, room in ((chunks[:1], 52), (chunks[1:], 50)):
        loaded = pl.pallas_call(
            functools.partial(load_kernel, [3 * first for first, _ in some]),
            name="load_modes",
            out_shape=[jax.ShapeDtypeStruct((3 * count, 2, plane), BF16) for _, count in some],
            in_specs=[anywhere] * (1 + len(own[-1:])),
            out_specs=[vmem] * len(some),
            scratch_shapes=[pltpu.SemaphoreType.DMA((len(some), PIECES))],
            compiler_params=params(room),
            cost_estimate=cost(0, 12 * modes * plane),
        )(raw, *own[-1:])
        for part, (_, count) in zip(loaded, some):
            part = part.reshape(count, 3, 2, plane).transpose(1, 2, 0, 3)
            own.append(part)
            upper.append(lax.ppermute(part, "sx", route))

    where = lax.axis_index("sx").reshape(1).astype(jnp.int32)
    owners = slots.arrange(slots.codes(ownership).reshape(devices, here))
    near = 1
    while near * near < devices:
        near *= 2
    far = devices // near
    assert near * far == devices
    flops = 4 * modes * modes * depth * 2
    wide = pltpu.VMEM((2 * modes, depth), BF16)
    table = (slots.LOW, slots.depth)
    fold_scratch = pltpu.VMEM((TM // 2, modes, LANES), F32)
    chosen_scratch = pltpu.VMEM((2, devices // 2 * slots.all_rows, slots.depth), BF16)

    block = (slots.rows, LANES)
    *sent_inner, links_x, left = pl.pallas_call(
        functools.partial(inner_kernel, slots, (near, far)),
        name="inner_directions",
        out_shape=[jax.ShapeDtypeStruct((far, 2) + block, BF16)] * near
        + [
            jax.ShapeDtypeStruct((18, tiles, LANES), F32),
            jax.ShapeDtypeStruct((2 * modes, depth), BF16),
        ],
        in_specs=[smem, smem, vmem] + [anywhere] * 3,
        out_specs=[vmem] * (near + 1) + [anywhere],
        scratch_shapes=[
            wide,
            wide,
            wide,
            pltpu.VMEM((3, 18, tiles, LANES), F32),
            pltpu.VMEM((2,) + table, F32),
            fold_scratch,
            chosen_scratch,
            pltpu.VMEM((devices, 2) + block, BF16),
            pltpu.SemaphoreType.DMA((3, 6)),
            pltpu.SemaphoreType.DMA,
        ],
        compiler_params=params(40),
        cost_estimate=cost(6 * flops, 8 * 2**20),
    )(link_seed, where, owners, *own)
    sizes = [count for _, count in chunks]

    def outer_scratch(size):
        return [
            pltpu.VMEM((2 * size, depth), BF16),
            wide,
            pltpu.VMEM((2 * size, depth), BF16),
            pltpu.SemaphoreType.DMA((2, 6)),
        ]

    def outer(kernel, name, which, shape, before):
        return pl.pallas_call(
            kernel,
            name=name,
            out_shape=jax.ShapeDtypeStruct(shape, F32),
            in_specs=[vmem] + [anywhere] * (2 + len(before)),
            out_specs=vmem,
            scratch_shapes=outer_scratch(sizes[which]),
            compiler_params=params(24),
            cost_estimate=cost(2**20, 2**18),
        )(links_x, upper[which], left, *before)

    first_x = outer(wide_kernel, "outer_first", 0, (2, modes, sizes[0]), [])
    second_x = outer(narrow_kernel, "outer_second", 1, (modes, 2 * sizes[1]), [first_x])
    sent = pl.pallas_call(
        functools.partial(last_kernel, slots, (near, far)),
        name="outer_last",
        out_shape=[jax.ShapeDtypeStruct((far,) + block, BF16)] * near,
        in_specs=[smem] + [vmem] * 4 + [anywhere] * 2,
        out_specs=[anywhere] * near,
        scratch_shapes=outer_scratch(sizes[2])
        + [
            pltpu.VMEM(table, F32),
            fold_scratch,
            chosen_scratch,
            pltpu.VMEM((devices,) + block, BF16),
            pltpu.SemaphoreType.DMA((near,)),
        ],
        compiler_params=params(24),
        cost_estimate=cost(2**20, 2**18),
    )(where, owners, first_x, second_x, links_x, upper[2], left)

    def onward(step, array, size, inner):
        def target(i):
            index = i // inner % size
            return i + ((index + step) % size - index) * inner

        return lax.ppermute(array, "sx", [(i, target(i)) for i in range(devices)])

    gathered = [
        array if k == 0 else onward(k, array, near, 1)
        for arrays in (sent, sent_inner)
        for k, array in enumerate(arrays)
    ]
    halfway = pl.pallas_call(
        near_sum_kernel,
        name="sum_near",
        out_shape=[
            jax.ShapeDtypeStruct((3,) + block, F32 if m == 0 else BF16) for m in range(far)
        ],
        in_specs=[smem] + [vmem] * (2 * near),
        out_specs=[vmem] * far,
        compiler_params=params(8),
        cost_estimate=cost(2**20, 2**20),
    )(where, *gathered)
    arrived = [halfway[0]] + [onward(m, halfway[m], far, near) for m in range(1, far)]

    extent_x = layers * devices
    normalise = 1.0 / math.sqrt(12.0 * extent_x * plane)
    return pl.pallas_call(
        functools.partial(finish_kernel, normalise, slots),
        name="sum_far",
        out_shape=jax.ShapeDtypeStruct((here, 3 * slots.columns), F32),
        in_specs=[vmem] * far,
        out_specs=vmem,
        compiler_params=params(8),
    )(*arrived)


def solution(mesh):
    return jax.shard_map(
        per_device,
        mesh=mesh,
        in_specs=(P("cfg", None, None, "sx", None), P("cfg"), P()),
        out_specs=P(("cfg", "sx"), None),
        check_vma=False,
    )
```

```python
import functools
import math

import jax
import jax.numpy as jnp
from jax import lax
from jax.experimental import pallas as pl
from jax.experimental.pallas import tpu as pltpu
from jax.sharding import PartitionSpec as P

TM = 4
NZ = 64
LANES = 128
MODULUS = 46337
STEP = 32
PIECES = 4
F32 = jnp.float32
BF16 = jnp.bfloat16
NT = (((1,), (1,)), ((), ()))


def dot(left, right, dims=(((1,), (0,)), ((), ()))):
    return lax.dot_general(left, right, dims, preferred_element_type=F32)


def iota(shape, axis):
    return lax.broadcasted_iota(jnp.int32, shape, axis)


def round_up(value, step):
    return -(-value // step) * step


def divide(value):
    quotient = (value.astype(F32) * (1.0 / MODULUS)).astype(jnp.int32)
    rest = value - quotient * MODULUS
    below, above = rest < 0, rest >= MODULUS
    rest = jnp.where(below, rest + MODULUS, jnp.where(above, rest - MODULUS, rest))
    quotient = jnp.where(below, quotient - 1, jnp.where(above, quotient + 1, quotient))
    return quotient, rest


def link_angles(seed, site):
    high, low = divide(site)
    mixed = divide(seed * seed + low)[1]
    mixed = divide(mixed * mixed + high * 977 + 31)[1]
    angles = []
    for index in range(7):
        g = divide(mixed + (5171 * index + 1))[1]
        g = divide(g * g + low)[1]
        g = divide(g * g + 12345)[1]
        angles.append(g.astype(F32) * (2.0 * math.pi / MODULUS) - math.pi)
    return angles


def store_links(u_ref, seed, site):
    a = link_angles(seed, site)
    ca, sa = jnp.cos(a[0]), jnp.sin(a[0])
    cb, sb = jnp.cos(a[1]), jnp.sin(a[1])
    cg, sg = jnp.cos(a[2]), jnp.sin(a[2])
    rotation = [
        [ca * cb * cg - sa * sg, -ca * cb * sg - sa * cg, ca * sb],
        [sa * cb * cg + ca * sg, -sa * cb * sg + ca * cg, sa * sb],
        [-sb * cg, sb * sg, cb],
    ]
    def phases(first, second):
        c1, s1, c2, s2 = jnp.cos(first), jnp.sin(first), jnp.cos(second), jnp.sin(second)
        return [(c1, s1), (c2, s2), (c1 * c2 - s1 * s2, -(s1 * c2 + c1 * s2))]

    left, right = phases(a[3], a[4]), phases(a[5], a[6])
    for c in range(3):
        for s in range(3):
            (cl, sl), (cr, sr) = left[c], right[s]
            u_ref[2 * (3 * c + s)] = rotation[c][s] * (cl * cr - sl * sr)
            u_ref[2 * (3 * c + s) + 1] = rotation[c][s] * (sl * cr + cl * sr)


def hop(vector_ref, out_ref, u_ref, first, count):
    all_modes, plane = vector_ref.shape[0] // 2, vector_ref.shape[1] // 3
    wide = (STEP // 8, 8, LANES)
    for t in range(plane // LANES):
        u = [jnp.broadcast_to(u_ref[k, t : t + 1, :], (8, LANES)) for k in range(18)]

        def body(block, carry, t=t, u=u):
            rows = [
                pl.ds(pl.multiple_of(part * all_modes + first + block * STEP, STEP), STEP)
                for part in range(2)
            ]
            lanes = [slice(c * plane + t * LANES, c * plane + (t + 1) * LANES) for c in range(3)]
            v = [
                [vector_ref[rows[part], lanes[c]].astype(F32).reshape(wide) for part in range(2)]
                for c in range(3)
            ]
            for c in range(3):
                real = imag = None
                for s in range(3):
                    ur, ui = u[2 * (3 * c + s)], u[2 * (3 * c + s) + 1]
                    re, im = v[s]
                    real = ur * re if real is None else real + ur * re
                    real = real - ui * im
                    imag = ur * im if imag is None else imag + ur * im
                    imag = imag + ui * re
                for part, value in ((0, real), (1, imag)):
                    out_ref[rows[part], lanes[c]] = value.reshape(STEP, LANES).astype(BF16)
            return carry

        lax.fori_loop(0, count // STEP, body, 0)


def products(left_ref, hop_ref):
    n, modes = left_ref.shape[0] // 2, hop_ref.shape[0] // 2
    by_real = dot(left_ref[:n, :], hop_ref[...], NT)
    by_imag = dot(left_ref[n:, :], hop_ref[...], NT)
    if modes % LANES:
        crossed = pltpu.roll(by_imag, modes, 1)
        low = iota(crossed.shape, 1) < modes
        return jnp.where(low, by_real + crossed, by_real - crossed)
    real = by_real[:, :modes] + by_imag[:, modes:]
    imag = by_real[:, modes:] - by_imag[:, :modes]
    return real, imag


class Slots:
    LOW = 2 * LANES

    def __init__(self, all_modes, slots):
        self.tiles = all_modes // TM
        assert 2 * self.tiles == LANES
        self.half = self.tiles // 2
        self.columns = 2 * TM * TM
        self.high = self.half * self.tiles // self.LOW
        assert self.high * self.columns == self.LOW
        self.depth = self.LOW + LANES
        self.groups = LANES // self.columns
        self.per_group = -(-slots // self.groups)
        self.rows = round_up(self.per_group, 8)
        self.all_rows = round_up(self.groups * self.rows, 16)
        assert self.all_rows == self.groups * self.rows

    def codes(self, pair):
        n = self.tiles

        def start(i):
            return i * n - (i * (i - 1)) // 2

        inside = ((2 * n + 1) ** 2 - 8 * pair).astype(F32)
        i = ((2 * n + 1 - jnp.sqrt(inside)) * 0.5).astype(jnp.int32)
        i = jnp.where(start(i) > pair, i - 1, i)
        i = jnp.where(start(i + 1) <= pair, i + 1, i)
        j = i + pair - start(i)
        first = i < self.half
        place = jnp.where(first, i * n + j, (n - 1 - i) * n + (n - 1 - j))
        corner = jnp.logical_and(jnp.logical_not(first), i == j)
        high = jnp.where(corner, 0, place // self.LOW)
        low = jnp.where(corner, self.LOW + (n - 1 - i), place % self.LOW)
        return high * 512 + low

    def arrange(self, codes):
        devices, slots = codes.shape
        spread = jnp.pad(
            codes, ((0, 0), (0, self.groups * self.per_group - slots)), constant_values=-1
        ).reshape(devices, self.groups, self.per_group)
        spread = jnp.pad(
            spread, ((0, 0), (0, 0), (0, self.rows - self.per_group)), constant_values=-1
        )
        return spread.reshape(devices, self.all_rows).T


def store_table(table_ref, fold_ref, real, imag, slots):
    all_modes = real.shape[0]
    n, half = slots.tiles, slots.half
    parts = [real - real.T, imag + imag.T]

    def choose(count, width, turned):
        row, column = iota((count, all_modes), 0), iota((count, all_modes), 1)
        r, i = row // width, row % width
        if turned:
            i = n - 1 - i
        return (column == i * TM + r).astype(F32).astype(BF16)

    pick = [choose(TM * half, half, turned) for turned in (False, True)]
    spread = [choose(all_modes, n, turned) for turned in (False, True)]
    row_i = iota((TM * half, all_modes), 0) % half
    lane_j = iota((TM * half, all_modes), 1) % n
    corners = []
    for part in range(2):
        entries = parts[part].astype(BF16)
        straight, turned = [
            dot(dot(pick[k], entries).astype(BF16), spread[k], NT) for k in range(2)
        ]
        folded = jnp.where(lane_j >= row_i, straight, turned)
        for k in range(TM // 2):
            fold_ref[k, part * TM * half : (part + 1) * TM * half, :] = folded[
                :, k * LANES : (k + 1) * LANES
            ]
        diagonal = jnp.where(lane_j == row_i, turned, 0.0)
        for r in range(TM):
            corners.append(
                jnp.sum(diagonal[r * half : (r + 1) * half], axis=0, keepdims=True)
            )
    low = iota((2 * TM, LANES), 1) < n

    def split(even, odd, high, lanes):
        for pair in range(TM // 2):
            e, o = even[pair], odd[pair]
            top = high * slots.columns + 2 * pair * 2 * TM
            table_ref[top : top + 2 * TM, lanes] = jnp.where(low, e, pltpu.roll(o, n, 1))
            table_ref[top + 2 * TM : top + 4 * TM, lanes] = jnp.where(
                low, pltpu.roll(e, n, 1), o
            )

    halves = [slice(k * LANES, (k + 1) * LANES) for k in range(TM // 2)]
    for two in range(half // 2):
        even = [fold_ref[k, pl.ds(2 * two, 2 * TM, stride=half), :] for k in range(TM // 2)]
        odd = [fold_ref[k, pl.ds(2 * two + 1, 2 * TM, stride=half), :] for k in range(TM // 2)]
        at = two * LANES % slots.LOW
        split(even, odd, two * LANES // slots.LOW, slice(at, at + LANES))
    corner = jnp.concatenate(corners, 0)
    nothing = jnp.zeros((2 * TM, LANES), F32)
    table_ref[:, slots.LOW :] = jnp.zeros((slots.LOW, LANES), F32)
    split([corner[:, h] for h in halves], [nothing] * len(halves), 0, slice(slots.LOW, slots.depth))


def pick_tiles(emit, owner_ref, tables, chosen_ref, slots):
    inside, column = iota((slots.LOW, LANES), 0) % slots.columns, iota((slots.LOW, LANES), 1)
    entry = (inside % (2 * TM)) * TM + inside // (2 * TM)
    fold = (column % slots.columns == entry).astype(F32).astype(BF16)
    rows = slots.all_rows
    lane16 = iota((16, LANES), 1)
    lanes = [
        (lane16 + t * LANES).astype(jnp.int16) for t in range(slots.depth // LANES)
    ]
    one, zero = jnp.ones((16, LANES), BF16), jnp.zeros((16, LANES), BF16)
    lane_group = iota((slots.rows, LANES), 1) // slots.columns
    high_group = iota((rows, LANES), 1) // slots.columns
    count = owner_ref.shape[1] // 2
    for half in range(2):
        high = []
        for k in range(count):
            n = half * count + k
            code = jnp.broadcast_to(owner_ref[:, n : n + 1], (rows, LANES))
            high.append(code >> 9)
            low = (code & 511).astype(jnp.int16)
            for top in range(0, rows, 16):
                for t in range(slots.depth // LANES):
                    chosen_ref[
                        half, k * rows + top : k * rows + top + 16, t * LANES : (t + 1) * LANES
                    ] = jnp.where(low[top : top + 16] == lanes[t], one, zero)
        for d, table in enumerate(tables):
            parts = dot(chosen_ref[half], table, NT)
            masked = jnp.concatenate(
                [
                    jnp.concatenate(
                        [
                            jnp.where(
                                high[k] == high_group + side * slots.groups,
                                parts[k * rows : (k + 1) * rows, side * LANES : (side + 1) * LANES],
                                0.0,
                            )
                            for side in range(2)
                        ],
                        1,
                    ).astype(BF16)
                    for k in range(count)
                ],
                0,
            )
            picked = dot(masked, fold)
            for k in range(count):
                top = k * rows
                packed = picked[top : top + slots.rows]
                for g in range(1, slots.groups):
                    piece = picked[top + g * slots.rows : top + (g + 1) * slots.rows]
                    packed = jnp.where(lane_group == g, piece, packed)
                emit(half * count + k, d, packed)


def store_all_links(links_ref, seed_ref, x):
    _, _, tiles, _ = links_ref.shape
    plane = tiles * LANES
    place = iota((tiles, LANES), 0) * LANES + iota((tiles, LANES), 1)
    before_y = jnp.where(place < NZ, place + (plane - NZ), place - NZ)
    before_z = jnp.where(place % NZ == 0, place + (NZ - 1), place - 1)
    for d, source in enumerate((place, before_y, before_z)):
        store_links(links_ref.at[d], seed_ref[d], source + x * plane)


def load_modes(planar_hbm, out_ref, sems, first):
    _, _, count, plane = planar_hbm.shape
    modes = out_ref.shape[0] // 2
    copies = [
        pltpu.make_async_copy(
            planar_hbm.at[c, part],
            out_ref.at[pl.ds(part * modes + first, count), pl.ds(c * plane, plane)],
            sems.at[2 * c + part],
        )
        for c in range(3)
        for part in range(2)
    ]
    for copy in copies:
        copy.start()
    return copies


def load_all(parts, out_ref, sems):
    quarter = out_ref.shape[0] // 8
    copies = []
    for k, (first, _) in enumerate(chunks_of(4 * quarter)):
        copies += load_modes(parts[k], out_ref, sems.at[k], first)
    return copies


def wait_all(copies):
    for copy in copies:
        copy.wait()


def store_left_y(out_ref, left_ref, plane):
    wide = 2 * LANES
    source, target = iota((wide, wide), 0), iota((wide, wide), 1)
    halves = source == (target // LANES) * LANES + (target + NZ) % LANES
    halves = halves.astype(F32).astype(BF16)
    low = iota((left_ref.shape[0], LANES), 1) < NZ
    for c in range(3):
        swapped = []
        for start in range(c * plane, (c + 1) * plane, wide):
            both = dot(left_ref[:, start : start + wide], halves)
            swapped += [both[:, :LANES], both[:, LANES:]]
        for t in range(plane // LANES):
            lanes = slice(c * plane + t * LANES, c * plane + (t + 1) * LANES)
            out_ref[:, lanes] = jnp.where(low, swapped[t - 1], swapped[t]).astype(BF16)


def store_left_z(out_ref, left_ref, plane):
    wide = 2 * LANES
    source, target = iota((wide, wide), 0), iota((wide, wide), 1)
    before = jnp.where(target % NZ == 0, target + (NZ - 1), target - 1)
    behind = (source == before).astype(F32).astype(BF16)
    for start in range(0, 3 * plane, wide):
        piece = dot(left_ref[:, start : start + wide], behind)
        out_ref[:, start : start + wide] = piece.astype(BF16)


def load_kernel(starts, whole_hbm, *refs):
    parts, sems = refs[-1 - len(starts) : -1], refs[-1]
    copies = []
    for k, (start, part) in enumerate(zip(starts, parts)):
        count = part.shape[0] // PIECES
        for piece in range(PIECES):
            copies.append(
                pltpu.make_async_copy(
                    whole_hbm.at[pl.ds(start + piece * count, count)],
                    part.at[pl.ds(piece * count, count)],
                    sems.at[k, piece],
                )
            )
    for copy in copies:
        copy.start()
    wait_all(copies)


def place_of(n, here, near, far):
    return lax.rem(n % near + near - lax.rem(here, near), near) * far + n // near


def inner_kernel(
    slots,
    grid,
    seed_ref,
    where_ref,
    owner_ref,
    a,
    b,
    c,
    *refs,
):
    near, far = grid
    sent, refs = refs[:near], refs[near:]
    links_x_ref, own_hbm, vector_ref, left_ref, hop_ref, links_ref, *refs = refs
    table_ref, fold_ref, chosen_ref, stage_ref, sems, own_sem = refs
    modes, plane = vector_ref.shape[0] // 2, vector_ref.shape[1] // 3
    copies = load_all((a, b, c), vector_ref, sems)
    store_all_links(links_ref, seed_ref, where_ref[0])
    links_x_ref[...] = links_ref[0]
    wait_all(copies)
    own = pltpu.make_async_copy(vector_ref, own_hbm, own_sem)
    own.start()
    tables = []
    for d, store_left in ((1, store_left_y), (2, store_left_z)):
        store_left(left_ref, vector_ref, plane)
        hop(vector_ref, hop_ref, links_ref.at[d], 0, modes)
        real, imag = products(left_ref, hop_ref)
        store_table(table_ref.at[d - 1], fold_ref, real, imag, slots)
        tables.append(table_ref.at[d - 1])

    def emit(n, d, packed):
        stage_ref[place_of(n, where_ref[0], near, far), d] = packed.astype(BF16)

    pick_tiles(emit, owner_ref, [t[...].astype(BF16) for t in tables], chosen_ref, slots)
    for k in range(near):
        sent[k][...] = stage_ref[k * far : (k + 1) * far]
    own.wait()


def outer_chunk(links_ref, upper_hbm, own_hbm, vector_ref, left_ref, hop_ref, sems):
    arriving = load_modes(upper_hbm, vector_ref, sems.at[0], 0)
    count = left_ref.shape[0] // PIECES
    own = [
        pltpu.make_async_copy(
            own_hbm.at[pl.ds(piece * count, count)],
            left_ref.at[pl.ds(piece * count, count)],
            sems.at[1, piece],
        )
        for piece in range(PIECES)
    ]
    for copy in own:
        copy.start()
    wait_all(arriving)
    hop(vector_ref, hop_ref, links_ref, 0, vector_ref.shape[0] // 2)
    wait_all(own)
    return products(left_ref, hop_ref)


def wide_kernel(links_ref, upper_hbm, own_hbm, out_ref, *scratch):
    out_ref[0], out_ref[1] = outer_chunk(links_ref, upper_hbm, own_hbm, *scratch)


def narrow_kernel(links_ref, upper_hbm, own_hbm, before_hbm, out_ref, *scratch):
    del before_hbm
    out_ref[...] = outer_chunk(links_ref, upper_hbm, own_hbm, *scratch)


def last_kernel(
    slots,
    grid,
    where_ref,
    owner_ref,
    first_ref,
    second_ref,
    links_ref,
    upper_hbm,
    own_hbm,
    *refs,
):
    near, far = grid
    sent_hbm, refs = refs[:near], refs[near:]
    vector_ref, left_ref, hop_ref, sems, table_ref, fold_ref, chosen_ref, stage_ref, out_sems = refs
    last = outer_chunk(links_ref, upper_hbm, own_hbm, vector_ref, left_ref, hop_ref, sems)
    quarter = last.shape[1] // 2
    low = iota(last.shape, 1) < quarter
    second = second_ref[...]
    real = [first_ref[0], jnp.where(low, second, pltpu.roll(last, quarter, 1))]
    imag = [first_ref[1], jnp.where(low, pltpu.roll(second, quarter, 1), last)]
    store_table(
        table_ref, fold_ref, jnp.concatenate(real, 1), jnp.concatenate(imag, 1), slots
    )

    def emit(n, d, packed):
        stage_ref[place_of(n, where_ref[0], near, far)] = packed.astype(BF16)

    pick_tiles(emit, owner_ref, [table_ref[...].astype(BF16)], chosen_ref, slots)
    leaving = [
        pltpu.make_async_copy(stage_ref.at[pl.ds(k * far, far)], sent_hbm[k], out_sems.at[k])
        for k in range(near)
    ]
    for copy in leaving:
        copy.start()
    wait_all(leaving)


def near_sum_kernel(where_ref, *refs):
    far = refs[0].shape[0]
    sources, outs = refs[:-far], refs[-far:]
    near = len(sources) // 2
    here = where_ref[0] // near

    def total(arrays, block):
        value = arrays[0][block].astype(F32)
        for array in arrays[1:]:
            value = value + array[block].astype(F32)
        return value

    for m in range(far):
        block = lax.rem(here + m, far)
        outs[m][0] = total(sources[:near], block).astype(outs[m].dtype)
        outs[m][1:] = total(sources[near:], block).astype(outs[m].dtype)


def finish_kernel(normalise, slots, *refs):
    sources, out_ref = refs[:-1], refs[-1]
    here = out_ref.shape[0]
    total = sources[0][...]
    for source in sources[1:]:
        total = total + source[...].astype(F32)
    for d in range(3):
        value = total[d]
        value = value * normalise
        for group in range(slots.groups):
            first = group * slots.per_group
            count = min(slots.per_group, here - first)
            out_ref[first : first + count, d * slots.columns : (d + 1) * slots.columns] = value[
                :count, group * slots.columns : (group + 1) * slots.columns
            ]


def params(mib):
    return pltpu.CompilerParams(vmem_limit_bytes=mib * 1024 * 1024)


def cost(flops, moved):
    return pl.CostEstimate(flops=flops, bytes_accessed=moved, transcendentals=0)


def chunks_of(modes):
    quarter = modes // 4
    return ((0, 2 * quarter), (2 * quarter, quarter), (3 * quarter, quarter))


def per_device(eigvecs, link_seed, ownership):
    modes, _, _, layers, plane = eigvecs.shape
    assert layers == 1
    devices = lax.axis_size("sx")
    here = ownership.shape[0] // devices
    depth = 3 * plane
    tiles = plane // LANES
    slots = Slots(modes, here)
    vmem = pl.BlockSpec(memory_space=pltpu.VMEM)
    smem = pl.BlockSpec(memory_space=pltpu.SMEM)
    anywhere = pl.BlockSpec(memory_space=pl.ANY)

    raw = eigvecs.transpose(0, 2, 3, 1, 4).reshape(3 * modes, 2, plane)
    route = [(i, (i - 1) % devices) for i in range(devices)]
    chunks = chunks_of(modes)
    own, upper = [], []
    for some, room in ((chunks[:1], 52), (chunks[1:], 50)):
        loaded = pl.pallas_call(
            functools.partial(load_kernel, [3 * first for first, _ in some]),
            name="load_modes",
            out_shape=[jax.ShapeDtypeStruct((3 * count, 2, plane), BF16) for _, count in some],
            in_specs=[anywhere] * (1 + len(own[-1:])),
            out_specs=[vmem] * len(some),
            scratch_shapes=[pltpu.SemaphoreType.DMA((len(some), PIECES))],
            compiler_params=params(room),
            cost_estimate=cost(0, 12 * modes * plane),
        )(raw, *own[-1:])
        for part, (_, count) in zip(loaded, some):
            part = part.reshape(count, 3, 2, plane).transpose(1, 2, 0, 3)
            own.append(part)
            upper.append(lax.ppermute(part, "sx", route))

    where = lax.axis_index("sx").reshape(1).astype(jnp.int32)
    owners = slots.arrange(slots.codes(ownership).reshape(devices, here))
    near = 1
    while near * near < devices:
        near *= 2
    far = devices // near
    assert near * far == devices
    flops = 4 * modes * modes * depth * 2
    wide = pltpu.VMEM((2 * modes, depth), BF16)
    table = (slots.LOW, slots.depth)
    fold_scratch = pltpu.VMEM((TM // 2, modes, LANES), F32)
    chosen_scratch = pltpu.VMEM((2, devices // 2 * slots.all_rows, slots.depth), BF16)

    block = (slots.rows, LANES)
    *sent_inner, links_x, left = pl.pallas_call(
        functools.partial(inner_kernel, slots, (near, far)),
        name="inner_directions",
        out_shape=[jax.ShapeDtypeStruct((far, 2) + block, BF16)] * near
        + [
            jax.ShapeDtypeStruct((18, tiles, LANES), F32),
            jax.ShapeDtypeStruct((2 * modes, depth), BF16),
        ],
        in_specs=[smem, smem, vmem] + [anywhere] * 3,
        out_specs=[vmem] * (near + 1) + [anywhere],
        scratch_shapes=[
            wide,
            wide,
            wide,
            pltpu.VMEM((3, 18, tiles, LANES), F32),
            pltpu.VMEM((2,) + table, F32),
            fold_scratch,
            chosen_scratch,
            pltpu.VMEM((devices, 2) + block, BF16),
            pltpu.SemaphoreType.DMA((3, 6)),
            pltpu.SemaphoreType.DMA,
        ],
        compiler_params=params(20),
        cost_estimate=cost(6 * flops, 8 * 2**20),
    )(link_seed, where, owners, *own)
    sizes = [count for _, count in chunks]

    def outer_scratch(size):
        return [
            pltpu.VMEM((2 * size, depth), BF16),
            wide,
            pltpu.VMEM((2 * size, depth), BF16),
            pltpu.SemaphoreType.DMA((2, 6)),
        ]

    def outer(kernel, name, which, shape, before):
        return pl.pallas_call(
            kernel,
            name=name,
            out_shape=jax.ShapeDtypeStruct(shape, F32),
            in_specs=[vmem] + [anywhere] * (2 + len(before)),
            out_specs=vmem,
            scratch_shapes=outer_scratch(sizes[which]),
            compiler_params=params(20),
            cost_estimate=cost(2**20, 2**18),
        )(links_x, upper[which], left, *before)

    first_x = outer(wide_kernel, "outer_first", 0, (2, modes, sizes[0]), [])
    second_x = outer(narrow_kernel, "outer_second", 1, (modes, 2 * sizes[1]), [first_x])
    sent = pl.pallas_call(
        functools.partial(last_kernel, slots, (near, far)),
        name="outer_last",
        out_shape=[jax.ShapeDtypeStruct((far,) + block, BF16)] * near,
        in_specs=[smem] + [vmem] * 4 + [anywhere] * 2,
        out_specs=[anywhere] * near,
        scratch_shapes=outer_scratch(sizes[2])
        + [
            pltpu.VMEM(table, F32),
            fold_scratch,
            chosen_scratch,
            pltpu.VMEM((devices,) + block, BF16),
            pltpu.SemaphoreType.DMA((near,)),
        ],
        compiler_params=params(20),
        cost_estimate=cost(2**20, 2**18),
    )(where, owners, first_x, second_x, links_x, upper[2], left)

    def onward(step, array, size, inner):
        def target(i):
            index = i // inner % size
            return i + ((index + step) % size - index) * inner

        return lax.ppermute(array, "sx", [(i, target(i)) for i in range(devices)])

    gathered = [
        array if k == 0 else onward(k, array, near, 1)
        for arrays in (sent, sent_inner)
        for k, array in enumerate(arrays)
    ]
    halfway = pl.pallas_call(
        near_sum_kernel,
        name="sum_near",
        out_shape=[
            jax.ShapeDtypeStruct((3,) + block, F32 if m == 0 else BF16) for m in range(far)
        ],
        in_specs=[smem] + [vmem] * (2 * near),
        out_specs=[vmem] * far,
        compiler_params=params(8),
        cost_estimate=cost(2**20, 2**20),
    )(where, *gathered)
    arrived = [halfway[0]] + [onward(m, halfway[m], far, near) for m in range(1, far)]

    extent_x = layers * devices
    normalise = 1.0 / math.sqrt(12.0 * extent_x * plane)
    return pl.pallas_call(
        functools.partial(finish_kernel, normalise, slots),
        name="sum_far",
        out_shape=jax.ShapeDtypeStruct((here, 3 * slots.columns), F32),
        in_specs=[vmem] * far,
        out_specs=vmem,
        compiler_params=params(8),
    )(*arrived)


def solution(mesh):
    return jax.shard_map(
        per_device,
        mesh=mesh,
        in_specs=(P("cfg", None, None, "sx", None), P("cfg"), P()),
        out_specs=P(("cfg", "sx"), None),
        check_vma=False,
    )
```

```python
import functools
import math

import jax
import jax.numpy as jnp
from jax import lax
from jax.experimental import pallas as pl
from jax.experimental.pallas import tpu as pltpu
from jax.sharding import PartitionSpec as P

TM = 4
NZ = 64
LANES = 128
MODULUS = 46337
STEP = 32
PIECES = 4
F32 = jnp.float32
BF16 = jnp.bfloat16
NT = (((1,), (1,)), ((), ()))


def dot(left, right, dims=(((1,), (0,)), ((), ()))):
    return lax.dot_general(left, right, dims, preferred_element_type=F32)


def iota(shape, axis):
    return lax.broadcasted_iota(jnp.int32, shape, axis)


def round_up(value, step):
    return -(-value // step) * step


def divide(value):
    quotient = (value.astype(F32) * (1.0 / MODULUS)).astype(jnp.int32)
    rest = value - quotient * MODULUS
    below, above = rest < 0, rest >= MODULUS
    rest = jnp.where(below, rest + MODULUS, jnp.where(above, rest - MODULUS, rest))
    quotient = jnp.where(below, quotient - 1, jnp.where(above, quotient + 1, quotient))
    return quotient, rest


def link_angles(seed, site):
    high, low = divide(site)
    mixed = divide(seed * seed + low)[1]
    mixed = divide(mixed * mixed + high * 977 + 31)[1]
    angles = []
    for index in range(7):
        g = divide(mixed + (5171 * index + 1))[1]
        g = divide(g * g + low)[1]
        g = divide(g * g + 12345)[1]
        angles.append(g.astype(F32) * (2.0 * math.pi / MODULUS) - math.pi)
    return angles


def store_links(u_ref, seed, site):
    a = link_angles(seed, site)
    ca, sa = jnp.cos(a[0]), jnp.sin(a[0])
    cb, sb = jnp.cos(a[1]), jnp.sin(a[1])
    cg, sg = jnp.cos(a[2]), jnp.sin(a[2])
    rotation = [
        [ca * cb * cg - sa * sg, -ca * cb * sg - sa * cg, ca * sb],
        [sa * cb * cg + ca * sg, -sa * cb * sg + ca * cg, sa * sb],
        [-sb * cg, sb * sg, cb],
    ]
    def phases(first, second):
        c1, s1, c2, s2 = jnp.cos(first), jnp.sin(first), jnp.cos(second), jnp.sin(second)
        return [(c1, s1), (c2, s2), (c1 * c2 - s1 * s2, -(s1 * c2 + c1 * s2))]

    left, right = phases(a[3], a[4]), phases(a[5], a[6])
    for c in range(3):
        for s in range(3):
            (cl, sl), (cr, sr) = left[c], right[s]
            u_ref[2 * (3 * c + s)] = rotation[c][s] * (cl * cr - sl * sr)
            u_ref[2 * (3 * c + s) + 1] = rotation[c][s] * (sl * cr + cl * sr)


def hop(vector_ref, out_ref, u_ref, first, count):
    all_modes, plane = vector_ref.shape[0] // 2, vector_ref.shape[1] // 3
    wide = (STEP // 8, 8, LANES)
    for t in range(plane // LANES):
        u = [jnp.broadcast_to(u_ref[k, t : t + 1, :], (8, LANES)) for k in range(18)]

        def body(block, carry, t=t, u=u):
            rows = [
                pl.ds(pl.multiple_of(part * all_modes + first + block * STEP, STEP), STEP)
                for part in range(2)
            ]
            lanes = [slice(c * plane + t * LANES, c * plane + (t + 1) * LANES) for c in range(3)]
            v = [
                [vector_ref[rows[part], lanes[c]].astype(F32).reshape(wide) for part in range(2)]
                for c in range(3)
            ]
            for c in range(3):
                real = imag = None
                for s in range(3):
                    ur, ui = u[2 * (3 * c + s)], u[2 * (3 * c + s) + 1]
                    re, im = v[s]
                    real = ur * re if real is None else real + ur * re
                    real = real - ui * im
                    imag = ur * im if imag is None else imag + ur * im
                    imag = imag + ui * re
                for part, value in ((0, real), (1, imag)):
                    out_ref[rows[part], lanes[c]] = value.reshape(STEP, LANES).astype(BF16)
            return carry

        lax.fori_loop(0, count // STEP, body, 0)


def products(left_ref, hop_ref):
    n, modes = left_ref.shape[0] // 2, hop_ref.shape[0] // 2
    by_real = dot(left_ref[:n, :], hop_ref[...], NT)
    by_imag = dot(left_ref[n:, :], hop_ref[...], NT)
    if modes % LANES:
        crossed = pltpu.roll(by_imag, modes, 1)
        low = iota(crossed.shape, 1) < modes
        return jnp.where(low, by_real + crossed, by_real - crossed)
    real = by_real[:, :modes] + by_imag[:, modes:]
    imag = by_real[:, modes:] - by_imag[:, :modes]
    return real, imag


class Slots:
    LOW = 2 * LANES

    def __init__(self, all_modes, slots):
        self.tiles = all_modes // TM
        assert 2 * self.tiles == LANES
        self.half = self.tiles // 2
        self.columns = 2 * TM * TM
        self.high = self.half * self.tiles // self.LOW
        assert self.high * self.columns == self.LOW
        self.depth = self.LOW + LANES
        self.groups = LANES // self.columns
        self.per_group = -(-slots // self.groups)
        self.rows = round_up(self.per_group, 8)
        self.all_rows = round_up(self.groups * self.rows, 16)
        assert self.all_rows == self.groups * self.rows

    def codes(self, pair):
        n = self.tiles

        def start(i):
            return i * n - (i * (i - 1)) // 2

        inside = ((2 * n + 1) ** 2 - 8 * pair).astype(F32)
        i = ((2 * n + 1 - jnp.sqrt(inside)) * 0.5).astype(jnp.int32)
        i = jnp.where(start(i) > pair, i - 1, i)
        i = jnp.where(start(i + 1) <= pair, i + 1, i)
        j = i + pair - start(i)
        first = i < self.half
        place = jnp.where(first, i * n + j, (n - 1 - i) * n + (n - 1 - j))
        corner = jnp.logical_and(jnp.logical_not(first), i == j)
        high = jnp.where(corner, 0, place // self.LOW)
        low = jnp.where(corner, self.LOW + (n - 1 - i), place % self.LOW)
        return high * 512 + low

    def arrange(self, codes):
        devices, slots = codes.shape
        spread = jnp.pad(
            codes, ((0, 0), (0, self.groups * self.per_group - slots)), constant_values=-1
        ).reshape(devices, self.groups, self.per_group)
        spread = jnp.pad(
            spread, ((0, 0), (0, 0), (0, self.rows - self.per_group)), constant_values=-1
        )
        return spread.reshape(devices, self.all_rows).T


def store_table(table_ref, fold_ref, real, imag, slots):
    all_modes = real.shape[0]
    n, half = slots.tiles, slots.half
    parts = [real - real.T, imag + imag.T]

    def choose(count, width, turned):
        row, column = iota((count, all_modes), 0), iota((count, all_modes), 1)
        r, i = row // width, row % width
        if turned:
            i = n - 1 - i
        return (column == i * TM + r).astype(F32).astype(BF16)

    pick = [choose(TM * half, half, turned) for turned in (False, True)]
    spread = [choose(all_modes, n, turned) for turned in (False, True)]
    row_i = iota((TM * half, all_modes), 0) % half
    lane_j = iota((TM * half, all_modes), 1) % n
    corners = []
    for part in range(2):
        entries = parts[part].astype(BF16)
        straight, turned = [
            dot(dot(pick[k], entries).astype(BF16), spread[k], NT) for k in range(2)
        ]
        folded = jnp.where(lane_j >= row_i, straight, turned)
        for k in range(TM // 2):
            fold_ref[k, part * TM * half : (part + 1) * TM * half, :] = folded[
                :, k * LANES : (k + 1) * LANES
            ]
        diagonal = jnp.where(lane_j == row_i, turned, 0.0)
        for r in range(TM):
            corners.append(
                jnp.sum(diagonal[r * half : (r + 1) * half], axis=0, keepdims=True)
            )
    low = iota((2 * TM, LANES), 1) < n

    def split(even, odd, high, lanes):
        for pair in range(TM // 2):
            e, o = even[pair], odd[pair]
            top = high * slots.columns + 2 * pair * 2 * TM
            table_ref[top : top + 2 * TM, lanes] = jnp.where(low, e, pltpu.roll(o, n, 1))
            table_ref[top + 2 * TM : top + 4 * TM, lanes] = jnp.where(
                low, pltpu.roll(e, n, 1), o
            )

    halves = [slice(k * LANES, (k + 1) * LANES) for k in range(TM // 2)]
    for two in range(half // 2):
        even = [fold_ref[k, pl.ds(2 * two, 2 * TM, stride=half), :] for k in range(TM // 2)]
        odd = [fold_ref[k, pl.ds(2 * two + 1, 2 * TM, stride=half), :] for k in range(TM // 2)]
        at = two * LANES % slots.LOW
        split(even, odd, two * LANES // slots.LOW, slice(at, at + LANES))
    corner = jnp.concatenate(corners, 0)
    nothing = jnp.zeros((2 * TM, LANES), F32)
    table_ref[:, slots.LOW :] = jnp.zeros((slots.LOW, LANES), F32)
    split([corner[:, h] for h in halves], [nothing] * len(halves), 0, slice(slots.LOW, slots.depth))


def pick_tiles(emit, owner_ref, tables, chosen_ref, slots):
    inside, column = iota((slots.LOW, LANES), 0) % slots.columns, iota((slots.LOW, LANES), 1)
    entry = (inside % (2 * TM)) * TM + inside // (2 * TM)
    fold = (column % slots.columns == entry).astype(F32).astype(BF16)
    rows = slots.all_rows
    lane16 = iota((16, LANES), 1)
    lanes = [
        (lane16 + t * LANES).astype(jnp.int16) for t in range(slots.depth // LANES)
    ]
    one, zero = jnp.ones((16, LANES), BF16), jnp.zeros((16, LANES), BF16)
    lane_group = iota((slots.rows, LANES), 1) // slots.columns
    high_group = iota((rows, LANES), 1) // slots.columns
    count = owner_ref.shape[1] // 2
    for half in range(2):
        high = []
        for k in range(count):
            n = half * count + k
            code = jnp.broadcast_to(owner_ref[:, n : n + 1], (rows, LANES))
            high.append(code >> 9)
            low = (code & 511).astype(jnp.int16)
            for top in range(0, rows, 16):
                for t in range(slots.depth // LANES):
                    chosen_ref[
                        half, k * rows + top : k * rows + top + 16, t * LANES : (t + 1) * LANES
                    ] = jnp.where(low[top : top + 16] == lanes[t], one, zero)
        for d, table in enumerate(tables):
            parts = dot(chosen_ref[half], table, NT)
            masked = jnp.concatenate(
                [
                    jnp.concatenate(
                        [
                            jnp.where(
                                high[k] == high_group + side * slots.groups,
                                parts[k * rows : (k + 1) * rows, side * LANES : (side + 1) * LANES],
                                0.0,
                            )
                            for side in range(2)
                        ],
                        1,
                    ).astype(BF16)
                    for k in range(count)
                ],
                0,
            )
            picked = dot(masked, fold)
            for k in range(count):
                top = k * rows
                packed = picked[top : top + slots.rows]
                for g in range(1, slots.groups):
                    piece = picked[top + g * slots.rows : top + (g + 1) * slots.rows]
                    packed = jnp.where(lane_group == g, piece, packed)
                emit(half * count + k, d, packed)


def store_all_links(links_ref, seed_ref, x):
    _, _, tiles, _ = links_ref.shape
    plane = tiles * LANES
    place = iota((tiles, LANES), 0) * LANES + iota((tiles, LANES), 1)
    before_y = jnp.where(place < NZ, place + (plane - NZ), place - NZ)
    before_z = jnp.where(place % NZ == 0, place + (NZ - 1), place - 1)
    for d, source in enumerate((place, before_y, before_z)):
        store_links(links_ref.at[d], seed_ref[d], source + x * plane)


def load_modes(planar_hbm, out_ref, sems, first):
    _, _, count, plane = planar_hbm.shape
    modes = out_ref.shape[0] // 2
    copies = [
        pltpu.make_async_copy(
            planar_hbm.at[c, part],
            out_ref.at[pl.ds(part * modes + first, count), pl.ds(c * plane, plane)],
            sems.at[2 * c + part],
        )
        for c in range(3)
        for part in range(2)
    ]
    for copy in copies:
        copy.start()
    return copies


def load_all(parts, out_ref, sems):
    quarter = out_ref.shape[0] // 8
    copies = []
    for k, (first, _) in enumerate(chunks_of(4 * quarter)):
        copies += load_modes(parts[k], out_ref, sems.at[k], first)
    return copies


def wait_all(copies):
    for copy in copies:
        copy.wait()


def store_left_y(out_ref, left_ref, plane):
    wide = 2 * LANES
    source, target = iota((wide, wide), 0), iota((wide, wide), 1)
    halves = source == (target // LANES) * LANES + (target + NZ) % LANES
    halves = halves.astype(F32).astype(BF16)
    low = iota((left_ref.shape[0], LANES), 1) < NZ
    for c in range(3):
        swapped = []
        for start in range(c * plane, (c + 1) * plane, wide):
            both = dot(left_ref[:, start : start + wide], halves)
            swapped += [both[:, :LANES], both[:, LANES:]]
        for t in range(plane // LANES):
            lanes = slice(c * plane + t * LANES, c * plane + (t + 1) * LANES)
            out_ref[:, lanes] = jnp.where(low, swapped[t - 1], swapped[t]).astype(BF16)


def store_left_z(out_ref, left_ref, plane):
    wide = 2 * LANES
    source, target = iota((wide, wide), 0), iota((wide, wide), 1)
    before = jnp.where(target % NZ == 0, target + (NZ - 1), target - 1)
    behind = (source == before).astype(F32).astype(BF16)
    for start in range(0, 3 * plane, wide):
        piece = dot(left_ref[:, start : start + wide], behind)
        out_ref[:, start : start + wide] = piece.astype(BF16)


def load_kernel(starts, whole_hbm, *refs):
    parts, sems = refs[-1 - len(starts) : -1], refs[-1]
    copies = []
    for k, (start, part) in enumerate(zip(starts, parts)):
        count = part.shape[0] // PIECES
        for piece in range(PIECES):
            copies.append(
                pltpu.make_async_copy(
                    whole_hbm.at[pl.ds(start + piece * count, count)],
                    part.at[pl.ds(piece * count, count)],
                    sems.at[k, piece],
                )
            )
    for copy in copies:
        copy.start()
    wait_all(copies)


def place_of(n, here, near, far):
    return lax.rem(n % near + near - lax.rem(here, near), near) * far + n // near


def inner_kernel(
    slots,
    grid,
    seed_ref,
    where_ref,
    owner_ref,
    a,
    b,
    c,
    *refs,
):
    near, far = grid
    sent, refs = refs[:near], refs[near:]
    links_x_ref, own_hbm, vector_ref, left_ref, hop_ref, links_ref, *refs = refs
    table_ref, fold_ref, chosen_ref, stage_ref, sems, own_sem = refs
    modes, plane = vector_ref.shape[0] // 2, vector_ref.shape[1] // 3
    copies = load_all((a, b, c), vector_ref, sems)
    store_all_links(links_ref, seed_ref, where_ref[0])
    links_x_ref[...] = links_ref[0]
    wait_all(copies)
    own = pltpu.make_async_copy(vector_ref, own_hbm, own_sem)
    own.start()
    tables = []
    for d, store_left in ((1, store_left_y), (2, store_left_z)):
        store_left(left_ref, vector_ref, plane)
        hop(vector_ref, hop_ref, links_ref.at[d], 0, modes)
        real, imag = products(left_ref, hop_ref)
        store_table(table_ref.at[d - 1], fold_ref, real, imag, slots)
        tables.append(table_ref.at[d - 1])

    def emit(n, d, packed):
        stage_ref[place_of(n, where_ref[0], near, far), d] = packed.astype(BF16)

    pick_tiles(emit, owner_ref, [t[...].astype(BF16) for t in tables], chosen_ref, slots)
    for k in range(near):
        sent[k][...] = stage_ref[k * far : (k + 1) * far]
    own.wait()


def outer_chunk(links_ref, upper_hbm, own_hbm, vector_ref, left_ref, hop_ref, sems):
    arriving = load_modes(upper_hbm, vector_ref, sems.at[3], 0)
    if len(own_hbm) > 1:
        own = load_all(own_hbm, left_ref, sems)
    else:
        count = left_ref.shape[0] // PIECES
        own = [
            pltpu.make_async_copy(
                own_hbm[0].at[pl.ds(piece * count, count)],
                left_ref.at[pl.ds(piece * count, count)],
                sems.at[1, piece],
            )
            for piece in range(PIECES)
        ]
        for copy in own:
            copy.start()
    wait_all(arriving)
    hop(vector_ref, hop_ref, links_ref, 0, vector_ref.shape[0] // 2)
    wait_all(own)
    return products(left_ref, hop_ref)


def wide_kernel(links_ref, upper_hbm, own_hbm, out_ref, *scratch):
    out_ref[0], out_ref[1] = outer_chunk(links_ref, upper_hbm, (own_hbm,), *scratch)


def narrow_kernel(links_ref, upper_hbm, a, b, c, before_hbm, out_ref, *scratch):
    del before_hbm
    out_ref[...] = outer_chunk(links_ref, upper_hbm, (a, b, c), *scratch)


def last_kernel(
    slots,
    grid,
    where_ref,
    owner_ref,
    first_ref,
    second_ref,
    links_ref,
    upper_hbm,
    a,
    b,
    c,
    *refs,
):
    near, far = grid
    sent_hbm, refs = refs[:near], refs[near:]
    vector_ref, left_ref, hop_ref, sems, table_ref, fold_ref, chosen_ref, stage_ref, out_sems = refs
    last = outer_chunk(links_ref, upper_hbm, (a, b, c), vector_ref, left_ref, hop_ref, sems)
    quarter = last.shape[1] // 2
    low = iota(last.shape, 1) < quarter
    second = second_ref[...]
    real = [first_ref[0], jnp.where(low, second, pltpu.roll(last, quarter, 1))]
    imag = [first_ref[1], jnp.where(low, pltpu.roll(second, quarter, 1), last)]
    store_table(
        table_ref, fold_ref, jnp.concatenate(real, 1), jnp.concatenate(imag, 1), slots
    )

    def emit(n, d, packed):
        stage_ref[place_of(n, where_ref[0], near, far)] = packed.astype(BF16)

    pick_tiles(emit, owner_ref, [table_ref[...].astype(BF16)], chosen_ref, slots)
    leaving = [
        pltpu.make_async_copy(stage_ref.at[pl.ds(k * far, far)], sent_hbm[k], out_sems.at[k])
        for k in range(near)
    ]
    for copy in leaving:
        copy.start()
    wait_all(leaving)


def near_sum_kernel(where_ref, *refs):
    far = refs[0].shape[0]
    sources, outs = refs[:-far], refs[-far:]
    near = len(sources) // 2
    here = where_ref[0] // near

    def total(arrays, block):
        value = arrays[0][block].astype(F32)
        for array in arrays[1:]:
            value = value + array[block].astype(F32)
        return value

    for m in range(far):
        block = lax.rem(here + m, far)
        outs[m][0] = total(sources[:near], block).astype(outs[m].dtype)
        outs[m][1:] = total(sources[near:], block).astype(outs[m].dtype)


def finish_kernel(normalise, slots, *refs):
    sources, out_ref = refs[:-1], refs[-1]
    here = out_ref.shape[0]
    total = sources[0][...]
    for source in sources[1:]:
        total = total + source[...].astype(F32)
    for d in range(3):
        value = total[d]
        value = value * normalise
        for group in range(slots.groups):
            first = group * slots.per_group
            count = min(slots.per_group, here - first)
            out_ref[first : first + count, d * slots.columns : (d + 1) * slots.columns] = value[
                :count, group * slots.columns : (group + 1) * slots.columns
            ]


def params(mib):
    return pltpu.CompilerParams(vmem_limit_bytes=mib * 1024 * 1024)


def cost(flops, moved):
    return pl.CostEstimate(flops=flops, bytes_accessed=moved, transcendentals=0)


def chunks_of(modes):
    quarter = modes // 4
    return ((0, 2 * quarter), (2 * quarter, quarter), (3 * quarter, quarter))


def per_device(eigvecs, link_seed, ownership):
    modes, _, _, layers, plane = eigvecs.shape
    assert layers == 1
    devices = lax.axis_size("sx")
    here = ownership.shape[0] // devices
    depth = 3 * plane
    tiles = plane // LANES
    slots = Slots(modes, here)
    vmem = pl.BlockSpec(memory_space=pltpu.VMEM)
    smem = pl.BlockSpec(memory_space=pltpu.SMEM)
    anywhere = pl.BlockSpec(memory_space=pl.ANY)

    raw = eigvecs.transpose(0, 2, 3, 1, 4).reshape(3 * modes, 2, plane)
    route = [(i, (i - 1) % devices) for i in range(devices)]
    chunks = chunks_of(modes)
    own, upper = [], []
    for some, room in ((chunks[:1], 52), (chunks[1:], 50)):
        loaded = pl.pallas_call(
            functools.partial(load_kernel, [3 * first for first, _ in some]),
            name="load_modes",
            out_shape=[jax.ShapeDtypeStruct((3 * count, 2, plane), BF16) for _, count in some],
            in_specs=[anywhere] * (1 + len(own[-1:])),
            out_specs=[vmem] * len(some),
            scratch_shapes=[pltpu.SemaphoreType.DMA((len(some), PIECES))],
            compiler_params=params(room),
            cost_estimate=cost(0, 12 * modes * plane),
        )(raw, *own[-1:])
        for part, (_, count) in zip(loaded, some):
            part = part.reshape(count, 3, 2, plane).transpose(1, 2, 0, 3)
            own.append(part)
            upper.append(lax.ppermute(part, "sx", route))

    where = lax.axis_index("sx").reshape(1).astype(jnp.int32)
    owners = slots.arrange(slots.codes(ownership).reshape(devices, here))
    near = 1
    while near * near < devices:
        near *= 2
    far = devices // near
    assert near * far == devices
    flops = 4 * modes * modes * depth * 2
    wide = pltpu.VMEM((2 * modes, depth), BF16)
    table = (slots.LOW, slots.depth)
    fold_scratch = pltpu.VMEM((TM // 2, modes, LANES), F32)
    chosen_scratch = pltpu.VMEM((2, devices // 2 * slots.all_rows, slots.depth), BF16)

    block = (slots.rows, LANES)
    *sent_inner, links_x, left = pl.pallas_call(
        functools.partial(inner_kernel, slots, (near, far)),
        name="inner_directions",
        out_shape=[jax.ShapeDtypeStruct((far, 2) + block, BF16)] * near
        + [
            jax.ShapeDtypeStruct((18, tiles, LANES), F32),
            jax.ShapeDtypeStruct((2 * modes, depth), BF16),
        ],
        in_specs=[smem, smem, vmem] + [anywhere] * 3,
        out_specs=[vmem] * (near + 1) + [anywhere],
        scratch_shapes=[
            wide,
            wide,
            wide,
            pltpu.VMEM((3, 18, tiles, LANES), F32),
            pltpu.VMEM((2,) + table, F32),
            fold_scratch,
            chosen_scratch,
            pltpu.VMEM((devices, 2) + block, BF16),
            pltpu.SemaphoreType.DMA((3, 6)),
            pltpu.SemaphoreType.DMA,
        ],
        compiler_params=params(40),
        cost_estimate=cost(6 * flops, 8 * 2**20),
    )(link_seed, where, owners, *own)
    sizes = [count for _, count in chunks]

    def outer_scratch(size):
        return [
            pltpu.VMEM((2 * size, depth), BF16),
            wide,
            pltpu.VMEM((2 * size, depth), BF16),
            pltpu.SemaphoreType.DMA((4, 6)),
        ]

    def outer(kernel, name, which, shape, side):
        return pl.pallas_call(
            kernel,
            name=name,
            out_shape=jax.ShapeDtypeStruct(shape, F32),
            in_specs=[vmem] + [anywhere] * (1 + len(side)),
            out_specs=vmem,
            scratch_shapes=outer_scratch(sizes[which]),
            compiler_params=params(24),
            cost_estimate=cost(2**20, 2**18),
        )(links_x, upper[which], *side)

    first_x = outer(wide_kernel, "outer_first", 0, (2, modes, sizes[0]), [left])
    second_x = outer(narrow_kernel, "outer_second", 1, (modes, 2 * sizes[1]), own + [first_x])
    sent = pl.pallas_call(
        functools.partial(last_kernel, slots, (near, far)),
        name="outer_last",
        out_shape=[jax.ShapeDtypeStruct((far,) + block, BF16)] * near,
        in_specs=[smem] + [vmem] * 4 + [anywhere] * 4,
        out_specs=[anywhere] * near,
        scratch_shapes=outer_scratch(sizes[2])
        + [
            pltpu.VMEM(table, F32),
            fold_scratch,
            chosen_scratch,
            pltpu.VMEM((devices,) + block, BF16),
            pltpu.SemaphoreType.DMA((near,)),
        ],
        compiler_params=params(24),
        cost_estimate=cost(2**20, 2**18),
    )(where, owners, first_x, second_x, links_x, upper[2], *own)

    def onward(step, array, size, inner):
        def target(i):
            index = i // inner % size
            return i + ((index + step) % size - index) * inner

        return lax.ppermute(array, "sx", [(i, target(i)) for i in range(devices)])

    gathered = [
        array if k == 0 else onward(k, array, near, 1)
        for arrays in (sent, sent_inner)
        for k, array in enumerate(arrays)
    ]
    halfway = pl.pallas_call(
        near_sum_kernel,
        name="sum_near",
        out_shape=[
            jax.ShapeDtypeStruct((3,) + block, F32 if m == 0 else BF16) for m in range(far)
        ],
        in_specs=[smem] + [vmem] * (2 * near),
        out_specs=[vmem] * far,
        compiler_params=params(8),
        cost_estimate=cost(2**20, 2**20),
    )(where, *gathered)
    arrived = [halfway[0]] + [onward(m, halfway[m], far, near) for m in range(1, far)]

    extent_x = layers * devices
    normalise = 1.0 / math.sqrt(12.0 * extent_x * plane)
    return pl.pallas_call(
        functools.partial(finish_kernel, normalise, slots),
        name="sum_far",
        out_shape=jax.ShapeDtypeStruct((here, 3 * slots.columns), F32),
        in_specs=[vmem] * far,
        out_specs=vmem,
        compiler_params=params(8),
    )(*arrived)


def solution(mesh):
    return jax.shard_map(
        per_device,
        mesh=mesh,
        in_specs=(P("cfg", None, None, "sx", None), P("cfg"), P()),
        out_specs=P(("cfg", "sx"), None),
        check_vma=False,
    )
```
